128 devices in a mesh: sec: 2 (over y_hi), gz: 16 (over y_lo, x, core), gx: 4 (over z).
Axes of the slice: x: 4, y: 4 (y_hi: 2, y_lo: 2; y = y_hi * 2 + y_lo), z: 4, core: 2. Of those that a mesh axis runs over, the one named last changes fastest.
Arguments:
- velocity: float32 [3, 32, 64, 2048], P(None, 'gx', 'sec', 'gz'), may hold values from -6 to 6
- test_fields: float32 [4, 3, 32, 64, 2048], P('sec', None, 'gx', None, 'gz'), may hold values from -6 to 6
Outputs:
- velocity_next: float32 [3, 32, 64, 2048], P(None, 'gx', 'sec', 'gz')
- test_next: float32 [4, 3, 32, 64, 2048], P('sec', None, 'gx', None, 'gz')
The draws below stay inside these ranges and needn't reach their ends.
All inputs are finite; a program needn't handle non-finite values.
Results may differ from the reference program's by a relative error of at most 0.0001.
Values sent between devices are 32-bit elements; how exact they have to be, the bound alone decides.
No kernel may reach another device: no remote copies, remote signals or barrier semaphores. Data moves between devices by JAX's collectives and lax.ppermute only.
A program may use at most 128 MiB of HBM per device.

```python
import math
import jax
import jax.numpy as jnp

YD = 64
PROBLEMS = 4
NXW = 32
NZ = 2048


def steps_of(rng, dims, cuts, least, largest):
    loudness = 1.0
    for position, blocks in cuts:
        steps = jax.random.uniform(jax.random.fold_in(jax.random.fold_in(rng, 6), position), (blocks,), jnp.float32, least / len(cuts), largest / len(cuts))
        loudness = loudness * jnp.repeat(jnp.exp(steps), dims[position] // blocks).reshape((-1,) + (1,) * (len(dims) - 1 - position))
    return loudness


def gaussian(own_key, dims, spread, most, shards=(), kind=jnp.bfloat16):
    gain = steps_of(own_key, dims, shards, -0.22, 0.18) if shards else 1.0
    entries = jax.random.normal(own_key, dims, jnp.float32) * spread * gain
    return jnp.minimum(jnp.maximum(entries, -most), most).astype(kind)


def setup_inputs(seed: int = 0) -> dict:
    splits = jax.random.split(jax.random.key(seed), 3)
    return {
        "velocity": gaussian(splits[0], (3, NXW, YD, NZ), 1.0, 6.0, ((1, 4), (2, 2), (3, 16)), jnp.float32),
        "test_fields": gaussian(splits[1], (PROBLEMS, 3, NXW, YD, NZ), 1.0, 6.0, ((0, 2), (2, 4), (4, 16)), jnp.float32),
    }


ALPHA_LEFT = 1.0 / 3.0
COEF_NEAR = 14.0 / 9.0
COEF_FAR = 1.0 / 9.0
TIME_STEP = 0.2
VISCOSITY = 0.1
DIFFUSIVITY = 0.1
FORCE_AMPLITUDE = 1.0

def first_rolled(values, axis_dim):

    def shifted(offset):
        return jnp.roll(values, -offset, axis=axis_dim)
    return (45.0 * (shifted(1) - shifted(-1)) - 9.0 * (shifted(2) - shifted(-2)) + (shifted(3) - shifted(-3))) / 60.0

def second_rolled(values, axis_dim):

    def shifted(offset):
        return jnp.roll(values, -offset, axis=axis_dim)
    return (2.0 * (shifted(3) + shifted(-3)) - 27.0 * (shifted(2) + shifted(-2)) + 270.0 * (shifted(1) + shifted(-1)) - 490.0 * values) / 180.0

def spectral_dz(values):
    length = values.shape[-1]
    angles = jnp.arange(length // 2 + 1).astype(jnp.float32) * (2.0 * math.pi / length)
    ratio = (COEF_NEAR * jnp.sin(angles) + 0.5 * COEF_FAR * jnp.sin(2.0 * angles)) / (1.0 + 2.0 * ALPHA_LEFT * jnp.cos(angles))
    spectrum = jnp.fft.rfft(values, axis=-1)
    return jnp.fft.irfft(spectrum * (1j * ratio), n=length, axis=-1).astype(values.dtype)

def drive_field(x_index, y_index, cells_x, cells_y):
    phase_x = 2.0 * math.pi / cells_x * x_index.astype(jnp.float32)[:, None]
    phase_y = 2.0 * math.pi / cells_y * y_index.astype(jnp.float32)[None, :]
    stacked = jnp.stack([jnp.sin(phase_x) * jnp.cos(phase_y), -jnp.cos(phase_x) * jnp.sin(phase_y), math.sqrt(2.0) * jnp.sin(phase_x) * jnp.sin(phase_y)])
    return FORCE_AMPLITUDE * stacked[..., None]

def cross_vector(centred, total):
    return jnp.stack([centred[1] * total[2] - centred[2] * total[1], centred[2] * total[0] - centred[0] * total[2], centred[0] * total[1] - centred[1] * total[0]])

def reference(velocity, test_fields):
    cells_x = velocity.shape[1]
    cells_y = velocity.shape[2]
    cells_z = velocity.shape[3]
    drive = drive_field(jnp.arange(cells_x, dtype=jnp.int32), jnp.arange(cells_y, dtype=jnp.int32), cells_x, cells_y)
    grad_x = first_rolled(velocity, 1)
    grad_y = first_rolled(velocity, 2)
    grad_z = spectral_dz(velocity)
    laplace = second_rolled(velocity, 1) + second_rolled(velocity, 2) + second_rolled(velocity, 3)
    advect = velocity[0:1] * grad_x + velocity[1:2] * grad_y + velocity[2:3] * grad_z
    velocity_next = velocity + TIME_STEP * (VISCOSITY * laplace - advect + drive)
    centred = 0.5 * (velocity + velocity_next)
    angle = 2.0 * math.pi / cells_z * jnp.arange(cells_z, dtype=jnp.int32).astype(jnp.float32)
    results = []
    for problem in range(test_fields.shape[0]):
        wave = jnp.cos(angle) if problem % 2 == 0 else jnp.sin(angle)
        component_mask = (jnp.arange(3) == problem // 2).astype(jnp.float32)
        solution = test_fields[problem]
        total = solution + component_mask[:, None, None, None] * wave[None, None, None, :]
        cross = cross_vector(centred, total)
        dz_cross = spectral_dz(cross[0:2])
        dx_cross = first_rolled(cross[1:3], 1)
        dy_cross = first_rolled(cross, 2)
        curl = jnp.stack([dy_cross[2] - dz_cross[1], dz_cross[0] - dx_cross[1], dx_cross[0] - dy_cross[0]])
        laplace_test = second_rolled(solution, 1) + second_rolled(solution, 2) + second_rolled(solution, 3)
        results.append(solution + TIME_STEP * (curl + DIFFUSIVITY * laplace_test))
    return (velocity_next, jnp.stack(results))
```

```python
import math

import jax
import jax.numpy as jnp
import numpy as np
from jax import lax
from jax.experimental import pallas as pl
from jax.experimental.pallas import tpu as pltpu
from jax.sharding import PartitionSpec as P

STEP = 0.2
VISC = 0.1
DIFF = 0.1
FIRST = (45.0 / 60.0, -9.0 / 60.0, 1.0 / 60.0)
SECOND = (270.0 / 180.0, -27.0 / 180.0, 2.0 / 180.0)
MID = -490.0 / 180.0
ROOT = math.sqrt(5.0 / 9.0)
DECAY = -(1.0 - ROOT) / (2.0 / 3.0)
HIGHEST = lax.Precision.HIGHEST
VMEM_LIMIT = 48 * 1024 * 1024


def compact_weight(distance):
    d = np.asarray(distance)

    def green(k):
        return DECAY ** np.abs(k) / ROOT

    return 7.0 / 9.0 * (green(d + 1) - green(d - 1)) + 1.0 / 36.0 * (green(d + 2) - green(d - 2))


def second_weight(distance):
    d = np.abs(distance)
    table = np.array([MID, *SECOND, 0.0])
    return table[np.minimum(d, 4)]


TAIL = float(compact_weight(2)) / DECAY**2
CORNER = float(compact_weight(1)) - TAIL * DECAY


def z_tables(n):
    j = np.arange(n)
    gap = j[None, :] - j[:, None]
    inner_first = compact_weight(gap)
    inner_second = second_weight(gap)
    pick = np.zeros((8, n))
    for k in range(3):
        pick[k, n - 1 - k] = 1.0
        pick[4 + k, k] = 1.0
    pick[3] = DECAY ** (n - 1 - j)
    pick[7] = DECAY**j
    spread_first = np.zeros((8, n))
    spread_second = np.zeros((8, n))
    for k in range(3):
        for z in range(3 - k):
            spread_second[k, z] = SECOND[z + k]
            spread_second[4 + k, n - 1 - z] = SECOND[z + k]
    spread_first[0, 0] = CORNER
    spread_first[4, n - 1] = -CORNER
    spread_first[3] = TAIL * DECAY ** (j + 1)
    spread_first[7] = -TAIL * DECAY ** (n - j)
    lay_test = np.zeros((8, n))
    lay_cross = np.zeros((8, n))
    for z in range(3):
        for k in range(3 - z):
            lay_test[z, n - 1 - k] = STEP * DIFF * SECOND[z + k]
            lay_test[4 + z, k] = STEP * DIFF * SECOND[z + k]
    lay_cross[0, n - 1] = STEP * CORNER
    lay_cross[4, 0] = -STEP * CORNER
    lay_cross[3] = STEP * DECAY ** (n - 1 - j)
    lay_cross[7] = STEP * DECAY**j
    land = np.zeros((8, n))
    for z in range(3):
        land[z, z] = 1.0
        land[4 + z, n - 1 - z] = 1.0
    land[3] = spread_first[3]
    land[7] = spread_first[7]
    f32 = np.float32
    return {
        "inner": np.concatenate([inner_first, inner_second], 1).astype(f32),
        "pick": pick.astype(f32),
        "spread": np.concatenate([spread_first, spread_second], 1).astype(f32),
        "lay": np.stack([lay_test, lay_cross]).astype(f32),
        "land": land.astype(f32),
        "first": (STEP * inner_first).astype(f32),
        "second": (STEP * DIFF * inner_second).astype(f32),
    }


def split(values):
    high = values.astype(jnp.bfloat16)
    low = (values - high.astype(jnp.float32)).astype(jnp.bfloat16)
    return high, low


def dot(a, b):
    return jnp.dot(a, b, preferred_element_type=jnp.float32)


def dot_nt(a, b):
    return lax.dot_general(
        a, b, (((1,), (1,)), ((), ())), precision=HIGHEST, preferred_element_type=jnp.float32
    )


def dot_tn(a, b):
    return lax.dot_general(
        a, b, (((0,), (0,)), ((), ())), precision=HIGHEST, preferred_element_type=jnp.float32
    )


def edges_kernel(v_ref, pick_ref, low_ref, high_ref, ends_ref, right_ref, left_ref):
    _, nx, ny, n = v_ref.shape
    low_ref[...] = v_ref[:, 0:3]
    high_ref[...] = v_ref[:, nx - 3 : nx]
    ends_ref[:, :, 0:4] = v_ref[:, :, 0:4]
    ends_ref[:, :, 4:8] = v_ref[:, :, ny - 4 : ny]
    picked = dot_nt(pick_ref[...], v_ref[...].reshape(-1, n))
    right_ref[...] = picked[0:4]
    left_ref[...] = picked[4:8]


def flow_kernel(
    places, v_ref, low_ref, high_ref, ends_ref, from_left, from_right, inner_ref, spread_ref,
    next_ref, centred_ref, padded, halo, along_z,
):
    _, nx, ny, n = v_ref.shape
    halo[0:4] = from_left[...]
    halo[4:8] = from_right[...]
    along_z[...] = jnp.dot(
        v_ref[...].reshape(-1, n), inner_ref[...], precision=HIGHEST, preferred_element_type=jnp.float32
    ) + dot_tn(halo[...], spread_ref[...])
    padded[:, :, 0:8] = ends_ref[...]
    padded[:, :, 8 : 8 + ny] = v_ref[...]
    padded[:, :, 8 + ny : 16 + ny] = ends_ref[...]
    section, column = places[0], places[1]
    rows_x = lax.broadcasted_iota(jnp.int32, (nx, n), 0) + column * nx
    rows_y = lax.broadcasted_iota(jnp.int32, (ny, n), 0) + section * ny
    phase_x = rows_x.astype(jnp.float32) * (2.0 * math.pi / 32)
    phase_y = rows_y.astype(jnp.float32) * (2.0 * math.pi / 64)
    sin_x, cos_x = jnp.sin(phase_x), jnp.cos(phase_x)
    sin_y, cos_y = jnp.sin(phase_y), jnp.cos(phase_y)
    for i in range(nx):
        drive = (
            sin_x[i : i + 1] * cos_y,
            -(cos_x[i : i + 1] * sin_y),
            math.sqrt(2.0) * (sin_x[i : i + 1] * sin_y),
        )
        own = [v_ref[c, i] for c in range(3)]
        for c in range(3):

            def at_x(k, c=c):
                if k < 0:
                    return low_ref[c, k + 3]
                if k >= nx:
                    return high_ref[c, k - nx]
                return v_ref[c, k]

            def at_y(k, c=c, i=i):
                return padded[c, i, 8 + k : 8 + k + ny]

            up_x = [at_x(i + k) for k in (1, 2, 3)]
            down_x = [at_x(i - k) for k in (1, 2, 3)]
            up_y = [at_y(k) for k in (1, 2, 3)]
            down_y = [at_y(-k) for k in (1, 2, 3)]
            grad_x = sum(w * (a - b) for w, a, b in zip(FIRST, up_x, down_x))
            grad_y = sum(w * (a - b) for w, a, b in zip(FIRST, up_y, down_y))
            lap = sum(
                w * ((a + b) + (d + e)) for w, a, b, d, e in zip(SECOND, up_x, down_x, up_y, down_y)
            )
            base = (c * nx + i) * ny
            grad_z = along_z[base : base + ny, 0:n]
            lap = lap + (2.0 * MID) * own[c] + along_z[base : base + ny, n : 2 * n]
            advect = own[0] * grad_x + own[1] * grad_y + own[2] * grad_z
            moved = own[c] + STEP * (VISC * lap - advect + drive[c])
            next_ref[c, i] = moved
            centred_ref[c, i] = 0.5 * (own[c] + moved)


def faces_kernel(tests_ref, low_ref, high_ref, sems):
    nx = tests_ref.shape[2]
    first = pltpu.make_async_copy(tests_ref.at[:, :, pl.ds(0, 3)], low_ref, sems.at[0])
    second = pltpu.make_async_copy(tests_ref.at[:, :, pl.ds(nx - 3, 3)], high_ref, sems.at[1])
    first.start()
    second.start()
    first.wait()
    second.wait()


def wave_of(problem, slab, n):
    z = lax.broadcasted_iota(jnp.int32, (8, n), 1) + slab * n
    angle = z.astype(jnp.float32) * (2.0 * math.pi / 2048)
    return jnp.where(problem == 0, jnp.cos(angle), jnp.sin(angle))[0:1]


def cross_kernel(
    places, tests_ref, own_ref, other_ref, lay_ref,
    cross_ref, low_ref, high_ref, right_ref, left_ref, whole,
):
    _, _, nx, ny, n = tests_ref.shape
    problem = pl.program_id(0)
    section = places[0]
    half = ny // 2

    @pl.when(problem == 0)
    def _():
        whole[:, :, pl.ds(pl.multiple_of(section * half, half), half)] = own_ref[...]
        whole[:, :, pl.ds(pl.multiple_of((1 - section) * half, half), half)] = other_ref[...]
        low_ref[...] = whole[:, 0:3]
        high_ref[...] = whole[:, nx - 3 : nx]

    wave = wave_of(problem, places[2], n)
    wave_x = jnp.where(section == 0, wave, 0.0)
    wave_y = jnp.where(section == 0, 0.0, wave)
    for i in range(nx):
        cx, cy, cz = whole[0, i], whole[1, i], whole[2, i]
        tx, ty, tz = tests_ref[0, 0, i] + wave_x, tests_ref[0, 1, i] + wave_y, tests_ref[0, 2, i]
        cross_ref[0, 0, i] = cx * tz - cz * tx
        cross_ref[0, 1, i] = cy * tz - cz * ty
        cross_ref[0, 2, i] = cx * ty - cy * tx
    sent = dot_nt(lay_ref[0], tests_ref[0].reshape(-1, n))
    lines = nx * ny
    first = dot_nt(lay_ref[1], cross_ref[0, 0:2].reshape(-1, n))
    sent_xy = sent[:, 0 : 2 * lines] + first
    right_ref[:, 0 : 2 * lines] = sent_xy[0:4]
    right_ref[:, 2 * lines :] = sent[0:4, 2 * lines :]
    left_ref[:, 0 : 2 * lines] = sent_xy[4:8]
    left_ref[:, 2 * lines :] = sent[4:8, 2 * lines :]


def local_kernel(tests_ref, cross_ref, first_ref, second_ref, out_ref, pad_t, pad_c):
    _, _, nx, ny, n = tests_ref.shape
    first_high, first_low = split(first_ref[...])
    second_high, second_low = split(second_ref[...])
    for c in range(3):
        t_high, t_low = split(tests_ref[0, c].reshape(-1, n))
        total = dot(t_high, second_high) + dot(t_low, second_high) + dot(t_high, second_low)
        if c < 2:
            c_high, c_low = split(cross_ref[0, c].reshape(-1, n))
            total = total + dot(c_high, first_high) + dot(c_low, first_high) + dot(c_high, first_low)
        out_ref[0, c] = total.reshape(nx, ny, n)
    for i in range(nx):
        for c in range(3):
            pad_t[c, 0:8] = tests_ref[0, c, i, ny - 8 : ny]
            pad_t[c, 8 : 8 + ny] = tests_ref[0, c, i]
            pad_t[c, 8 + ny : 16 + ny] = tests_ref[0, c, i, 0:8]
        for c in (1, 2):
            pad_c[c - 1, 0:8] = cross_ref[0, c, i, ny - 8 : ny]
            pad_c[c - 1, 8 : 8 + ny] = cross_ref[0, c, i]
            pad_c[c - 1, 8 + ny : 16 + ny] = cross_ref[0, c, i, 0:8]

        def first_y(c):
            return sum(
                (STEP * w) * (pad_c[c, 8 + k : 8 + k + ny] - pad_c[c, 8 - k : 8 - k + ny])
                for k, w in zip((1, 2, 3), FIRST)
            )

        def first_x(c, scale, i=i):
            total = None
            for k, w in zip((1, 2, 3), FIRST):
                for j, sign in ((i + k, scale), (i - k, -scale)):
                    if 0 <= j < nx:
                        term = (STEP * sign * w) * cross_ref[0, c, j]
                        total = term if total is None else total + term
            return total

        for c in range(3):
            value = out_ref[0, c, i] + (1.0 + STEP * DIFF * 2.0 * MID) * tests_ref[0, c, i]
            for k, w in zip((1, 2, 3), SECOND):
                near = pad_t[c, 8 + k : 8 + k + ny] + pad_t[c, 8 - k : 8 - k + ny]
                for j in (i + k, i - k):
                    if 0 <= j < nx:
                        near = near + tests_ref[0, c, j]
                value = value + (STEP * DIFF * w) * near
            if c == 0:
                value = value + first_y(1)
            elif c == 1:
                value = value + first_x(2, -1.0)
            else:
                value = value + first_x(0, -1.0) - first_y(0)
            out_ref[0, c, i] = value


def finish_kernel(
    places, part_ref, t_low_ref, t_high_ref, c_low_ref, c_high_ref, from_left, from_right, land_ref,
    out_ref, halo, cross,
):
    _, _, nx, ny, n = part_ref.shape
    problem = pl.program_id(0)
    section = places[0]
    halo[0:4] = from_left[...]
    halo[4:8] = from_right[...]
    out_ref[...] = part_ref[...] + dot_tn(halo[...], land_ref[...]).reshape(out_ref.shape)
    wave = wave_of(problem, places[2], n)
    wave_x = jnp.where(section == 0, wave, 0.0)
    wave_y = jnp.where(section == 0, 0.0, wave)
    for side, (t_ref, c_ref) in enumerate(((t_low_ref, c_low_ref), (t_high_ref, c_high_ref))):
        for h in range(3):
            cx, cy, cz = c_ref[0, h], c_ref[1, h], c_ref[2, h]
            tx, ty, tz = t_ref[0, 0, h] + wave_x, t_ref[0, 1, h] + wave_y, t_ref[0, 2, h]
            cross[0, h] = cz * tx - cx * tz
            cross[1, h] = cx * ty - cy * tx
        sign = -STEP if side == 0 else STEP
        for m in range(3):
            i = m if side == 0 else nx - 1 - m
            value = [out_ref[0, c, i] for c in range(3)]
            for d in range(m + 1, 4):
                h = 3 + m - d if side == 0 else d - 1 - m
                for c in range(3):
                    value[c] = value[c] + (STEP * DIFF * SECOND[d - 1]) * t_ref[0, c, h]
                value[1] = value[1] - (sign * FIRST[d - 1]) * cross[1, h]
                value[2] = value[2] + (sign * FIRST[d - 1]) * cross[0, h]
            for c in range(3):
                out_ref[0, c, i] = value[c]


def passed(block, axis, distance):
    count = lax.axis_size(axis)
    return lax.ppermute(block, axis, [(i, (i + distance) % count) for i in range(count)])


def shards(velocity, tests):
    _, nx, half, n = velocity.shape
    problems, _, _, ny, _ = tests.shape
    f32 = jnp.float32
    lines = nx * ny
    tables = {k: jnp.asarray(v) for k, v in z_tables(n).items()}
    places = jnp.stack([lax.axis_index(name) for name in ("sec", "gx", "gz")]).astype(jnp.int32)
    smem = pl.BlockSpec(memory_space=pltpu.SMEM)
    params = pltpu.CompilerParams(vmem_limit_bytes=VMEM_LIMIT)

    def shape(*dims):
        return jax.ShapeDtypeStruct(dims, f32)

    def cost(flops, moved):
        return pl.CostEstimate(flops=flops, bytes_accessed=moved, transcendentals=0)

    low, high, ends, to_right, to_left = pl.pallas_call(
        edges_kernel,
        out_shape=[
            shape(3, 3, half, n), shape(3, 3, half, n), shape(3, nx, 8, n),
            shape(4, 3 * nx * half), shape(4, 3 * nx * half),
        ],
        compiler_params=params,
        name="edges",
    )(velocity, tables["pick"])
    from_low = passed(high, "gx", 1)
    from_high = passed(low, "gx", -1)
    ends = passed(ends, "sec", 1)
    from_left = passed(to_right, "gz", 1)
    from_right = passed(to_left, "gz", -1)
    velocity_next, centred = pl.pallas_call(
        flow_kernel,
        in_specs=[smem] + [pl.BlockSpec(memory_space=pltpu.VMEM)] * 8,
        out_shape=[shape(3, nx, half, n)] * 2,
        scratch_shapes=[
            pltpu.VMEM((3, nx, half + 16, n), f32),
            pltpu.VMEM((8, 3 * nx * half), f32),
            pltpu.VMEM((3 * nx * half, 2 * n), f32),
        ],
        compiler_params=params,
        name="flow",
    )(places, velocity, from_low, from_high, ends, from_left, from_right, tables["inner"], tables["spread"])
    other = passed(centred, "sec", 1)
    tests_after, _ = lax.optimization_barrier((tests, centred))
    t_low, t_high = pl.pallas_call(
        faces_kernel,
        in_specs=[pl.BlockSpec(memory_space=pl.ANY)],
        out_specs=[pl.BlockSpec(memory_space=pl.ANY)] * 2,
        out_shape=[shape(problems, 3, 3, ny, n)] * 2,
        scratch_shapes=[pltpu.SemaphoreType.DMA((2,))],
        compiler_params=params,
        name="faces",
    )(tests_after)
    t_from_low = passed(t_high, "gx", 1)
    t_from_high = passed(t_low, "gx", -1)

    block = pl.BlockSpec((1, 3, nx, ny, n), lambda p: (p, 0, 0, 0, 0))
    face = pl.BlockSpec((1, 3, 3, ny, n), lambda p: (p, 0, 0, 0, 0))
    line = pl.BlockSpec((4, 3 * lines), lambda p: (0, p))

    def fixed(*dims):
        return pl.BlockSpec(dims, lambda p: (0,) * len(dims))

    cross, c_low, c_high, to_right, to_left = pl.pallas_call(
        cross_kernel,
        grid=(problems,),
        in_specs=[smem, block, fixed(3, nx, half, n), fixed(3, nx, half, n), fixed(2, 8, n)],
        out_specs=[block, fixed(3, 3, ny, n), fixed(3, 3, ny, n), line, line],
        out_shape=[
            shape(problems, 3, nx, ny, n), shape(3, 3, ny, n), shape(3, 3, ny, n),
            shape(4, problems * 3 * lines), shape(4, problems * 3 * lines),
        ],
        scratch_shapes=[pltpu.VMEM((3, nx, ny, n), f32)],
        compiler_params=params,
        name="cross",
    )(places, tests, centred, other, tables["lay"])
    c_from_low = passed(c_high, "gx", 1)
    c_from_high = passed(c_low, "gx", -1)
    from_left = passed(to_right, "gz", 1)
    from_right = passed(to_left, "gz", -1)
    part = pl.pallas_call(
        local_kernel,
        grid=(problems,),
        in_specs=[block, block, fixed(n, n), fixed(n, n)],
        out_specs=block,
        out_shape=shape(problems, 3, nx, ny, n),
        scratch_shapes=[pltpu.VMEM((3, ny + 16, n), f32), pltpu.VMEM((2, ny + 16, n), f32)],
        compiler_params=params,
        cost_estimate=cost(10**9, 6 * 10**6),
        name="local",
    )(tests, cross, tables["first"], tables["second"])
    test_next = pl.pallas_call(
        finish_kernel,
        grid=(problems,),
        in_specs=[smem, block, face, face, fixed(3, 3, ny, n), fixed(3, 3, ny, n), line, line, fixed(8, n)],
        out_specs=block,
        out_shape=shape(problems, 3, nx, ny, n),
        scratch_shapes=[pltpu.VMEM((8, 3 * lines), f32), pltpu.VMEM((2, 3, ny, n), f32)],
        compiler_params=params,
        name="finish",
    )(places, part, t_from_low, t_from_high, c_from_low, c_from_high, from_left, from_right, tables["land"])
    return velocity_next, test_next


def solution(mesh):
    placed = (P(None, "gx", "sec", "gz"), P("sec", None, "gx", None, "gz"))
    return jax.shard_map(shards, mesh=mesh, in_specs=placed, out_specs=placed, check_vma=False)
```

```python
import math

import jax
import jax.numpy as jnp
import numpy as np
from jax import lax
from jax.experimental import pallas as pl
from jax.experimental.pallas import tpu as pltpu
from jax.sharding import PartitionSpec as P

STEP = 0.2
VISC = 0.1
DIFF = 0.1
FIRST = (45.0 / 60.0, -9.0 / 60.0, 1.0 / 60.0)
SECOND = (270.0 / 180.0, -27.0 / 180.0, 2.0 / 180.0)
MID = -490.0 / 180.0
ROOT = math.sqrt(5.0 / 9.0)
DECAY = -(1.0 - ROOT) / (2.0 / 3.0)
VMEM_LIMIT = 48 * 1024 * 1024
F32 = jnp.float32
BF16 = jnp.bfloat16


def compact_weight(distance):
    d = np.asarray(distance)

    def green(k):
        return DECAY ** np.abs(k) / ROOT

    return 7.0 / 9.0 * (green(d + 1) - green(d - 1)) + 1.0 / 36.0 * (green(d + 2) - green(d - 2))


def second_weight(distance):
    table = np.array([MID, *SECOND, 0.0])
    return table[np.minimum(np.abs(distance), 4)]


TAIL = float(compact_weight(2)) / DECAY**2
CORNER = float(compact_weight(1)) - TAIL * DECAY


def halves(table):
    table = np.asarray(table, np.float32)
    high = np.asarray(np.asarray(table, jnp.bfloat16), np.float32)
    low = np.asarray(np.asarray(table - high, jnp.bfloat16), np.float32)
    return high, low


def make_tables(n, x_total, y_total, z_total):
    j = np.arange(n)
    gap = j[None, :] - j[:, None]
    inner_first = compact_weight(gap)
    inner_second = second_weight(gap)
    pick = np.zeros((8, n))
    for k in range(3):
        pick[k, n - 1 - k] = 1.0
        pick[4 + k, k] = 1.0
    pick[3] = DECAY ** (n - 1 - j)
    pick[7] = DECAY**j
    spread_first = np.zeros((8, n))
    spread_second = np.zeros((8, n))
    for k in range(3):
        for z in range(3 - k):
            spread_second[k, z] = SECOND[z + k]
            spread_second[4 + k, n - 1 - z] = SECOND[z + k]
    spread_first[0, 0] = CORNER
    spread_first[4, n - 1] = -CORNER
    spread_first[3] = TAIL * DECAY ** (j + 1)
    spread_first[7] = -TAIL * DECAY ** (n - j)
    lay_test = np.zeros((8, n))
    lay_cross = np.zeros((8, n))
    for z in range(3):
        for k in range(3 - z):
            lay_test[z, n - 1 - k] = STEP * DIFF * SECOND[z + k]
            lay_test[4 + z, k] = STEP * DIFF * SECOND[z + k]
    lay_cross[0, n - 1] = STEP * CORNER
    lay_cross[4, 0] = -STEP * CORNER
    lay_cross[3] = STEP * DECAY ** (n - 1 - j)
    lay_cross[7] = STEP * DECAY**j
    land = np.zeros((8, n))
    for z in range(3):
        land[z, z] = 1.0
        land[4 + z, n - 1 - z] = 1.0
    land[3] = spread_first[3]
    land[7] = spread_first[7]

    def stacked(table):
        high, low = halves(table)
        return np.concatenate([high, high, low, np.zeros_like(high)])

    def wide(column):
        return np.broadcast_to(np.asarray(column)[:, None], (len(column), n))

    phase_x = 2.0 * math.pi / x_total * np.arange(x_total)
    phase_y = 2.0 * math.pi / y_total * np.arange(y_total)
    angle = 2.0 * math.pi / z_total * np.arange(z_total)
    parts = {
        "pick": np.concatenate(halves(pick)),
        "lay_test": np.concatenate(halves(lay_test)),
        "lay_cross": np.concatenate(halves(lay_cross)),
        "spread_first": stacked(spread_first),
        "spread_second": stacked(spread_second),
        "land": stacked(land),
        "flow_first": np.concatenate(halves(inner_first)),
        "flow_second": np.concatenate(halves(inner_second)),
        "test_first": np.concatenate(halves(STEP * inner_first)),
        "test_second": np.concatenate(halves(STEP * DIFF * inner_second)),
        "sin_x": wide(np.sin(phase_x)),
        "cos_x": wide(np.cos(phase_x)),
        "sin_y": wide(np.sin(phase_y)),
        "cos_y": wide(np.cos(phase_y)),
        "wave": np.concatenate([np.cos(angle), np.sin(angle)]).reshape(-1, n),
    }
    places, rows = {}, 0
    for name, part in parts.items():
        places[name] = (rows, len(part))
        rows += len(part)
    return np.concatenate(list(parts.values())).astype(np.float32), places


def split(values):
    high = values.astype(BF16)
    low = (values - high.astype(F32)).astype(BF16)
    return high, low


def dot(a, b):
    return jnp.dot(a, b, preferred_element_type=F32)


def three(values, high, low):
    a, b = split(values)
    return dot(a, high) + dot(b, high) + dot(a, low)


def lines_out(values, both):
    a, b = split(values)
    nt = (((1,), (1,)), ((), ()))
    main = lax.dot_general(both, a, nt, preferred_element_type=F32)
    rest = lax.dot_general(both, b, nt, preferred_element_type=F32)
    return main[0:8] + main[8:16] + rest[0:8]


def lines_in(raw, tables):
    high = raw.astype(BF16).astype(F32)
    low = raw - high
    packed = jnp.concatenate([high, low, high, jnp.zeros_like(high)], 0).astype(BF16)
    return lax.dot_general(packed, tables, (((0,), (0,)), ((), ())), preferred_element_type=F32)


class Tables:
    def __init__(self, ref, places):
        self.ref = ref
        self.places = places

    def get(self, name):
        start, rows = self.places[name]
        return self.ref[start : start + rows]

    def pair(self, name):
        start, rows = self.places[name]
        half = rows // 2
        return self.ref[start : start + half].astype(BF16), self.ref[start + half : start + rows].astype(BF16)

    def row(self, name, index):
        return self.ref[pl.ds(self.places[name][0] + index, 1)]


def in_chip():
    return lax.rem(lax.axis_index("gz"), 2) == 0


def hand_out(sent, inner_ref, outer_ref):
    even = in_chip()
    inner_ref[...] = jnp.where(even, sent[0:4], sent[4:8])
    outer_ref[...] = jnp.where(even, sent[4:8], sent[0:4])


def taken_in(inner_ref, outer_ref):
    even = in_chip()
    left = jnp.where(even, outer_ref[...], inner_ref[...])
    right = jnp.where(even, inner_ref[...], outer_ref[...])
    return jnp.concatenate([left, right], 0)


def wave_parts(tables, problem, slabs):
    wave = tables.row("wave", problem * slabs + lax.axis_index("gz"))
    first = lax.axis_index("sec") == 0
    return jnp.where(first, wave, 0.0), jnp.where(first, 0.0, wave)


def wrap(pad, k, values):
    ny = values.shape[0]
    pad[k, 0:8] = values[ny - 8 : ny]
    pad[k, 8 : 8 + ny] = values
    pad[k, 8 + ny : 16 + ny] = values[0:8]


def tables_kernel(source, out):
    out[...] = source[...]


def faces_kernel(tests_ref, low_ref, high_ref):
    nx = tests_ref.shape[2]
    low_ref[...] = tests_ref[:, :, 0:3]
    high_ref[...] = tests_ref[:, :, nx - 3 : nx]


def spread_kernel(places, tests_ref, tables_ref, out_ref, sent_ref, pad):
    problems, _, nx, ny, n = tests_ref.shape
    tables = Tables(tables_ref, places)
    high, low = tables.pair("test_second")
    lay = tables.get("lay_test").astype(BF16)
    lines = nx * ny
    for p in range(problems):
        for c in range(3):
            flat = tests_ref[p, c].reshape(lines, n)
            out_ref[p, c] = three(flat, high, low).reshape(nx, ny, n)
            at = (3 * p + c) * lines
            sent_ref[:, at : at + lines] = lines_out(flat, lay)
        for i in range(nx):
            for c in range(3):
                wrap(pad, c, tests_ref[p, c, i])
            for c in range(3):
                value = out_ref[p, c, i] + (1.0 + STEP * DIFF * 2.0 * MID) * tests_ref[p, c, i]
                for k, w in zip((1, 2, 3), SECOND):
                    near = pad[c, 8 + k : 8 + k + ny] + pad[c, 8 - k : 8 - k + ny]
                    for j in (i + k, i - k):
                        if 0 <= j < nx:
                            near = near + tests_ref[p, c, j]
                    value = value + (STEP * DIFF * w) * near
                out_ref[p, c, i] = value


def whole_kernel(places, own_ref, other_ref, tables_ref, whole_ref, low_ref, high_ref, inner_ref, outer_ref):
    _, nx, half, n = own_ref.shape
    section = lax.axis_index("sec")
    whole_ref[:, :, pl.ds(pl.multiple_of(section * half, half), half)] = own_ref[...]
    whole_ref[:, :, pl.ds(pl.multiple_of((1 - section) * half, half), half)] = other_ref[...]
    low_ref[...] = whole_ref[:, 0:3]
    high_ref[...] = whole_ref[:, nx - 3 : nx]
    pick = Tables(tables_ref, places).get("pick").astype(BF16)
    hand_out(lines_out(whole_ref[...].reshape(-1, n), pick), inner_ref, outer_ref)


def flow_kernel(places, whole_ref, tables_ref, acc_ref, pad, grad_z, lap_z):
    _, nx, ny, n = whole_ref.shape
    tables = Tables(tables_ref, places)
    flat = whole_ref[...].reshape(-1, n)
    grad_z[...] = three(flat, *tables.pair("flow_first")).reshape(grad_z.shape)
    lap_z[...] = three(flat, *tables.pair("flow_second")).reshape(lap_z.shape)
    sin_y, cos_y = tables.get("sin_y"), tables.get("cos_y")
    column = lax.axis_index("gx") * nx
    for i in range(nx):
        sin_x, cos_x = tables.row("sin_x", column + i), tables.row("cos_x", column + i)
        drive = (sin_x * cos_y, -(cos_x * sin_y), math.sqrt(2.0) * (sin_x * sin_y))
        for c in range(3):
            wrap(pad, c, whole_ref[c, i])
        own = [whole_ref[c, i] for c in range(3)]
        for c in range(3):
            grad_x = grad_y = None
            lap = lap_z[c, i] + (2.0 * MID) * own[c]
            for k, first, second in zip((1, 2, 3), FIRST, SECOND):
                up, down = pad[c, 8 + k : 8 + k + ny], pad[c, 8 - k : 8 - k + ny]
                term = first * (up - down)
                grad_y = term if grad_y is None else grad_y + term
                near = up + down
                for j, sign in ((i + k, first), (i - k, -first)):
                    if 0 <= j < nx:
                        value = whole_ref[c, j]
                        near = near + value
                        grad_x = sign * value if grad_x is None else grad_x + sign * value
                lap = lap + second * near
            advect = own[0] * grad_x + own[1] * grad_y + own[2] * grad_z[c, i]
            acc_ref[c, i] = own[c] + STEP * (VISC * lap - advect + drive[c])


def step_kernel(
    places, whole_ref, acc_ref, low_ref, high_ref, inner_in, outer_in, tests_ref, sent_ref, tables_ref,
    next_ref, cross_ref, low_out, high_out, inner_out, outer_out, moved_ref, grad_z, lap_z,
):
    _, nx, ny, n = whole_ref.shape
    half = ny // 2
    problems = tests_ref.shape[0]
    tables = Tables(tables_ref, places)
    raw = taken_in(inner_in, outer_in)
    grad_z[...] = lines_in(raw, tables.get("spread_first").astype(BF16)).reshape(grad_z.shape)
    lap_z[...] = lines_in(raw, tables.get("spread_second").astype(BF16)).reshape(lap_z.shape)
    mine = pl.ds(pl.multiple_of(lax.axis_index("sec") * half, half), half)
    waves = [wave_parts(tables, p, places["wave"][1] // 2) for p in range(problems)]
    for i in range(nx):
        own = [whole_ref[c, i] for c in range(3)]
        centred = []
        for c in range(3):
            lap, grad_x = lap_z[c, i], None
            for k, first, second in zip((1, 2, 3), FIRST, SECOND):
                for j, sign in ((i + k, first), (i - k, -first)):
                    if not 0 <= j < nx:
                        value = low_ref[c, j + 3] if j < 0 else high_ref[c, j - nx]
                        lap = lap + second * value
                        grad_x = sign * value if grad_x is None else grad_x + sign * value
            advect = own[2] * grad_z[c, i]
            if grad_x is not None:
                advect = advect + own[0] * grad_x
            moved = acc_ref[c, i] + STEP * (VISC * lap - advect)
            moved_ref[c, i] = moved
            next_ref[c, i] = moved_ref[c, i, mine]
            centred.append(0.5 * (own[c] + moved))
            if i < 3:
                low_out[c, i] = centred[c]
            if i >= nx - 3:
                high_out[c, i - nx + 3] = centred[c]
        cx, cy, cz = centred
        for p in range(problems):
            tx, ty, tz = tests_ref[p, 0, i] + waves[p][0], tests_ref[p, 1, i] + waves[p][1], tests_ref[p, 2, i]
            cross_ref[p, 0, i] = cx * tz - cz * tx
            cross_ref[p, 1, i] = cy * tz - cz * ty
            cross_ref[p, 2, i] = cx * ty - cy * tx
    lay = tables.get("lay_cross").astype(BF16)
    lines = nx * ny
    even = in_chip()
    for p in range(problems):
        at = 3 * p * lines
        added = lines_out(cross_ref[p, 0:2].reshape(-1, n), lay)
        for start, stop, sent in (
            (at, at + 2 * lines, sent_ref[:, at : at + 2 * lines] + added),
            (at + 2 * lines, at + 3 * lines, sent_ref[:, at + 2 * lines : at + 3 * lines]),
        ):
            inner_out[:, start:stop] = jnp.where(even, sent[0:4], sent[4:8])
            outer_out[:, start:stop] = jnp.where(even, sent[4:8], sent[0:4])


def curl_kernel(places, part_ref, cross_ref, low_ref, high_ref, tables_ref, out_ref, pad):
    problems, _, nx, ny, n = part_ref.shape
    tables = Tables(tables_ref, places)
    high, low = tables.pair("test_first")
    for p in range(problems):
        for c in range(2):
            total = three(cross_ref[p, c].reshape(-1, n), high, low)
            out_ref[p, c] = part_ref[p, c] + total.reshape(nx, ny, n)
        for i in range(nx):
            wrap(pad, 0, cross_ref[p, 1, i])
            wrap(pad, 1, cross_ref[p, 2, i])
            value = [out_ref[p, 0, i], out_ref[p, 1, i], part_ref[p, 2, i]]
            for k, first, second in zip((1, 2, 3), FIRST, SECOND):
                w = STEP * first
                value[0] = value[0] + w * (pad[1, 8 + k : 8 + k + ny] - pad[1, 8 - k : 8 - k + ny])
                value[2] = value[2] - w * (pad[0, 8 + k : 8 + k + ny] - pad[0, 8 - k : 8 - k + ny])
                for j, sign in ((i + k, w), (i - k, -w)):
                    if 0 <= j < nx:
                        value[1] = value[1] - sign * cross_ref[p, 2, j]
                        value[2] = value[2] - sign * cross_ref[p, 0, j]
                    else:
                        face, h = (low_ref, j + 3) if j < 0 else (high_ref, j - nx)
                        for c in range(3):
                            value[c] = value[c] + (STEP * DIFF * second) * face[p, c, h]
            for c in range(3):
                out_ref[p, c, i] = value[c]


def finish_kernel(
    places, part_ref, t_low_ref, t_high_ref, c_low_ref, c_high_ref, inner_in, outer_in, tables_ref,
    out_ref, held, cross, sems,
):
    problems, _, nx, ny, n = part_ref.shape
    tables = Tables(tables_ref, places)
    land = tables.get("land").astype(BF16)
    raw = taken_in(inner_in, outer_in)
    lines = nx * ny
    copies = []
    for p in range(problems):
        wave_x, wave_y = wave_parts(tables, p, places["wave"][1] // 2)
        for c in range(3):
            at = (3 * p + c) * lines
            held[p, c] = part_ref[p, c] + lines_in(raw[:, at : at + lines], land).reshape(nx, ny, n)
            if c == 0:
                copies.append(pltpu.make_async_copy(held.at[p, c], out_ref.at[p, c], sems.at[3 * p + c]))
                copies[-1].start()
        for side, (t_ref, c_ref) in enumerate(((t_low_ref, c_low_ref), (t_high_ref, c_high_ref))):
            for h in range(3):
                cx, cy, cz = c_ref[0, h], c_ref[1, h], c_ref[2, h]
                tx, ty, tz = t_ref[p, 0, h] + wave_x, t_ref[p, 1, h] + wave_y, t_ref[p, 2, h]
                cross[0, h] = cz * tx - cx * tz
                cross[1, h] = cx * ty - cy * tx
            sign = -STEP if side == 0 else STEP
            for m in range(3):
                i = m if side == 0 else nx - 1 - m
                second, third = held[p, 1, i], held[p, 2, i]
                for d in range(m + 1, 4):
                    h = 3 + m - d if side == 0 else d - 1 - m
                    second = second - (sign * FIRST[d - 1]) * cross[1, h]
                    third = third + (sign * FIRST[d - 1]) * cross[0, h]
                held[p, 1, i] = second
                held[p, 2, i] = third
        for c in (1, 2):
            copies.append(pltpu.make_async_copy(held.at[p, c], out_ref.at[p, c], sems.at[3 * p + c]))
            copies[-1].start()
    for copy in copies:
        copy.wait()


def shifted(block, axis, distance):
    count = lax.axis_size(axis)
    return lax.ppermute(block, axis, [(i, (i + distance) % count) for i in range(count)])


def swapped(block, axis, first):
    count = lax.axis_size(axis)
    pairs = [(i % count, (i + 1) % count) for i in range(first, count + first, 2)]
    return lax.ppermute(block, axis, pairs + [(b, a) for a, b in pairs])


def shards(velocity, tests):
    _, nx, half, n = velocity.shape
    problems, _, _, ny, _ = tests.shape
    lines = nx * ny
    constants, places = make_tables(n, nx * lax.axis_size("gx"), ny, n * lax.axis_size("gz"))
    params = pltpu.CompilerParams(vmem_limit_bytes=VMEM_LIMIT)
    vmem = pl.BlockSpec(memory_space=pltpu.VMEM)

    def shape(*dims):
        return jax.ShapeDtypeStruct(dims, F32)

    def run(kernel, name, args, outs, scratch=(), flops=10**8, out_specs=None, bind=True):
        body = kernel if not bind else (lambda *refs: kernel(places, *refs))
        moved = 4 * sum(math.prod(a.shape) for a in (*args, *outs))
        return pl.pallas_call(
            body,
            in_specs=[vmem] * len(args),
            out_specs=[vmem] * len(outs) if out_specs is None else out_specs,
            out_shape=list(outs),
            scratch_shapes=list(scratch),
            compiler_params=params,
            cost_estimate=pl.CostEstimate(flops=flops, bytes_accessed=moved, transcendentals=0),
            name=name,
        )(*args)

    whole_shape = (3, nx, ny, n)
    tests_shape = (problems, 3, nx, ny, n)
    other = shifted(velocity, "sec", 1)
    (tables,) = run(tables_kernel, "tables", [jnp.asarray(constants)], [shape(*constants.shape)], bind=False)
    t_low, t_high = run(faces_kernel, "faces", [tests], [shape(problems, 3, 3, ny, n)] * 2, bind=False)
    t_from_low = shifted(t_high, "gx", 1)
    t_from_high = shifted(t_low, "gx", -1)
    part, sent = run(
        spread_kernel, "spread", [tests, tables],
        [shape(*tests_shape), shape(8, problems * 3 * lines)],
        [pltpu.VMEM((3, ny + 16, n), F32)], flops=10**9,
    )
    whole, low, high, inner, outer = run(
        whole_kernel, "whole", [velocity, other, tables],
        [shape(*whole_shape), shape(3, 3, ny, n), shape(3, 3, ny, n), shape(4, 3 * lines), shape(4, 3 * lines)],
    )
    from_low = shifted(high, "gx", 1)
    from_high = shifted(low, "gx", -1)
    outer = swapped(outer, "gz", 1)
    inner = swapped(inner, "gz", 0)
    (acc,) = run(
        flow_kernel, "flow", [whole, tables], [shape(*whole_shape)],
        [pltpu.VMEM((3, ny + 16, n), F32), pltpu.VMEM(whole_shape, F32), pltpu.VMEM(whole_shape, F32)],
        flops=10**9,
    )
    velocity_next, cross, low, high, inner, outer = run(
        step_kernel, "step", [whole, acc, from_low, from_high, inner, outer, tests, sent, tables],
        [
            shape(3, nx, half, n), shape(*tests_shape), shape(3, 3, ny, n), shape(3, 3, ny, n),
            shape(4, problems * 3 * lines), shape(4, problems * 3 * lines),
        ],
        [pltpu.VMEM(whole_shape, F32)] * 3, flops=10**9,
    )
    from_low = shifted(high, "gx", 1)
    from_high = shifted(low, "gx", -1)
    outer = swapped(outer, "gz", 1)
    inner = swapped(inner, "gz", 0)
    (part,) = run(
        curl_kernel, "curl", [part, cross, t_from_low, t_from_high, tables], [shape(*tests_shape)],
        [pltpu.VMEM((2, ny + 16, n), F32)], flops=10**9,
    )
    (test_next,) = run(
        finish_kernel, "finish",
        [part, t_from_low, t_from_high, from_low, from_high, inner, outer, tables],
        [shape(*tests_shape)],
        [
            pltpu.VMEM(tests_shape, F32), pltpu.VMEM((2, 3, ny, n), F32),
            pltpu.SemaphoreType.DMA((3 * problems,)),
        ],
        flops=10**9, out_specs=[pl.BlockSpec(memory_space=pl.ANY)],
    )
    return velocity_next, test_next


def solution(mesh):
    placed = (P(None, "gx", "sec", "gz"), P("sec", None, "gx", None, "gz"))
    return jax.shard_map(shards, mesh=mesh, in_specs=placed, out_specs=placed, check_vma=False)
```

```python
import math

import jax
import jax.numpy as jnp
import numpy as np
from jax import lax
from jax.experimental import pallas as pl
from jax.experimental.pallas import tpu as pltpu
from jax.sharding import PartitionSpec as P

STEP = 0.2
VISC = 0.1
DIFF = 0.1
FIRST = (45.0 / 60.0, -9.0 / 60.0, 1.0 / 60.0)
SECOND = (270.0 / 180.0, -27.0 / 180.0, 2.0 / 180.0)
MID = -490.0 / 180.0
ROOT = math.sqrt(5.0 / 9.0)
DECAY = -(1.0 - ROOT) / (2.0 / 3.0)
VMEM_LIMIT = 12 * 1024 * 1024
F32 = jnp.float32
BF16 = jnp.bfloat16


def compact_weight(distance):
    d = np.asarray(distance)

    def green(k):
        return DECAY ** np.abs(k) / ROOT

    return 7.0 / 9.0 * (green(d + 1) - green(d - 1)) + 1.0 / 36.0 * (green(d + 2) - green(d - 2))


def second_weight(distance):
    table = np.array([MID, *SECOND, 0.0])
    return table[np.minimum(np.abs(distance), 4)]


TAIL = float(compact_weight(2)) / DECAY**2
CORNER = float(compact_weight(1)) - TAIL * DECAY


def halves(table):
    table = np.asarray(table, np.float32)
    high = np.asarray(np.asarray(table, jnp.bfloat16), np.float32)
    low = np.asarray(np.asarray(table - high, jnp.bfloat16), np.float32)
    return high, low


def make_tables(n, x_total, y_total, z_total):
    j = np.arange(n)
    gap = j[None, :] - j[:, None]
    inner_first = compact_weight(gap)
    inner_second = second_weight(gap)
    pick = np.zeros((8, n))
    for k in range(3):
        pick[k, n - 1 - k] = 1.0
        pick[4 + k, k] = 1.0
    pick[3] = DECAY ** (n - 1 - j)
    pick[7] = DECAY**j
    spread_first = np.zeros((8, n))
    spread_second = np.zeros((8, n))
    for k in range(3):
        for z in range(3 - k):
            spread_second[k, z] = SECOND[z + k]
            spread_second[4 + k, n - 1 - z] = SECOND[z + k]
    spread_first[0, 0] = CORNER
    spread_first[4, n - 1] = -CORNER
    spread_first[3] = TAIL * DECAY ** (j + 1)
    spread_first[7] = -TAIL * DECAY ** (n - j)
    lay_test = np.zeros((8, n))
    lay_cross = np.zeros((8, n))
    for z in range(3):
        for k in range(3 - z):
            lay_test[z, n - 1 - k] = STEP * DIFF * SECOND[z + k]
            lay_test[4 + z, k] = STEP * DIFF * SECOND[z + k]
    lay_cross[0, n - 1] = STEP * CORNER
    lay_cross[4, 0] = -STEP * CORNER
    lay_cross[3] = STEP * DECAY ** (n - 1 - j)
    lay_cross[7] = STEP * DECAY**j
    land = np.zeros((8, n))
    for z in range(3):
        land[z, z] = 1.0
        land[4 + z, n - 1 - z] = 1.0
    land[3] = spread_first[3]
    land[7] = spread_first[7]

    def stacked(table):
        high, low = halves(table)
        return np.concatenate([high, high, low, np.zeros_like(high)])

    def wide(column):
        return np.broadcast_to(np.asarray(column)[:, None], (len(column), n))

    phase_x = 2.0 * math.pi / x_total * np.arange(x_total)
    phase_y = 2.0 * math.pi / y_total * np.arange(y_total)
    angle = 2.0 * math.pi / z_total * np.arange(z_total)
    parts = {
        "pick": np.concatenate(halves(pick)),
        "lay_test": np.concatenate(halves(lay_test)),
        "lay_cross": np.concatenate(halves(lay_cross)),
        "spread_first": stacked(spread_first),
        "spread_second": stacked(spread_second),
        "land": stacked(land),
        "flow_first": np.concatenate(halves(inner_first)),
        "flow_second": np.concatenate(halves(inner_second)),
        "test_first": np.concatenate(halves(STEP * inner_first)),
        "test_second": np.concatenate(halves(STEP * DIFF * inner_second)),
        "sin_x": wide(np.sin(phase_x)),
        "cos_x": wide(np.cos(phase_x)),
        "sin_y": wide(np.sin(phase_y)),
        "cos_y": wide(np.cos(phase_y)),
        "wave": np.concatenate([np.cos(angle), np.sin(angle)]).reshape(-1, n),
    }
    places, rows = {}, 0
    for name, part in parts.items():
        places[name] = (rows, len(part))
        rows += len(part)
    return np.concatenate(list(parts.values())).astype(np.float32), places


def split(values):
    high = values.astype(BF16)
    low = (values - high.astype(F32)).astype(BF16)
    return high, low


def dot(a, b):
    return jnp.dot(a, b, preferred_element_type=F32)


def three(values, high, low):
    a, b = split(values)
    return dot(a, high) + dot(b, high) + dot(a, low)


def lines_out(values, both):
    a, b = split(values)
    nt = (((1,), (1,)), ((), ()))
    main = lax.dot_general(both, a, nt, preferred_element_type=F32)
    rest = lax.dot_general(both, b, nt, preferred_element_type=F32)
    return main[0:8] + main[8:16] + rest[0:8]


def lines_in(raw, tables):
    high = raw.astype(BF16).astype(F32)
    low = raw - high
    packed = jnp.concatenate([high, low, high, jnp.zeros_like(high)], 0).astype(BF16)
    return lax.dot_general(packed, tables, (((0,), (0,)), ((), ())), preferred_element_type=F32)


class Tables:
    def __init__(self, ref, places):
        self.ref = ref
        self.places = places

    def get(self, name):
        start, rows = self.places[name]
        return self.ref[start : start + rows]

    def pair(self, name):
        start, rows = self.places[name]
        half = rows // 2
        return self.ref[start : start + half].astype(BF16), self.ref[start + half : start + rows].astype(BF16)

    def row(self, name, index):
        return self.ref[pl.ds(self.places[name][0] + index, 1)]


def in_chip():
    return lax.rem(lax.axis_index("gz"), 2) == 0


def hand_out(sent, inner_ref, outer_ref):
    even = in_chip()
    inner_ref[...] = jnp.where(even, sent[0:4], sent[4:8])
    outer_ref[...] = jnp.where(even, sent[4:8], sent[0:4])


def taken_in(inner_ref, outer_ref):
    even = in_chip()
    left = jnp.where(even, outer_ref[...], inner_ref[...])
    right = jnp.where(even, inner_ref[...], outer_ref[...])
    return jnp.concatenate([left, right], 0)


def wave_parts(tables, problem, slabs):
    wave = tables.row("wave", problem * slabs + lax.axis_index("gz"))
    first = lax.axis_index("sec") == 0
    return jnp.where(first, wave, 0.0), jnp.where(first, 0.0, wave)


def wrap(pad, k, values):
    ny = values.shape[0]
    pad[k, 0:8] = values[ny - 8 : ny]
    pad[k, 8 : 8 + ny] = values
    pad[k, 8 + ny : 16 + ny] = values[0:8]


def tables_kernel(source, out):
    out[...] = source[...]


def early_rows(shape, half):
    problems, _, _, ny, _ = shape
    tests = {(p, h): (p * 3 + h) * ny for p in range(problems) for h in range(3)}
    first = problems * 3 * ny
    flow = {(c, h): first + (c * 3 + h) * half for c in range(3) for h in range(3)}
    return tests, flow, first + 9 * half


def faces_kernel(tests_ref, own_ref, low_ref, high_ref):
    nx, ny = tests_ref.shape[2:4]
    half = own_ref.shape[2]
    tests, flow, _ = early_rows(tests_ref.shape, half)
    for out, start in ((low_ref, 0), (high_ref, nx - 3)):
        for (p, h), at in tests.items():
            out[at : at + ny] = tests_ref[p, 0, start + h]
        for (c, h), at in flow.items():
            out[at : at + half] = own_ref[c, start + h]


def spread_kernel(places, tests_ref, tables_ref, out_ref, sent_ref, pad):
    problems, _, nx, ny, n = tests_ref.shape
    tables = Tables(tables_ref, places)
    high, low = tables.pair("test_second")
    lay = tables.get("lay_test").astype(BF16)
    lines = nx * ny
    for p in range(problems):
        for c in range(3):
            flat = tests_ref[p, c].reshape(lines, n)
            out_ref[p, c] = three(flat, high, low).reshape(nx, ny, n)
            at = (3 * p + c) * lines
            sent_ref[:, at : at + lines] = lines_out(flat, lay)
        for i in range(nx):
            for c in range(3):
                wrap(pad, c, tests_ref[p, c, i])
            for c in range(3):
                value = out_ref[p, c, i] + (1.0 + STEP * DIFF * 2.0 * MID) * tests_ref[p, c, i]
                for k, w in zip((1, 2, 3), SECOND):
                    near = pad[c, 8 + k : 8 + k + ny] + pad[c, 8 - k : 8 - k + ny]
                    for j in (i + k, i - k):
                        if 0 <= j < nx:
                            near = near + tests_ref[p, c, j]
                    value = value + (STEP * DIFF * w) * near
                out_ref[p, c, i] = value


def whole_kernel(places, own_ref, other_ref, tables_ref, whole_ref, low_ref, high_ref, inner_ref, outer_ref):
    _, nx, half, n = own_ref.shape
    section = lax.axis_index("sec")
    whole_ref[:, :, pl.ds(pl.multiple_of(section * half, half), half)] = own_ref[...]
    whole_ref[:, :, pl.ds(pl.multiple_of((1 - section) * half, half), half)] = other_ref[...]
    low_ref[...] = other_ref[:, 0:3]
    high_ref[...] = other_ref[:, nx - 3 : nx]
    pick = Tables(tables_ref, places).get("pick").astype(BF16)
    hand_out(lines_out(whole_ref[...].reshape(-1, n), pick), inner_ref, outer_ref)


def flow_kernel(places, whole_ref, tables_ref, acc_ref, pad, grad_z, lap_z):
    _, nx, ny, n = whole_ref.shape
    tables = Tables(tables_ref, places)
    flat = whole_ref[...].reshape(-1, n)
    grad_z[...] = three(flat, *tables.pair("flow_first")).reshape(grad_z.shape)
    lap_z[...] = three(flat, *tables.pair("flow_second")).reshape(lap_z.shape)
    sin_y, cos_y = tables.get("sin_y"), tables.get("cos_y")
    column = lax.axis_index("gx") * nx
    for i in range(nx):
        sin_x, cos_x = tables.row("sin_x", column + i), tables.row("cos_x", column + i)
        drive = (sin_x * cos_y, -(cos_x * sin_y), math.sqrt(2.0) * (sin_x * sin_y))
        for c in range(3):
            wrap(pad, c, whole_ref[c, i])
        own = [whole_ref[c, i] for c in range(3)]
        for c in range(3):
            grad_x = grad_y = None
            lap = lap_z[c, i] + (2.0 * MID) * own[c]
            for k, first, second in zip((1, 2, 3), FIRST, SECOND):
                up, down = pad[c, 8 + k : 8 + k + ny], pad[c, 8 - k : 8 - k + ny]
                term = first * (up - down)
                grad_y = term if grad_y is None else grad_y + term
                near = up + down
                for j, sign in ((i + k, first), (i - k, -first)):
                    if 0 <= j < nx:
                        value = whole_ref[c, j]
                        near = near + value
                        grad_x = sign * value if grad_x is None else grad_x + sign * value
                lap = lap + second * near
            advect = own[0] * grad_x + own[1] * grad_y + own[2] * grad_z[c, i]
            acc_ref[c, i] = own[c] + STEP * (VISC * lap - advect + drive[c])


def step_kernel(
    places, whole_ref, acc_ref, low_early, high_early, low_other, high_other, inner_in, outer_in, tests_ref, sent_ref,
    tables_ref, next_ref, cross_ref, low_out, high_out, inner_out, outer_out, moved_ref, grad_z, lap_z, low_ref, high_ref,
):
    _, nx, ny, n = whole_ref.shape
    half = ny // 2
    problems = tests_ref.shape[0]
    section = lax.axis_index("sec")
    mine = pl.ds(pl.multiple_of(section * half, half), half)
    theirs = pl.ds(pl.multiple_of((1 - section) * half, half), half)
    for face, early, other in ((low_ref, low_early, low_other), (high_ref, high_early, high_other)):
        for (c, h), at in early_rows(tests_ref.shape, half)[1].items():
            face[c, h, mine] = early[at : at + half]
            face[c, h, theirs] = other[c, h]
    tables = Tables(tables_ref, places)
    raw = taken_in(inner_in, outer_in)
    grad_z[...] = lines_in(raw, tables.get("spread_first").astype(BF16)).reshape(grad_z.shape)
    lap_z[...] = lines_in(raw, tables.get("spread_second").astype(BF16)).reshape(lap_z.shape)
    waves = [wave_parts(tables, p, places["wave"][1] // 2) for p in range(problems)]
    for i in range(nx):
        own = [whole_ref[c, i] for c in range(3)]
        centred = []
        for c in range(3):
            lap, grad_x = lap_z[c, i], None
            for k, first, second in zip((1, 2, 3), FIRST, SECOND):
                for j, sign in ((i + k, first), (i - k, -first)):
                    if not 0 <= j < nx:
                        value = low_ref[c, j + 3] if j < 0 else high_ref[c, j - nx]
                        lap = lap + second * value
                        grad_x = sign * value if grad_x is None else grad_x + sign * value
            advect = own[2] * grad_z[c, i]
            if grad_x is not None:
                advect = advect + own[0] * grad_x
            moved = acc_ref[c, i] + STEP * (VISC * lap - advect)
            moved_ref[c, i] = moved
            next_ref[c, i] = moved_ref[c, i, mine]
            centred.append(0.5 * (own[c] + moved))
        cx, cy, cz = centred
        for p in range(problems):
            tx, ty, tz = tests_ref[p, 0, i] + waves[p][0], tests_ref[p, 1, i] + waves[p][1], tests_ref[p, 2, i]
            cross_ref[p, 0, i] = cx * tz - cz * tx
            cross_ref[p, 1, i] = cy * tz - cz * ty
            cross_ref[p, 2, i] = cx * ty - cy * tx
    for p in range(problems):
        for out, sign in ((low_out, 1.0), (high_out, -1.0)):
            for m in range(3):
                second = third = 0.0
                for d in range(m + 1, 4):
                    j = d - 1 - m if sign > 0 else nx + m - d
                    slope, bend = sign * STEP * FIRST[d - 1], STEP * DIFF * SECOND[d - 1]
                    second = second + (bend * tests_ref[p, 1, j] - slope * cross_ref[p, 2, j])
                    third = third + (bend * tests_ref[p, 2, j] - slope * cross_ref[p, 0, j])
                out[p, 0, m] = second
                out[p, 1, m] = third
    lay = tables.get("lay_cross").astype(BF16)
    lines = nx * ny
    even = in_chip()
    for p in range(problems):
        at = 3 * p * lines
        added = lines_out(cross_ref[p, 0:2].reshape(-1, n), lay)
        for start, stop, sent in (
            (at, at + 2 * lines, sent_ref[:, at : at + 2 * lines] + added),
            (at + 2 * lines, at + 3 * lines, sent_ref[:, at + 2 * lines : at + 3 * lines]),
        ):
            inner_out[:, start:stop] = jnp.where(even, sent[0:4], sent[4:8])
            outer_out[:, start:stop] = jnp.where(even, sent[4:8], sent[0:4])


def curl_kernel(places, part_ref, cross_ref, low_ref, high_ref, tables_ref, out_ref, pad):
    problems, _, nx, ny, n = part_ref.shape
    tables = Tables(tables_ref, places)
    high, low = tables.pair("test_first")
    early = early_rows(part_ref.shape, ny // 2)[0]
    for p in range(problems):
        for c in range(2):
            total = three(cross_ref[p, c].reshape(-1, n), high, low)
            out_ref[p, c] = part_ref[p, c] + total.reshape(nx, ny, n)
        for i in range(nx):
            wrap(pad, 0, cross_ref[p, 1, i])
            wrap(pad, 1, cross_ref[p, 2, i])
            value = [out_ref[p, 0, i], out_ref[p, 1, i], part_ref[p, 2, i]]
            for k, first, second in zip((1, 2, 3), FIRST, SECOND):
                w = STEP * first
                value[0] = value[0] + w * (pad[1, 8 + k : 8 + k + ny] - pad[1, 8 - k : 8 - k + ny])
                value[2] = value[2] - w * (pad[0, 8 + k : 8 + k + ny] - pad[0, 8 - k : 8 - k + ny])
                for j, sign in ((i + k, w), (i - k, -w)):
                    if 0 <= j < nx:
                        value[1] = value[1] - sign * cross_ref[p, 2, j]
                        value[2] = value[2] - sign * cross_ref[p, 0, j]
                    else:
                        face, h = (low_ref, j + 3) if j < 0 else (high_ref, j - nx)
                        at = early[p, h]
                        value[0] = value[0] + (STEP * DIFF * second) * face[at : at + ny]
            for c in range(3):
                out_ref[p, c, i] = value[c]


def finish_kernel(places, part_ref, low_ref, high_ref, inner_in, outer_in, tables_ref, out_ref, held, sems):
    problems, _, nx, ny, n = part_ref.shape
    land = Tables(tables_ref, places).get("land").astype(BF16)
    raw = taken_in(inner_in, outer_in)
    lines = nx * ny
    copies = []
    for p in range(problems):
        for c in range(3):
            at = (3 * p + c) * lines
            held[p, c] = part_ref[p, c] + lines_in(raw[:, at : at + lines], land).reshape(nx, ny, n)
            if c > 0:
                held[p, c, 0:3] += low_ref[p, c - 1]
                for m in range(3):
                    held[p, c, nx - 1 - m] += high_ref[p, c - 1, m]
            copies.append(pltpu.make_async_copy(held.at[p, c], out_ref.at[p, c], sems.at[3 * p + c]))
            copies[-1].start()
    for copy in copies:
        copy.wait()


def shifted(block, axis, distance):
    count = lax.axis_size(axis)
    return lax.ppermute(block, axis, [(i, (i + distance) % count) for i in range(count)])


def swapped(block, axis, first):
    count = lax.axis_size(axis)
    pairs = [(i % count, (i + 1) % count) for i in range(first, count + first, 2)]
    return lax.ppermute(block, axis, pairs + [(b, a) for a, b in pairs])


def shards(velocity, tests):
    _, nx, half, n = velocity.shape
    problems, _, _, ny, _ = tests.shape
    lines = nx * ny
    constants, places = make_tables(n, nx * lax.axis_size("gx"), ny, n * lax.axis_size("gz"))
    params = pltpu.CompilerParams(vmem_limit_bytes=VMEM_LIMIT)
    vmem = pl.BlockSpec(memory_space=pltpu.VMEM)

    def shape(*dims):
        return jax.ShapeDtypeStruct(dims, F32)

    def run(kernel, name, args, outs, scratch=(), flops=10**8, out_specs=None, bind=True):
        body = kernel if not bind else (lambda *refs: kernel(places, *refs))
        moved = 4 * sum(math.prod(a.shape) for a in (*args, *outs))
        return pl.pallas_call(
            body,
            in_specs=[vmem] * len(args),
            out_specs=[vmem] * len(outs) if out_specs is None else out_specs,
            out_shape=list(outs),
            scratch_shapes=list(scratch),
            compiler_params=params,
            cost_estimate=pl.CostEstimate(flops=flops, bytes_accessed=moved, transcendentals=0),
            name=name,
        )(*args)

    whole_shape = (3, nx, ny, n)
    tests_shape = (problems, 3, nx, ny, n)
    other = shifted(velocity, "sec", 1)
    (tables,) = run(tables_kernel, "tables", [jnp.asarray(constants)], [shape(*constants.shape)], bind=False)
    rows = early_rows(tests_shape, half)[2]
    low, high = run(faces_kernel, "faces", [tests, velocity], [shape(rows, n)] * 2, bind=False)
    early = [shifted(high, "gx", 1), shifted(low, "gx", -1)]
    part, sent = run(
        spread_kernel, "spread", [tests, tables],
        [shape(*tests_shape), shape(8, problems * 3 * lines)],
        [pltpu.VMEM((3, ny + 16, n), F32)], flops=10**9,
    )
    whole, low, high, inner, outer = run(
        whole_kernel, "whole", [velocity, other, tables],
        [shape(*whole_shape)] + [shape(3, 3, half, n)] * 2 + [shape(4, 3 * lines)] * 2,
    )
    from_low = shifted(high, "gx", 1)
    from_high = shifted(low, "gx", -1)
    outer = swapped(outer, "gz", 1)
    inner = swapped(inner, "gz", 0)
    (acc,) = run(
        flow_kernel, "flow", [whole, tables], [shape(*whole_shape)],
        [pltpu.VMEM((3, ny + 16, n), F32), pltpu.VMEM(whole_shape, F32), pltpu.VMEM(whole_shape, F32)],
        flops=10**9,
    )
    velocity_next, cross, low, high, inner, outer = run(
        step_kernel, "step", [whole, acc, *early, from_low, from_high, inner, outer, tests, sent, tables],
        [
            shape(3, nx, half, n), shape(*tests_shape), shape(problems, 2, 3, ny, n), shape(problems, 2, 3, ny, n),
            shape(4, problems * 3 * lines), shape(4, problems * 3 * lines),
        ],
        [pltpu.VMEM(whole_shape, F32)] * 3 + [pltpu.VMEM((3, 3, ny, n), F32)] * 2, flops=10**9,
    )
    from_low = shifted(high, "gx", 1)
    from_high = shifted(low, "gx", -1)
    outer = swapped(outer, "gz", 1)
    inner = swapped(inner, "gz", 0)
    (part,) = run(
        curl_kernel, "curl", [part, cross, *early, tables], [shape(*tests_shape)],
        [pltpu.VMEM((2, ny + 16, n), F32)], flops=10**9,
    )
    (test_next,) = run(
        finish_kernel, "finish",
        [part, from_low, from_high, inner, outer, tables],
        [shape(*tests_shape)],
        [pltpu.VMEM(tests_shape, F32), pltpu.SemaphoreType.DMA((3 * problems,))],
        flops=10**9, out_specs=[pl.BlockSpec(memory_space=pl.ANY)],
    )
    return velocity_next, test_next


def solution(mesh):
    placed = (P(None, "gx", "sec", "gz"), P("sec", None, "gx", None, "gz"))
    return jax.shard_map(shards, mesh=mesh, in_specs=placed, out_specs=placed, check_vma=False)
```

```python
import math

import jax
import jax.numpy as jnp
import numpy as np
from jax import lax
from jax.experimental import pallas as pl
from jax.experimental.pallas import tpu as pltpu
from jax.sharding import PartitionSpec as P

STEP = 0.2
VISC = 0.1
DIFF = 0.1
FIRST = (45.0 / 60.0, -9.0 / 60.0, 1.0 / 60.0)
SECOND = (270.0 / 180.0, -27.0 / 180.0, 2.0 / 180.0)
MID = -490.0 / 180.0
ROOT = math.sqrt(5.0 / 9.0)
DECAY = -(1.0 - ROOT) / (2.0 / 3.0)
VMEM_LIMIT = 12 * 1024 * 1024
FACES_LIMIT = 62 * 1024 * 1024 + 512 * 1024
F32 = jnp.float32
BF16 = jnp.bfloat16


def compact_weight(distance):
    d = np.asarray(distance)

    def green(k):
        return DECAY ** np.abs(k) / ROOT

    return 7.0 / 9.0 * (green(d + 1) - green(d - 1)) + 1.0 / 36.0 * (green(d + 2) - green(d - 2))


def second_weight(distance):
    table = np.array([MID, *SECOND, 0.0])
    return table[np.minimum(np.abs(distance), 4)]


TAIL = float(compact_weight(2)) / DECAY**2
CORNER = float(compact_weight(1)) - TAIL * DECAY


def halves(table):
    table = np.asarray(table, np.float32)
    high = np.asarray(np.asarray(table, jnp.bfloat16), np.float32)
    low = np.asarray(np.asarray(table - high, jnp.bfloat16), np.float32)
    return high, low


def make_tables(n, x_total, y_total, z_total):
    j = np.arange(n)
    gap = j[None, :] - j[:, None]
    inner_first = compact_weight(gap)
    inner_second = second_weight(gap)
    pick = np.zeros((8, n))
    for k in range(3):
        pick[k, n - 1 - k] = 1.0
        pick[4 + k, k] = 1.0
    pick[3] = DECAY ** (n - 1 - j)
    pick[7] = DECAY**j
    spread_first = np.zeros((8, n))
    spread_second = np.zeros((8, n))
    for k in range(3):
        for z in range(3 - k):
            spread_second[k, z] = SECOND[z + k]
            spread_second[4 + k, n - 1 - z] = SECOND[z + k]
    spread_first[0, 0] = CORNER
    spread_first[4, n - 1] = -CORNER
    spread_first[3] = TAIL * DECAY ** (j + 1)
    spread_first[7] = -TAIL * DECAY ** (n - j)
    lay_test = np.zeros((8, n))
    lay_cross = np.zeros((8, n))
    for z in range(3):
        for k in range(3 - z):
            lay_test[z, n - 1 - k] = STEP * DIFF * SECOND[z + k]
            lay_test[4 + z, k] = STEP * DIFF * SECOND[z + k]
    lay_cross[0, n - 1] = STEP * CORNER
    lay_cross[4, 0] = -STEP * CORNER
    lay_cross[3] = STEP * DECAY ** (n - 1 - j)
    lay_cross[7] = STEP * DECAY**j
    land = np.zeros((8, n))
    for z in range(3):
        land[z, z] = 1.0
        land[4 + z, n - 1 - z] = 1.0
    land[3] = spread_first[3]
    land[7] = spread_first[7]

    def stacked(table):
        high, low = halves(table)
        return np.concatenate([high, high, low, np.zeros_like(high)])

    def wide(column):
        return np.broadcast_to(np.asarray(column)[:, None], (len(column), n))

    phase_x = 2.0 * math.pi / x_total * np.arange(x_total)
    phase_y = 2.0 * math.pi / y_total * np.arange(y_total)
    angle = 2.0 * math.pi / z_total * np.arange(z_total)
    parts = {
        "pick": np.concatenate(halves(pick)),
        "lay_test": np.concatenate(halves(lay_test)),
        "lay_cross": np.concatenate(halves(lay_cross)),
        "spread_first": stacked(spread_first),
        "spread_second": stacked(spread_second),
        "land": stacked(land),
        "flow_first": np.concatenate(halves(inner_first)),
        "flow_second": np.concatenate(halves(inner_second)),
        "test_first": np.concatenate(halves(STEP * inner_first)),
        "test_second": np.concatenate(halves(STEP * DIFF * inner_second)),
        "sin_x": wide(np.sin(phase_x)),
        "cos_x": wide(np.cos(phase_x)),
        "sin_y": wide(np.sin(phase_y)),
        "cos_y": wide(np.cos(phase_y)),
        "wave": np.concatenate([np.cos(angle), np.sin(angle)]).reshape(-1, n),
    }
    places, rows = {}, 0
    for name, part in parts.items():
        places[name] = (rows, len(part))
        rows += len(part)
    return np.concatenate(list(parts.values())).astype(np.float32), places


def split(values):
    high = values.astype(BF16)
    low = (values - high.astype(F32)).astype(BF16)
    return high, low


def dot(a, b):
    return jnp.dot(a, b, preferred_element_type=F32)


def three(values, high, low):
    a, b = split(values)
    return dot(a, high) + dot(b, high) + dot(a, low)


def lines_out(values, both):
    a, b = split(values)
    nt = (((1,), (1,)), ((), ()))
    main = lax.dot_general(both, a, nt, preferred_element_type=F32)
    rest = lax.dot_general(both, b, nt, preferred_element_type=F32)
    return main[0:8] + main[8:16] + rest[0:8]


def lines_in(raw, tables):
    high = raw.astype(BF16).astype(F32)
    low = raw - high
    packed = jnp.concatenate([high, low, high, jnp.zeros_like(high)], 0).astype(BF16)
    return lax.dot_general(packed, tables, (((0,), (0,)), ((), ())), preferred_element_type=F32)


class Tables:
    def __init__(self, ref, places):
        self.ref = ref
        self.places = places

    def get(self, name):
        start, rows = self.places[name]
        return self.ref[start : start + rows]

    def pair(self, name):
        start, rows = self.places[name]
        half = rows // 2
        return self.ref[start : start + half].astype(BF16), self.ref[start + half : start + rows].astype(BF16)

    def row(self, name, index):
        return self.ref[pl.ds(self.places[name][0] + index, 1)]


def in_chip():
    return lax.rem(lax.axis_index("gz"), 2) == 0


def hand_out(sent, inner_ref, outer_ref):
    even = in_chip()
    inner_ref[...] = jnp.where(even, sent[0:4], sent[4:8])
    outer_ref[...] = jnp.where(even, sent[4:8], sent[0:4])


def taken_in(inner_ref, outer_ref):
    even = in_chip()
    left = jnp.where(even, outer_ref[...], inner_ref[...])
    right = jnp.where(even, inner_ref[...], outer_ref[...])
    return jnp.concatenate([left, right], 0)


def wave_parts(tables, problem, slabs):
    wave = tables.row("wave", problem * slabs + lax.axis_index("gz"))
    first = lax.axis_index("sec") == 0
    return jnp.where(first, wave, 0.0), jnp.where(first, 0.0, wave)


def wrap(pad, k, values):
    ny = values.shape[0]
    pad[k, 0:8] = values[ny - 8 : ny]
    pad[k, 8 : 8 + ny] = values
    pad[k, 8 + ny : 16 + ny] = values[0:8]


def tables_kernel(source, out):
    out[...] = source[...]


def early_rows(shape, half):
    problems, _, _, ny, _ = shape
    tests = {(p, h): (p * 3 + h) * ny for p in range(problems) for h in range(3)}
    first = problems * 3 * ny
    flow = {(c, h): first + (c * 3 + h) * half for c in range(3) for h in range(3)}
    return tests, flow, first + 9 * half


def faces_kernel(tests_ref, own_ref, low_ref, high_ref, sems):
    nx, ny, n = tests_ref.shape[2:5]
    half = own_ref.shape[2]
    tests, flow, _ = early_rows(tests_ref.shape, half)
    problems = tests_ref.shape[0]
    copies = []
    for out, start in ((low_ref, 0), (high_ref, nx - 3)):
        for p in range(problems):
            at = tests[p, 0]
            copies.append((tests_ref.at[p, 0, start : start + 3], out.at[at : at + 3 * ny].reshape(3, ny, n)))
        at = flow[0, 0]
        copies.append((own_ref.at[:, start : start + 3], out.at[at : at + 9 * half].reshape(3, 3, half, n)))
    copies = [pltpu.make_async_copy(source, out, sems.at[k]) for k, (source, out) in enumerate(copies)]
    for copy in copies:
        copy.start()
    for copy in copies:
        copy.wait()


def spread_kernel(places, tests_ref, tables_ref, out_ref, sent_ref, pad):
    problems, _, nx, ny, n = tests_ref.shape
    tables = Tables(tables_ref, places)
    high, low = tables.pair("test_second")
    lay = tables.get("lay_test").astype(BF16)
    lines = nx * ny
    for p in range(problems):
        for c in range(3):
            flat = tests_ref[p, c].reshape(lines, n)
            out_ref[p, c] = three(flat, high, low).reshape(nx, ny, n)
            at = (3 * p + c) * lines
            sent_ref[:, at : at + lines] = lines_out(flat, lay)
        for i in range(nx):
            for c in range(3):
                wrap(pad, c, tests_ref[p, c, i])
            for c in range(3):
                value = out_ref[p, c, i] + (1.0 + STEP * DIFF * 2.0 * MID) * tests_ref[p, c, i]
                for k, w in zip((1, 2, 3), SECOND):
                    near = pad[c, 8 + k : 8 + k + ny] + pad[c, 8 - k : 8 - k + ny]
                    for j in (i + k, i - k):
                        if 0 <= j < nx:
                            near = near + tests_ref[p, c, j]
                    value = value + (STEP * DIFF * w) * near
                out_ref[p, c, i] = value


def whole_kernel(places, own_ref, other_ref, tables_ref, _, whole_ref, low_ref, high_ref, inner_ref, outer_ref):
    _, nx, half, n = own_ref.shape
    section = lax.axis_index("sec")
    whole_ref[:, :, pl.ds(pl.multiple_of(section * half, half), half)] = own_ref[...]
    whole_ref[:, :, pl.ds(pl.multiple_of((1 - section) * half, half), half)] = other_ref[...]
    low_ref[...] = other_ref[:, 0:3]
    high_ref[...] = other_ref[:, nx - 3 : nx]
    pick = Tables(tables_ref, places).get("pick").astype(BF16)
    hand_out(lines_out(whole_ref[...].reshape(-1, n), pick), inner_ref, outer_ref)


def flow_kernel(places, whole_ref, tables_ref, acc_ref, pad, grad_z, lap_z):
    _, nx, ny, n = whole_ref.shape
    tables = Tables(tables_ref, places)
    flat = whole_ref[...].reshape(-1, n)
    grad_z[...] = three(flat, *tables.pair("flow_first")).reshape(grad_z.shape)
    lap_z[...] = three(flat, *tables.pair("flow_second")).reshape(lap_z.shape)
    sin_y, cos_y = tables.get("sin_y"), tables.get("cos_y")
    column = lax.axis_index("gx") * nx
    for i in range(nx):
        sin_x, cos_x = tables.row("sin_x", column + i), tables.row("cos_x", column + i)
        drive = (sin_x * cos_y, -(cos_x * sin_y), math.sqrt(2.0) * (sin_x * sin_y))
        for c in range(3):
            wrap(pad, c, whole_ref[c, i])
        own = [whole_ref[c, i] for c in range(3)]
        for c in range(3):
            grad_x = grad_y = None
            lap = lap_z[c, i] + (2.0 * MID) * own[c]
            for k, first, second in zip((1, 2, 3), FIRST, SECOND):
                up, down = pad[c, 8 + k : 8 + k + ny], pad[c, 8 - k : 8 - k + ny]
                term = first * (up - down)
                grad_y = term if grad_y is None else grad_y + term
                near = up + down
                for j, sign in ((i + k, first), (i - k, -first)):
                    if 0 <= j < nx:
                        value = whole_ref[c, j]
                        near = near + value
                        grad_x = sign * value if grad_x is None else grad_x + sign * value
                lap = lap + second * near
            advect = own[0] * grad_x + own[1] * grad_y + own[2] * grad_z[c, i]
            acc_ref[c, i] = own[c] + STEP * (VISC * lap - advect + drive[c])


def step_kernel(
    places, whole_ref, acc_ref, low_early, high_early, low_other, high_other, inner_in, outer_in, tests_ref,
    tables_ref, moved_ref, cross_ref, low_out, high_out, grad_z, lap_z, low_ref, high_ref,
):
    _, nx, ny, n = whole_ref.shape
    half = ny // 2
    problems = tests_ref.shape[0]
    section = lax.axis_index("sec")
    mine = pl.ds(pl.multiple_of(section * half, half), half)
    theirs = pl.ds(pl.multiple_of((1 - section) * half, half), half)
    for face, early, other in ((low_ref, low_early, low_other), (high_ref, high_early, high_other)):
        for (c, h), at in early_rows(tests_ref.shape, half)[1].items():
            face[c, h, mine] = early[at : at + half]
            face[c, h, theirs] = other[c, h]
    tables = Tables(tables_ref, places)
    raw = taken_in(inner_in, outer_in)
    grad_z[...] = lines_in(raw, tables.get("spread_first").astype(BF16)).reshape(grad_z.shape)
    lap_z[...] = lines_in(raw, tables.get("spread_second").astype(BF16)).reshape(lap_z.shape)
    waves = [wave_parts(tables, p, places["wave"][1] // 2) for p in range(problems)]
    for i in range(nx):
        own = [whole_ref[c, i] for c in range(3)]
        centred = []
        for c in range(3):
            lap, grad_x = lap_z[c, i], None
            for k, first, second in zip((1, 2, 3), FIRST, SECOND):
                for j, sign in ((i + k, first), (i - k, -first)):
                    if not 0 <= j < nx:
                        value = low_ref[c, j + 3] if j < 0 else high_ref[c, j - nx]
                        lap = lap + second * value
                        grad_x = sign * value if grad_x is None else grad_x + sign * value
            advect = own[2] * grad_z[c, i]
            if grad_x is not None:
                advect = advect + own[0] * grad_x
            moved = acc_ref[c, i] + STEP * (VISC * lap - advect)
            moved_ref[c, i] = moved
            centred.append(0.5 * (own[c] + moved))
        cx, cy, cz = centred
        for p in range(problems):
            tx, ty, tz = tests_ref[p, 0, i] + waves[p][0], tests_ref[p, 1, i] + waves[p][1], tests_ref[p, 2, i]
            cross_ref[p, 0, i] = cx * tz - cz * tx
            cross_ref[p, 1, i] = cy * tz - cz * ty
            cross_ref[p, 2, i] = cx * ty - cy * tx
    for p in range(problems):
        for out, sign in ((low_out, 1.0), (high_out, -1.0)):
            for m in range(3):
                second = third = 0.0
                for d in range(m + 1, 4):
                    j = d - 1 - m if sign > 0 else nx + m - d
                    slope, bend = sign * STEP * FIRST[d - 1], STEP * DIFF * SECOND[d - 1]
                    second = second + (bend * tests_ref[p, 1, j] - slope * cross_ref[p, 2, j])
                    third = third + (bend * tests_ref[p, 2, j] - slope * cross_ref[p, 0, j])
                out[p, 0, m] = second
                out[p, 1, m] = third


def sums_kernel(places, cross_ref, sent_ref, tables_ref, inner_out, outer_out):
    problems, _, nx, ny, n = cross_ref.shape
    tables = Tables(tables_ref, places)
    lay = tables.get("lay_cross").astype(BF16)
    lines = nx * ny
    even = in_chip()
    for p in range(problems):
        at = 3 * p * lines
        added = lines_out(cross_ref[p, 0:2].reshape(-1, n), lay)
        for start, stop, sent in (
            (at, at + 2 * lines, sent_ref[:, at : at + 2 * lines] + added),
            (at + 2 * lines, at + 3 * lines, sent_ref[:, at + 2 * lines : at + 3 * lines]),
        ):
            inner_out[:, start:stop] = jnp.where(even, sent[0:4], sent[4:8])
            outer_out[:, start:stop] = jnp.where(even, sent[4:8], sent[0:4])


def curl_kernel(places, part_ref, cross_ref, low_ref, high_ref, tables_ref, out_ref, pad):
    problems, _, nx, ny, n = part_ref.shape
    tables = Tables(tables_ref, places)
    high, low = tables.pair("test_first")
    early = early_rows(part_ref.shape, ny // 2)[0]
    for p in range(problems):
        for c in range(2):
            total = three(cross_ref[p, c].reshape(-1, n), high, low)
            out_ref[p, c] = part_ref[p, c] + total.reshape(nx, ny, n)
        for i in range(nx):
            wrap(pad, 0, cross_ref[p, 1, i])
            wrap(pad, 1, cross_ref[p, 2, i])
            value = [out_ref[p, 0, i], out_ref[p, 1, i], part_ref[p, 2, i]]
            for k, first, second in zip((1, 2, 3), FIRST, SECOND):
                w = STEP * first
                value[0] = value[0] + w * (pad[1, 8 + k : 8 + k + ny] - pad[1, 8 - k : 8 - k + ny])
                value[2] = value[2] - w * (pad[0, 8 + k : 8 + k + ny] - pad[0, 8 - k : 8 - k + ny])
                for j, sign in ((i + k, w), (i - k, -w)):
                    if 0 <= j < nx:
                        value[1] = value[1] - sign * cross_ref[p, 2, j]
                        value[2] = value[2] - sign * cross_ref[p, 0, j]
                    else:
                        face, h = (low_ref, j + 3) if j < 0 else (high_ref, j - nx)
                        at = early[p, h]
                        value[0] = value[0] + (STEP * DIFF * second) * face[at : at + ny]
            for c in range(3):
                out_ref[p, c, i] = value[c]


def land_kernel(
    places, part_ref, inner_in, outer_in, tables_ref, moved_ref, out_ref, edge_ref, next_ref, held, sems
):
    problems, _, nx, ny, n = part_ref.shape
    land = Tables(tables_ref, places).get("land").astype(BF16)
    raw = taken_in(inner_in, outer_in)
    lines = nx * ny
    half = ny // 2
    mine = pl.ds(pl.multiple_of(lax.axis_index("sec") * half, half), half)
    copies = [pltpu.make_async_copy(moved_ref.at[:, :, mine], next_ref, sems.at[3 * problems])]
    copies[0].start()
    for p in range(problems):
        for c in range(3):
            at = (3 * p + c) * lines
            held[p, c] = part_ref[p, c] + lines_in(raw[:, at : at + lines], land).reshape(nx, ny, n)
            whole = pl.ds(0, nx) if c == 0 else pl.ds(3, nx - 6)
            copies.append(pltpu.make_async_copy(held.at[p, c, whole], out_ref.at[p, c, whole], sems.at[3 * p + c]))
            copies[-1].start()
            if c > 0:
                edge_ref[p, c - 1, 0:3] = held[p, c, 0:3]
                edge_ref[p, c - 1, 3:6] = held[p, c, nx - 3 : nx]
    for copy in copies:
        copy.wait()


def finish_kernel(edge_ref, low_ref, high_ref, _, out_ref, held, sems):
    problems = edge_ref.shape[0]
    nx = out_ref.shape[2]
    copies = []
    for p in range(problems):
        for c in range(2):
            held[p, c, 0:3] = edge_ref[p, c, 0:3] + low_ref[p, c]
            for m in range(3):
                held[p, c, 5 - m] = edge_ref[p, c, 5 - m] + high_ref[p, c, m]
            for side, start in ((0, 0), (1, nx - 3)):
                copies.append(
                    pltpu.make_async_copy(
                        held.at[p, c, pl.ds(3 * side, 3)],
                        out_ref.at[p, c + 1, pl.ds(start, 3)],
                        sems.at[4 * p + 2 * c + side],
                    )
                )
                copies[-1].start()
    for copy in copies:
        copy.wait()


def shifted(block, axis, distance):
    count = lax.axis_size(axis)
    return lax.ppermute(block, axis, [(i, (i + distance) % count) for i in range(count)])


def swapped(block, axis, first):
    count = lax.axis_size(axis)
    pairs = [(i % count, (i + 1) % count) for i in range(first, count + first, 2)]
    return lax.ppermute(block, axis, pairs + [(b, a) for a, b in pairs])


def shards(velocity, tests):
    _, nx, half, n = velocity.shape
    problems, _, _, ny, _ = tests.shape
    lines = nx * ny
    constants, places = make_tables(n, nx * lax.axis_size("gx"), ny, n * lax.axis_size("gz"))
    vmem = pl.BlockSpec(memory_space=pltpu.VMEM)

    def shape(*dims):
        return jax.ShapeDtypeStruct(dims, F32)

    def run(kernel, name, args, outs, scratch=(), flops=10**8, out_specs=None, bind=True, in_space=pltpu.VMEM, limit=VMEM_LIMIT, alias=None):
        body = kernel if not bind else (lambda *refs: kernel(places, *refs))
        moved = 4 * sum(math.prod(a.shape) for a in (*args, *outs))
        return pl.pallas_call(
            body,
            in_specs=[
                pl.BlockSpec(memory_space=pl.ANY if k in (alias or {}) else in_space) for k in range(len(args))
            ],
            input_output_aliases=alias or {},
            out_specs=[vmem] * len(outs) if out_specs is None else out_specs,
            out_shape=list(outs),
            scratch_shapes=list(scratch),
            compiler_params=pltpu.CompilerParams(vmem_limit_bytes=limit),
            cost_estimate=pl.CostEstimate(flops=flops, bytes_accessed=moved, transcendentals=0),
            name=name,
        )(*args)

    whole_shape = (3, nx, ny, n)
    tests_shape = (problems, 3, nx, ny, n)
    other = shifted(velocity, "sec", 1)
    (tables,) = run(tables_kernel, "tables", [jnp.asarray(constants)], [shape(*constants.shape)], bind=False)
    rows = early_rows(tests_shape, half)[2]
    low, high = run(
        faces_kernel, "faces", [tests, velocity], [shape(rows, n)] * 2,
        [pltpu.SemaphoreType.DMA((2 * problems + 2,))], bind=False, in_space=pl.ANY, limit=FACES_LIMIT,
    )
    early = [shifted(high, "gx", 1), shifted(low, "gx", -1)]
    part, sent = run(
        spread_kernel, "spread", [tests, tables],
        [shape(*tests_shape), shape(8, problems * 3 * lines)],
        [pltpu.VMEM((3, ny + 16, n), F32)], flops=10**9,
    )
    whole, low, high, inner, outer = run(
        whole_kernel, "whole", [velocity, other, tables, sent],
        [shape(*whole_shape)] + [shape(3, 3, half, n)] * 2 + [shape(4, 3 * lines)] * 2,
    )
    from_low = shifted(high, "gx", 1)
    from_high = shifted(low, "gx", -1)
    outer = swapped(outer, "gz", 1)
    inner = swapped(inner, "gz", 0)
    (acc,) = run(
        flow_kernel, "flow", [whole, tables], [shape(*whole_shape)],
        [pltpu.VMEM((3, ny + 16, n), F32), pltpu.VMEM(whole_shape, F32), pltpu.VMEM(whole_shape, F32)],
        flops=10**9,
    )
    moved, cross, low, high = run(
        step_kernel, "step", [whole, acc, *early, from_low, from_high, inner, outer, tests, tables],
        [shape(*whole_shape), shape(*tests_shape)] + [shape(problems, 2, 3, ny, n)] * 2,
        [pltpu.VMEM(whole_shape, F32)] * 2 + [pltpu.VMEM((3, 3, ny, n), F32)] * 2, flops=10**9,
    )
    from_low = shifted(high, "gx", 1)
    from_high = shifted(low, "gx", -1)
    inner, outer = run(
        sums_kernel, "sums", [cross, sent, tables], [shape(4, problems * 3 * lines)] * 2,
    )
    outer = swapped(outer, "gz", 1)
    inner = swapped(inner, "gz", 0)
    (part,) = run(
        curl_kernel, "curl", [part, cross, *early, tables], [shape(*tests_shape)],
        [pltpu.VMEM((2, ny + 16, n), F32)], flops=10**9,
    )
    any_space = pl.BlockSpec(memory_space=pl.ANY)
    edge_shape = (problems, 2, 6, ny, n)
    test_next, edge, velocity_next = run(
        land_kernel, "land", [part, inner, outer, tables, moved],
        [shape(*tests_shape), shape(*edge_shape), shape(3, nx, half, n)],
        [pltpu.VMEM(tests_shape, F32), pltpu.SemaphoreType.DMA((3 * problems + 1,))],
        out_specs=[any_space, pl.BlockSpec(memory_space=pltpu.VMEM), any_space],
    )
    (test_next,) = run(
        finish_kernel, "finish", [edge, from_low, from_high, test_next], [shape(*tests_shape)],
        [pltpu.VMEM(edge_shape, F32), pltpu.SemaphoreType.DMA((4 * problems,))],
        out_specs=[any_space], bind=False, alias={3: 0},
    )
    return velocity_next, test_next


def solution(mesh):
    placed = (P(None, "gx", "sec", "gz"), P("sec", None, "gx", None, "gz"))
    return jax.shard_map(shards, mesh=mesh, in_specs=placed, out_specs=placed, check_vma=False)
```

```python
import math

import jax
import jax.numpy as jnp
import numpy as np
from jax import lax
from jax.experimental import pallas as pl
from jax.experimental.pallas import tpu as pltpu
from jax.sharding import PartitionSpec as P

STEP = 0.2
VISC = 0.1
DIFF = 0.1
FIRST = (45.0 / 60.0, -9.0 / 60.0, 1.0 / 60.0)
SECOND = (270.0 / 180.0, -27.0 / 180.0, 2.0 / 180.0)
MID = -490.0 / 180.0
ROOT = math.sqrt(5.0 / 9.0)
DECAY = -(1.0 - ROOT) / (2.0 / 3.0)
VMEM_LIMIT = 12 * 1024 * 1024
F32 = jnp.float32
BF16 = jnp.bfloat16


def compact_weight(distance):
    d = np.asarray(distance)

    def green(k):
        return DECAY ** np.abs(k) / ROOT

    return 7.0 / 9.0 * (green(d + 1) - green(d - 1)) + 1.0 / 36.0 * (green(d + 2) - green(d - 2))


def second_weight(distance):
    table = np.array([MID, *SECOND, 0.0])
    return table[np.minimum(np.abs(distance), 4)]


TAIL = float(compact_weight(2)) / DECAY**2
CORNER = float(compact_weight(1)) - TAIL * DECAY


def halves(table):
    table = np.asarray(table, np.float32)
    high = np.asarray(np.asarray(table, jnp.bfloat16), np.float32)
    low = np.asarray(np.asarray(table - high, jnp.bfloat16), np.float32)
    return high, low


def make_tables(n, x_total, y_total, z_total):
    j = np.arange(n)
    gap = j[None, :] - j[:, None]
    inner_first = compact_weight(gap)
    inner_second = second_weight(gap)
    pick = np.zeros((8, n))
    for k in range(3):
        pick[k, n - 1 - k] = 1.0
        pick[4 + k, k] = 1.0
    pick[3] = DECAY ** (n - 1 - j)
    pick[7] = DECAY**j
    spread_first = np.zeros((8, n))
    spread_second = np.zeros((8, n))
    for k in range(3):
        for z in range(3 - k):
            spread_second[k, z] = SECOND[z + k]
            spread_second[4 + k, n - 1 - z] = SECOND[z + k]
    spread_first[0, 0] = CORNER
    spread_first[4, n - 1] = -CORNER
    spread_first[3] = TAIL * DECAY ** (j + 1)
    spread_first[7] = -TAIL * DECAY ** (n - j)
    lay_test = np.zeros((8, n))
    lay_cross = np.zeros((8, n))
    for z in range(3):
        for k in range(3 - z):
            lay_test[z, n - 1 - k] = STEP * DIFF * SECOND[z + k]
            lay_test[4 + z, k] = STEP * DIFF * SECOND[z + k]
    lay_cross[0, n - 1] = STEP * CORNER
    lay_cross[4, 0] = -STEP * CORNER
    lay_cross[3] = STEP * DECAY ** (n - 1 - j)
    lay_cross[7] = STEP * DECAY**j
    land = np.zeros((8, n))
    for z in range(3):
        land[z, z] = 1.0
        land[4 + z, n - 1 - z] = 1.0
    land[3] = spread_first[3]
    land[7] = spread_first[7]

    def stacked(table):
        high, low = halves(table)
        return np.concatenate([high, high, low, np.zeros_like(high)])

    def wide(column):
        return np.broadcast_to(np.asarray(column)[:, None], (len(column), n))

    phase_x = 2.0 * math.pi / x_total * np.arange(x_total)
    phase_y = 2.0 * math.pi / y_total * np.arange(y_total)
    angle = 2.0 * math.pi / z_total * np.arange(z_total)
    parts = {
        "pick": np.concatenate(halves(pick)),
        "lay_test": np.concatenate(halves(lay_test)),
        "lay_cross": np.concatenate(halves(lay_cross)),
        "spread_first": stacked(spread_first),
        "spread_second": stacked(spread_second),
        "land": stacked(land),
        "flow_first": np.concatenate(halves(inner_first)),
        "flow_second": np.concatenate(halves(inner_second)),
        "test_first": np.concatenate(halves(STEP * inner_first)),
        "test_second": np.concatenate(halves(STEP * DIFF * inner_second)),
        "sin_x": wide(np.sin(phase_x)),
        "cos_x": wide(np.cos(phase_x)),
        "sin_y": wide(np.sin(phase_y)),
        "cos_y": wide(np.cos(phase_y)),
        "wave": np.concatenate([np.cos(angle), np.sin(angle)]).reshape(-1, n),
    }
    places, rows = {}, 0
    for name, part in parts.items():
        places[name] = (rows, len(part))
        rows += len(part)
    return np.concatenate(list(parts.values())).astype(np.float32), places


def split(values):
    high = values.astype(BF16)
    low = (values - high.astype(F32)).astype(BF16)
    return high, low


def dot(a, b):
    return jnp.dot(a, b, preferred_element_type=F32)


def three(values, high, low):
    a, b = split(values)
    return dot(a, high) + dot(b, high) + dot(a, low)


def lines_out(values, both):
    a, b = split(values)
    nt = (((1,), (1,)), ((), ()))
    main = lax.dot_general(both, a, nt, preferred_element_type=F32)
    rest = lax.dot_general(both, b, nt, preferred_element_type=F32)
    return main[0:8] + main[8:16] + rest[0:8]


def lines_in(raw, tables):
    high = raw.astype(BF16).astype(F32)
    low = raw - high
    packed = jnp.concatenate([high, low, high, jnp.zeros_like(high)], 0).astype(BF16)
    return lax.dot_general(packed, tables, (((0,), (0,)), ((), ())), preferred_element_type=F32)


class Tables:
    def __init__(self, ref, places):
        self.ref = ref
        self.places = places

    def get(self, name):
        start, rows = self.places[name]
        return self.ref[start : start + rows]

    def pair(self, name):
        start, rows = self.places[name]
        half = rows // 2
        return self.ref[start : start + half].astype(BF16), self.ref[start + half : start + rows].astype(BF16)

    def row(self, name, index):
        return self.ref[pl.ds(self.places[name][0] + index, 1)]


def in_chip():
    return lax.rem(lax.axis_index("gz"), 2) == 0


def hand_out(sent, inner_ref, outer_ref):
    even = in_chip()
    inner_ref[...] = jnp.where(even, sent[0:4], sent[4:8])
    outer_ref[...] = jnp.where(even, sent[4:8], sent[0:4])


def taken_in(inner_ref, outer_ref):
    even = in_chip()
    left = jnp.where(even, outer_ref[...], inner_ref[...])
    right = jnp.where(even, inner_ref[...], outer_ref[...])
    return jnp.concatenate([left, right], 0)


def wave_parts(tables, problem, slabs):
    wave = tables.row("wave", problem * slabs + lax.axis_index("gz"))
    first = lax.axis_index("sec") == 0
    return jnp.where(first, wave, 0.0), jnp.where(first, 0.0, wave)


def wrap(pad, k, values):
    ny = values.shape[0]
    pad[k, 0:8] = values[ny - 8 : ny]
    pad[k, 8 : 8 + ny] = values
    pad[k, 8 + ny : 16 + ny] = values[0:8]


def tables_kernel(source, out):
    out[...] = source[...]


def faces_kernel(ref, low_ref, high_ref):
    nx = ref.shape[-3]
    low_ref[...] = ref[..., 0:3, :, :]
    high_ref[...] = ref[..., nx - 3 : nx, :, :]


def pack_kernel(first, second, out):
    out[0] = first[...]
    out[1] = second[...]


def spread_kernel(places, tests_ref, tables_ref, out_ref, sent_ref, pad):
    problems, _, nx, ny, n = tests_ref.shape
    tables = Tables(tables_ref, places)
    high, low = tables.pair("test_second")
    lay = tables.get("lay_test").astype(BF16)
    lines = nx * ny
    for p in range(problems):
        for c in range(3):
            flat = tests_ref[p, c].reshape(lines, n)
            out_ref[p, c] = three(flat, high, low).reshape(nx, ny, n)
            at = (3 * p + c) * lines
            sent_ref[:, at : at + lines] = lines_out(flat, lay)
        for i in range(nx):
            for c in range(3):
                wrap(pad, c, tests_ref[p, c, i])
            for c in range(3):
                value = out_ref[p, c, i] + (1.0 + STEP * DIFF * 2.0 * MID) * tests_ref[p, c, i]
                for k, w in zip((1, 2, 3), SECOND):
                    near = pad[c, 8 + k : 8 + k + ny] + pad[c, 8 - k : 8 - k + ny]
                    for j in (i + k, i - k):
                        if 0 <= j < nx:
                            near = near + tests_ref[p, c, j]
                    value = value + (STEP * DIFF * w) * near
                out_ref[p, c, i] = value


def whole_kernel(places, own_ref, other_ref, tables_ref, whole_ref, inner_ref, outer_ref):
    _, nx, half, n = own_ref.shape
    section = lax.axis_index("sec")
    whole_ref[:, :, pl.ds(pl.multiple_of(section * half, half), half)] = own_ref[...]
    whole_ref[:, :, pl.ds(pl.multiple_of((1 - section) * half, half), half)] = other_ref[...]
    pick = Tables(tables_ref, places).get("pick").astype(BF16)
    hand_out(lines_out(whole_ref[...].reshape(-1, n), pick), inner_ref, outer_ref)


def flow_kernel(places, whole_ref, tables_ref, acc_ref, pad, grad_z, lap_z):
    _, nx, ny, n = whole_ref.shape
    tables = Tables(tables_ref, places)
    flat = whole_ref[...].reshape(-1, n)
    grad_z[...] = three(flat, *tables.pair("flow_first")).reshape(grad_z.shape)
    lap_z[...] = three(flat, *tables.pair("flow_second")).reshape(lap_z.shape)
    sin_y, cos_y = tables.get("sin_y"), tables.get("cos_y")
    column = lax.axis_index("gx") * nx
    for i in range(nx):
        sin_x, cos_x = tables.row("sin_x", column + i), tables.row("cos_x", column + i)
        drive = (sin_x * cos_y, -(cos_x * sin_y), math.sqrt(2.0) * (sin_x * sin_y))
        for c in range(3):
            wrap(pad, c, whole_ref[c, i])
        own = [whole_ref[c, i] for c in range(3)]
        for c in range(3):
            grad_x = grad_y = None
            lap = lap_z[c, i] + (2.0 * MID) * own[c]
            for k, first, second in zip((1, 2, 3), FIRST, SECOND):
                up, down = pad[c, 8 + k : 8 + k + ny], pad[c, 8 - k : 8 - k + ny]
                term = first * (up - down)
                grad_y = term if grad_y is None else grad_y + term
                near = up + down
                for j, sign in ((i + k, first), (i - k, -first)):
                    if 0 <= j < nx:
                        value = whole_ref[c, j]
                        near = near + value
                        grad_x = sign * value if grad_x is None else grad_x + sign * value
                lap = lap + second * near
            advect = own[0] * grad_x + own[1] * grad_y + own[2] * grad_z[c, i]
            acc_ref[c, i] = own[c] + STEP * (VISC * lap - advect + drive[c])


def local_kernel(places, whole_ref, tests_ref, tables_ref, acc_ref, part_ref, sent_ref, pad, grad_z, lap_z):
    flow_kernel(places, whole_ref, tables_ref, acc_ref, pad, grad_z, lap_z)
    spread_kernel(places, tests_ref, tables_ref, part_ref, sent_ref, pad)


def step_kernel(
    places, whole_ref, acc_ref, low_own, high_own, other_faces, inner_in, outer_in, tests_ref,
    tables_ref, moved_ref, cross_ref, low_out, high_out, grad_z, lap_z, low_ref, high_ref,
):
    _, nx, ny, n = whole_ref.shape
    half = ny // 2
    problems = tests_ref.shape[0]
    section = lax.axis_index("sec")
    mine = pl.ds(pl.multiple_of(section * half, half), half)
    theirs = pl.ds(pl.multiple_of((1 - section) * half, half), half)
    for side, (face, faces_own) in enumerate(((low_ref, low_own), (high_ref, high_own))):
        face[:, :, mine] = faces_own[...]
        face[:, :, theirs] = other_faces[side]
    tables = Tables(tables_ref, places)
    raw = taken_in(inner_in, outer_in)
    grad_z[...] = lines_in(raw, tables.get("spread_first").astype(BF16)).reshape(grad_z.shape)
    lap_z[...] = lines_in(raw, tables.get("spread_second").astype(BF16)).reshape(lap_z.shape)
    waves = [wave_parts(tables, p, places["wave"][1] // 2) for p in range(problems)]
    for i in range(nx):
        own = [whole_ref[c, i] for c in range(3)]
        centred = []
        for c in range(3):
            lap, grad_x = lap_z[c, i], None
            for k, first, second in zip((1, 2, 3), FIRST, SECOND):
                for j, sign in ((i + k, first), (i - k, -first)):
                    if not 0 <= j < nx:
                        value = low_ref[c, j + 3] if j < 0 else high_ref[c, j - nx]
                        lap = lap + second * value
                        grad_x = sign * value if grad_x is None else grad_x + sign * value
            advect = own[2] * grad_z[c, i]
            if grad_x is not None:
                advect = advect + own[0] * grad_x
            moved = acc_ref[c, i] + STEP * (VISC * lap - advect)
            moved_ref[c, i] = moved
            centred.append(0.5 * (own[c] + moved))
            if i < 3:
                low_out[c, i] = centred[c]
            if i >= nx - 3:
                high_out[c, i - nx + 3] = centred[c]
        cx, cy, cz = centred
        for p in range(problems):
            tx, ty, tz = tests_ref[p, 0, i] + waves[p][0], tests_ref[p, 1, i] + waves[p][1], tests_ref[p, 2, i]
            cross_ref[p, 0, i] = cx * tz - cz * tx
            cross_ref[p, 1, i] = cy * tz - cz * ty
            cross_ref[p, 2, i] = cx * ty - cy * tx


def sums_kernel(places, cross_ref, sent_ref, tables_ref, inner_out, outer_out):
    problems, _, nx, ny, n = cross_ref.shape
    tables = Tables(tables_ref, places)
    lay = tables.get("lay_cross").astype(BF16)
    lines = nx * ny
    even = in_chip()
    for p in range(problems):
        at = 3 * p * lines
        added = lines_out(cross_ref[p, 0:2].reshape(-1, n), lay)
        for start, stop, sent in (
            (at, at + 2 * lines, sent_ref[:, at : at + 2 * lines] + added),
            (at + 2 * lines, at + 3 * lines, sent_ref[:, at + 2 * lines : at + 3 * lines]),
        ):
            inner_out[:, start:stop] = jnp.where(even, sent[0:4], sent[4:8])
            outer_out[:, start:stop] = jnp.where(even, sent[4:8], sent[0:4])


def curl_kernel(places, part_ref, cross_ref, low_ref, high_ref, tables_ref, out_ref, pad):
    problems, _, nx, ny, n = part_ref.shape
    tables = Tables(tables_ref, places)
    high, low = tables.pair("test_first")
    for p in range(problems):
        for c in range(2):
            total = three(cross_ref[p, c].reshape(-1, n), high, low)
            out_ref[p, c] = part_ref[p, c] + total.reshape(nx, ny, n)
        for i in range(nx):
            wrap(pad, 0, cross_ref[p, 1, i])
            wrap(pad, 1, cross_ref[p, 2, i])
            value = [out_ref[p, 0, i], out_ref[p, 1, i], part_ref[p, 2, i]]
            for k, first, second in zip((1, 2, 3), FIRST, SECOND):
                w = STEP * first
                value[0] = value[0] + w * (pad[1, 8 + k : 8 + k + ny] - pad[1, 8 - k : 8 - k + ny])
                value[2] = value[2] - w * (pad[0, 8 + k : 8 + k + ny] - pad[0, 8 - k : 8 - k + ny])
                for j, sign in ((i + k, w), (i - k, -w)):
                    if 0 <= j < nx:
                        value[1] = value[1] - sign * cross_ref[p, 2, j]
                        value[2] = value[2] - sign * cross_ref[p, 0, j]
                    else:
                        face, h = (low_ref, j + 3) if j < 0 else (high_ref, j - nx)
                        for c in range(3):
                            value[c] = value[c] + (STEP * DIFF * second) * face[p, c, h]
            for c in range(3):
                out_ref[p, c, i] = value[c]


def finish_kernel(
    places, part_ref, inner_in, outer_in, t_low, t_high, c_low, c_high, moved_ref, tables_ref,
    out_ref, next_ref, held, cross, sems,
):
    problems, _, nx, ny, n = part_ref.shape
    tables = Tables(tables_ref, places)
    land = tables.get("land").astype(BF16)
    raw = taken_in(inner_in, outer_in)
    lines = nx * ny
    half = ny // 2
    mine = pl.ds(pl.multiple_of(lax.axis_index("sec") * half, half), half)
    copies = [pltpu.make_async_copy(moved_ref.at[:, :, mine], next_ref, sems.at[3 * problems])]
    copies[0].start()
    for p in range(problems):
        for c in range(3):
            at = (3 * p + c) * lines
            held[p, c] = part_ref[p, c] + lines_in(raw[:, at : at + lines], land).reshape(nx, ny, n)
            if c == 0:
                copies.append(pltpu.make_async_copy(held.at[p, c], out_ref.at[p, c], sems.at[3 * p]))
                copies[-1].start()
        wave_x, wave_y = wave_parts(tables, p, places["wave"][1] // 2)
        for side, (t_ref, c_ref, sign) in enumerate(((t_low, c_low, -STEP), (t_high, c_high, STEP))):
            for h in range(3):
                cx, cy, cz = c_ref[0, h], c_ref[1, h], c_ref[2, h]
                tx, ty, tz = t_ref[p, 0, h] + wave_x, t_ref[p, 1, h] + wave_y, t_ref[p, 2, h]
                cross[0, h] = cz * tx - cx * tz
                cross[1, h] = cx * ty - cy * tx
            for m in range(3):
                i = m if side == 0 else nx - 1 - m
                second, third = held[p, 1, i], held[p, 2, i]
                for d in range(m + 1, 4):
                    h = 3 + m - d if side == 0 else d - 1 - m
                    second = second - (sign * FIRST[d - 1]) * cross[1, h]
                    third = third + (sign * FIRST[d - 1]) * cross[0, h]
                held[p, 1, i] = second
                held[p, 2, i] = third
        for c in (1, 2):
            copies.append(pltpu.make_async_copy(held.at[p, c], out_ref.at[p, c], sems.at[3 * p + c]))
            copies[-1].start()
    for copy in copies:
        copy.wait()


def shifted(block, axis, distance):
    count = lax.axis_size(axis)
    return lax.ppermute(block, axis, [(i, (i + distance) % count) for i in range(count)])


def swapped(block, axis, first):
    count = lax.axis_size(axis)
    pairs = [(i % count, (i + 1) % count) for i in range(first, count + first, 2)]
    return lax.ppermute(block, axis, pairs + [(b, a) for a, b in pairs])


def shards(velocity, tests):
    _, nx, half, n = velocity.shape
    problems, _, _, ny, _ = tests.shape
    lines = nx * ny
    constants, places = make_tables(n, nx * lax.axis_size("gx"), ny, n * lax.axis_size("gz"))
    vmem = pl.BlockSpec(memory_space=pltpu.VMEM)

    def shape(*dims):
        return jax.ShapeDtypeStruct(dims, F32)

    def run(kernel, name, args, outs, scratch=(), flops=10**8, out_specs=None, bind=True):
        body = kernel if not bind else (lambda *refs: kernel(places, *refs))
        moved = 4 * sum(math.prod(a.shape) for a in (*args, *outs))
        return pl.pallas_call(
            body,
            in_specs=[vmem] * len(args),
            out_specs=[vmem] * len(outs) if out_specs is None else out_specs,
            out_shape=list(outs),
            scratch_shapes=list(scratch),
            compiler_params=pltpu.CompilerParams(vmem_limit_bytes=VMEM_LIMIT),
            cost_estimate=pl.CostEstimate(flops=flops, bytes_accessed=moved, transcendentals=0),
            name=name,
        )(*args)

    whole_shape = (3, nx, ny, n)
    tests_shape = (problems, 3, nx, ny, n)
    other = shifted(velocity, "sec", 1)
    (tables,) = run(tables_kernel, "tables", [jnp.asarray(constants)], [shape(*constants.shape)], bind=False)
    v_low, v_high = run(faces_kernel, "flow_faces", [velocity], [shape(3, 3, half, n)] * 2, bind=False)
    v_own = [shifted(v_high, "gx", 1), shifted(v_low, "gx", -1)]
    t_low, t_high = run(faces_kernel, "test_faces", [tests], [shape(problems, 3, 3, ny, n)] * 2, bind=False)
    t_faces = [shifted(t_high, "gx", 1), shifted(t_low, "gx", -1)]
    (packed,) = run(pack_kernel, "pack", v_own, [shape(2, 3, 3, half, n)], bind=False)
    v_other = shifted(packed, "sec", 1)
    whole, inner, outer = run(
        whole_kernel, "whole", [velocity, other, tables],
        [shape(*whole_shape)] + [shape(4, 3 * lines)] * 2,
    )
    outer = swapped(outer, "gz", 1)
    inner = swapped(inner, "gz", 0)
    acc, part, sent = run(
        local_kernel, "local", [whole, tests, tables],
        [shape(*whole_shape), shape(*tests_shape), shape(8, problems * 3 * lines)],
        [pltpu.VMEM((3, ny + 16, n), F32), pltpu.VMEM(whole_shape, F32), pltpu.VMEM(whole_shape, F32)],
        flops=4 * 10**9,
    )
    moved, cross, low, high = run(
        step_kernel, "step", [whole, acc, *v_own, v_other, inner, outer, tests, tables],
        [shape(*whole_shape), shape(*tests_shape)] + [shape(3, 3, ny, n)] * 2,
        [pltpu.VMEM(whole_shape, F32)] * 2 + [pltpu.VMEM((3, 3, ny, n), F32)] * 2, flops=10**9,
    )
    from_low = shifted(high, "gx", 1)
    from_high = shifted(low, "gx", -1)
    inner, outer = run(
        sums_kernel, "sums", [cross, sent, tables], [shape(4, problems * 3 * lines)] * 2,
    )
    outer = swapped(outer, "gz", 1)
    inner = swapped(inner, "gz", 0)
    (part,) = run(
        curl_kernel, "curl", [part, cross, *t_faces, tables], [shape(*tests_shape)],
        [pltpu.VMEM((2, ny + 16, n), F32)], flops=10**9,
    )
    test_next, velocity_next = run(
        finish_kernel, "finish",
        [part, inner, outer, *t_faces, from_low, from_high, moved, tables],
        [shape(*tests_shape), shape(3, nx, half, n)],
        [
            pltpu.VMEM(tests_shape, F32), pltpu.VMEM((2, 3, ny, n), F32),
            pltpu.SemaphoreType.DMA((3 * problems + 1,)),
        ],
        out_specs=[pl.BlockSpec(memory_space=pl.ANY)] * 2,
    )
    return velocity_next, test_next


def solution(mesh):
    placed = (P(None, "gx", "sec", "gz"), P("sec", None, "gx", None, "gz"))
    return jax.shard_map(shards, mesh=mesh, in_specs=placed, out_specs=placed, check_vma=False)
```

```python
import math

import jax
import jax.numpy as jnp
import numpy as np
from jax import lax
from jax.experimental import pallas as pl
from jax.experimental.pallas import tpu as pltpu
from jax.sharding import PartitionSpec as P

STEP = 0.2
VISC = 0.1
DIFF = 0.1
FIRST = (45.0 / 60.0, -9.0 / 60.0, 1.0 / 60.0)
SECOND = (270.0 / 180.0, -27.0 / 180.0, 2.0 / 180.0)
MID = -490.0 / 180.0
ROOT = math.sqrt(5.0 / 9.0)
DECAY = -(1.0 - ROOT) / (2.0 / 3.0)
VMEM_LIMIT = 12 * 1024 * 1024
F32 = jnp.float32
BF16 = jnp.bfloat16


def compact_weight(distance):
    d = np.asarray(distance)

    def green(k):
        return DECAY ** np.abs(k) / ROOT

    return 7.0 / 9.0 * (green(d + 1) - green(d - 1)) + 1.0 / 36.0 * (green(d + 2) - green(d - 2))


def second_weight(distance):
    table = np.array([MID, *SECOND, 0.0])
    return table[np.minimum(np.abs(distance), 4)]


TAIL = float(compact_weight(2)) / DECAY**2
CORNER = float(compact_weight(1)) - TAIL * DECAY


def halves(table):
    table = np.asarray(table, np.float32)
    high = np.asarray(np.asarray(table, jnp.bfloat16), np.float32)
    low = np.asarray(np.asarray(table - high, jnp.bfloat16), np.float32)
    return high, low


def make_tables(n, x_total, y_total, z_total):
    j = np.arange(n)
    gap = j[None, :] - j[:, None]
    inner_first = compact_weight(gap)
    inner_second = second_weight(gap)
    pick = np.zeros((8, n))
    for k in range(3):
        pick[k, n - 1 - k] = 1.0
        pick[4 + k, k] = 1.0
    pick[3] = DECAY ** (n - 1 - j)
    pick[7] = DECAY**j
    spread_first = np.zeros((8, n))
    spread_second = np.zeros((8, n))
    for k in range(3):
        for z in range(3 - k):
            spread_second[k, z] = SECOND[z + k]
            spread_second[4 + k, n - 1 - z] = SECOND[z + k]
    spread_first[0, 0] = CORNER
    spread_first[4, n - 1] = -CORNER
    spread_first[3] = TAIL * DECAY ** (j + 1)
    spread_first[7] = -TAIL * DECAY ** (n - j)
    lay_test = np.zeros((8, n))
    lay_cross = np.zeros((8, n))
    for z in range(3):
        for k in range(3 - z):
            lay_test[z, n - 1 - k] = STEP * DIFF * SECOND[z + k]
            lay_test[4 + z, k] = STEP * DIFF * SECOND[z + k]
    lay_cross[0, n - 1] = STEP * CORNER
    lay_cross[4, 0] = -STEP * CORNER
    lay_cross[3] = STEP * DECAY ** (n - 1 - j)
    lay_cross[7] = STEP * DECAY**j
    land = np.zeros((8, n))
    for z in range(3):
        land[z, z] = 1.0
        land[4 + z, n - 1 - z] = 1.0
    land[3] = spread_first[3]
    land[7] = spread_first[7]

    def stacked(table):
        high, low = halves(table)
        return np.concatenate([high, high, low, np.zeros_like(high)])

    def wide(column):
        return np.broadcast_to(np.asarray(column)[:, None], (len(column), n))

    phase_x = 2.0 * math.pi / x_total * np.arange(x_total)
    phase_y = 2.0 * math.pi / y_total * np.arange(y_total)
    angle = 2.0 * math.pi / z_total * np.arange(z_total)
    parts = {
        "pick": np.concatenate(halves(pick)),
        "lay_test": np.concatenate(halves(lay_test)),
        "lay_cross": np.concatenate(halves(lay_cross)),
        "spread_first": stacked(spread_first),
        "spread_second": stacked(spread_second),
        "land": stacked(land),
        "flow_first": np.concatenate(halves(inner_first)),
        "flow_second": np.concatenate(halves(inner_second)),
        "test_first": np.concatenate(halves(STEP * inner_first)),
        "test_second": np.concatenate(halves(STEP * DIFF * inner_second)),
        "sin_x": wide(np.sin(phase_x)),
        "cos_x": wide(np.cos(phase_x)),
        "sin_y": wide(np.sin(phase_y)),
        "cos_y": wide(np.cos(phase_y)),
        "wave": np.concatenate([np.cos(angle), np.sin(angle)]).reshape(-1, n),
    }
    places, rows = {}, 0
    for name, part in parts.items():
        places[name] = (rows, len(part))
        rows += len(part)
    return np.concatenate(list(parts.values())).astype(np.float32), places


def split(values):
    high = values.astype(BF16)
    low = (values - high.astype(F32)).astype(BF16)
    return high, low


def dot(a, b):
    return jnp.dot(a, b, preferred_element_type=F32)


def three(values, high, low):
    a, b = split(values)
    return dot(a, high) + dot(b, high) + dot(a, low)


def lines_out(values, both):
    a, b = split(values)
    nt = (((1,), (1,)), ((), ()))
    main = lax.dot_general(both, a, nt, preferred_element_type=F32)
    rest = lax.dot_general(both, b, nt, preferred_element_type=F32)
    return main[0:8] + main[8:16] + rest[0:8]


def lines_in(raw, tables):
    high = raw.astype(BF16).astype(F32)
    low = raw - high
    packed = jnp.concatenate([high, low, high, jnp.zeros_like(high)], 0).astype(BF16)
    return lax.dot_general(packed, tables, (((0,), (0,)), ((), ())), preferred_element_type=F32)


class Tables:
    def __init__(self, ref, places):
        self.ref = ref
        self.places = places

    def get(self, name):
        start, rows = self.places[name]
        return self.ref[start : start + rows]

    def pair(self, name):
        start, rows = self.places[name]
        half = rows // 2
        return self.ref[start : start + half].astype(BF16), self.ref[start + half : start + rows].astype(BF16)

    def row(self, name, index):
        return self.ref[pl.ds(self.places[name][0] + index, 1)]


def in_chip():
    return lax.rem(lax.axis_index("gz"), 2) == 0


def hand_out(sent, inner_ref, outer_ref):
    even = in_chip()
    inner_ref[...] = jnp.where(even, sent[0:4], sent[4:8])
    outer_ref[...] = jnp.where(even, sent[4:8], sent[0:4])


def taken_in(inner_ref, outer_ref):
    even = in_chip()
    left = jnp.where(even, outer_ref[...], inner_ref[...])
    right = jnp.where(even, inner_ref[...], outer_ref[...])
    return jnp.concatenate([left, right], 0)


def wave_parts(tables, problem, slabs):
    wave = tables.row("wave", problem * slabs + lax.axis_index("gz"))
    first = lax.axis_index("sec") == 0
    return jnp.where(first, wave, 0.0), jnp.where(first, 0.0, wave)


def wrap(pad, k, values):
    ny = values.shape[0]
    pad[k, 0:8] = values[ny - 8 : ny]
    pad[k, 8 : 8 + ny] = values
    pad[k, 8 + ny : 16 + ny] = values[0:8]


def tables_kernel(source, out):
    out[...] = source[...]


def faces_kernel(ref, low_ref, high_ref):
    nx = ref.shape[-3]
    low_ref[...] = ref[..., 0:3, :, :]
    high_ref[...] = ref[..., nx - 3 : nx, :, :]


def pack_kernel(first, second, out):
    out[0] = first[...]
    out[1] = second[...]


def spread_kernel(places, tests_ref, tables_ref, out_ref, sent_ref, pad):
    problems, _, nx, ny, n = tests_ref.shape
    tables = Tables(tables_ref, places)
    high, low = tables.pair("test_second")
    lay = tables.get("lay_test").astype(BF16)
    lines = nx * ny
    for p in range(problems):
        for c in range(3):
            flat = tests_ref[p, c].reshape(lines, n)
            out_ref[p, c] = three(flat, high, low).reshape(nx, ny, n)
            at = (3 * p + c) * lines
            sent_ref[:, at : at + lines] = lines_out(flat, lay)
        for i in range(nx):
            for c in range(3):
                wrap(pad, c, tests_ref[p, c, i])
            for c in range(3):
                value = out_ref[p, c, i] + (1.0 + STEP * DIFF * 2.0 * MID) * tests_ref[p, c, i]
                for k, w in zip((1, 2, 3), SECOND):
                    near = pad[c, 8 + k : 8 + k + ny] + pad[c, 8 - k : 8 - k + ny]
                    for j in (i + k, i - k):
                        if 0 <= j < nx:
                            near = near + tests_ref[p, c, j]
                    value = value + (STEP * DIFF * w) * near
                out_ref[p, c, i] = value


def whole_kernel(places, own_ref, other_ref, tables_ref, whole_ref, inner_ref, outer_ref):
    _, nx, half, n = own_ref.shape
    section = lax.axis_index("sec")
    whole_ref[:, :, pl.ds(pl.multiple_of(section * half, half), half)] = own_ref[...]
    whole_ref[:, :, pl.ds(pl.multiple_of((1 - section) * half, half), half)] = other_ref[...]
    pick = Tables(tables_ref, places).get("pick").astype(BF16)
    hand_out(lines_out(whole_ref[...].reshape(-1, n), pick), inner_ref, outer_ref)


def flow_kernel(places, whole_ref, tables_ref, acc_ref, pad, grad_z, lap_z):
    _, nx, ny, n = whole_ref.shape
    tables = Tables(tables_ref, places)
    flat = whole_ref[...].reshape(-1, n)
    grad_z[...] = three(flat, *tables.pair("flow_first")).reshape(grad_z.shape)
    lap_z[...] = three(flat, *tables.pair("flow_second")).reshape(lap_z.shape)
    sin_y, cos_y = tables.get("sin_y"), tables.get("cos_y")
    column = lax.axis_index("gx") * nx
    for i in range(nx):
        sin_x, cos_x = tables.row("sin_x", column + i), tables.row("cos_x", column + i)
        drive = (sin_x * cos_y, -(cos_x * sin_y), math.sqrt(2.0) * (sin_x * sin_y))
        for c in range(3):
            wrap(pad, c, whole_ref[c, i])
        own = [whole_ref[c, i] for c in range(3)]
        for c in range(3):
            grad_x = grad_y = None
            lap = lap_z[c, i] + (2.0 * MID) * own[c]
            for k, first, second in zip((1, 2, 3), FIRST, SECOND):
                up, down = pad[c, 8 + k : 8 + k + ny], pad[c, 8 - k : 8 - k + ny]
                term = first * (up - down)
                grad_y = term if grad_y is None else grad_y + term
                near = up + down
                for j, sign in ((i + k, first), (i - k, -first)):
                    if 0 <= j < nx:
                        value = whole_ref[c, j]
                        near = near + value
                        grad_x = sign * value if grad_x is None else grad_x + sign * value
                lap = lap + second * near
            advect = own[0] * grad_x + own[1] * grad_y + own[2] * grad_z[c, i]
            acc_ref[c, i] = own[c] + STEP * (VISC * lap - advect + drive[c])


def local_kernel(places, whole_ref, tests_ref, tables_ref, acc_ref, part_ref, sent_ref, pad, grad_z, lap_z):
    flow_kernel(places, whole_ref, tables_ref, acc_ref, pad, grad_z, lap_z)
    spread_kernel(places, tests_ref, tables_ref, part_ref, sent_ref, pad)


def step_kernel(
    places, whole_ref, acc_ref, low_own, high_own, other_faces, inner_in, outer_in, tests_ref,
    tables_ref, moved_ref, cross_ref, low_out, high_out, grad_z, lap_z, low_ref, high_ref,
):
    _, nx, ny, n = whole_ref.shape
    half = ny // 2
    problems = tests_ref.shape[0]
    section = lax.axis_index("sec")
    mine = pl.ds(pl.multiple_of(section * half, half), half)
    theirs = pl.ds(pl.multiple_of((1 - section) * half, half), half)
    for side, (face, faces_own) in enumerate(((low_ref, low_own), (high_ref, high_own))):
        face[:, :, mine] = faces_own[...]
        face[:, :, theirs] = other_faces[side]
    tables = Tables(tables_ref, places)
    raw = taken_in(inner_in, outer_in)
    grad_z[...] = lines_in(raw, tables.get("spread_first").astype(BF16)).reshape(grad_z.shape)
    lap_z[...] = lines_in(raw, tables.get("spread_second").astype(BF16)).reshape(lap_z.shape)
    waves = [wave_parts(tables, p, places["wave"][1] // 2) for p in range(problems)]
    for i in range(nx):
        own = [whole_ref[c, i] for c in range(3)]
        centred = []
        for c in range(3):
            lap, grad_x = lap_z[c, i], None
            for k, first, second in zip((1, 2, 3), FIRST, SECOND):
                for j, sign in ((i + k, first), (i - k, -first)):
                    if not 0 <= j < nx:
                        value = low_ref[c, j + 3] if j < 0 else high_ref[c, j - nx]
                        lap = lap + second * value
                        grad_x = sign * value if grad_x is None else grad_x + sign * value
            advect = own[2] * grad_z[c, i]
            if grad_x is not None:
                advect = advect + own[0] * grad_x
            moved = acc_ref[c, i] + STEP * (VISC * lap - advect)
            moved_ref[c, i] = moved
            centred.append(0.5 * (own[c] + moved))
            if i < 3:
                low_out[c, i] = centred[c]
            if i >= nx - 3:
                high_out[c, i - nx + 3] = centred[c]
        cx, cy, cz = centred
        for p in range(problems):
            tx, ty, tz = tests_ref[p, 0, i] + waves[p][0], tests_ref[p, 1, i] + waves[p][1], tests_ref[p, 2, i]
            cross_ref[p, 0, i] = cx * tz - cz * tx
            cross_ref[p, 1, i] = cy * tz - cz * ty
            cross_ref[p, 2, i] = cx * ty - cy * tx


def sums_kernel(places, cross_ref, sent_ref, tables_ref, inner_out, outer_out):
    problems, _, nx, ny, n = cross_ref.shape
    tables = Tables(tables_ref, places)
    lay = tables.get("lay_cross").astype(BF16)
    lines = nx * ny
    even = in_chip()
    for p in range(problems):
        at = 3 * p * lines
        added = lines_out(cross_ref[p, 0:2].reshape(-1, n), lay)
        for start, stop, sent in (
            (at, at + 2 * lines, sent_ref[:, at : at + 2 * lines] + added),
            (at + 2 * lines, at + 3 * lines, sent_ref[:, at + 2 * lines : at + 3 * lines]),
        ):
            inner_out[:, start:stop] = jnp.where(even, sent[0:4], sent[4:8])
            outer_out[:, start:stop] = jnp.where(even, sent[4:8], sent[0:4])


def curl_kernel(places, part_ref, cross_ref, low_ref, high_ref, moved_ref, tables_ref, out_ref, next_ref, pad, sem):
    problems, _, nx, ny, n = part_ref.shape
    half = ny // 2
    mine = pl.ds(pl.multiple_of(lax.axis_index("sec") * half, half), half)
    copy = pltpu.make_async_copy(moved_ref.at[:, :, mine], next_ref, sem)
    copy.start()
    tables = Tables(tables_ref, places)
    high, low = tables.pair("test_first")
    for p in range(problems):
        for c in range(2):
            total = three(cross_ref[p, c].reshape(-1, n), high, low)
            out_ref[p, c] = part_ref[p, c] + total.reshape(nx, ny, n)
        for i in range(nx):
            wrap(pad, 0, cross_ref[p, 1, i])
            wrap(pad, 1, cross_ref[p, 2, i])
            value = [out_ref[p, 0, i], out_ref[p, 1, i], part_ref[p, 2, i]]
            for k, first, second in zip((1, 2, 3), FIRST, SECOND):
                w = STEP * first
                value[0] = value[0] + w * (pad[1, 8 + k : 8 + k + ny] - pad[1, 8 - k : 8 - k + ny])
                value[2] = value[2] - w * (pad[0, 8 + k : 8 + k + ny] - pad[0, 8 - k : 8 - k + ny])
                for j, sign in ((i + k, w), (i - k, -w)):
                    if 0 <= j < nx:
                        value[1] = value[1] - sign * cross_ref[p, 2, j]
                        value[2] = value[2] - sign * cross_ref[p, 0, j]
                    else:
                        face, h = (low_ref, j + 3) if j < 0 else (high_ref, j - nx)
                        for c in range(3):
                            value[c] = value[c] + (STEP * DIFF * second) * face[p, c, h]
            for c in range(3):
                out_ref[p, c, i] = value[c]
    copy.wait()


def finish_kernel(
    places, part_ref, inner_in, outer_in, t_low, t_high, c_low, c_high, tables_ref,
    out_ref, held, cross, sems,
):
    problems, _, nx, ny, n = part_ref.shape
    tables = Tables(tables_ref, places)
    land = tables.get("land").astype(BF16)
    raw = taken_in(inner_in, outer_in)
    lines = nx * ny
    copies = []

    def landed(p, c):
        at = (3 * p + c) * lines
        held[p, c] = part_ref[p, c] + lines_in(raw[:, at : at + lines], land).reshape(nx, ny, n)

    def leave(p, c):
        copies.append(pltpu.make_async_copy(held.at[p, c], out_ref.at[p, c], sems.at[3 * p + c]))
        copies[-1].start()

    for p in range(problems):
        landed(p, 1)
        landed(p, 2)
        wave_x, wave_y = wave_parts(tables, p, places["wave"][1] // 2)
        for side, (t_ref, c_ref, sign) in enumerate(((t_low, c_low, -STEP), (t_high, c_high, STEP))):
            for h in range(3):
                cx, cy, cz = c_ref[0, h], c_ref[1, h], c_ref[2, h]
                tx, ty, tz = t_ref[p, 0, h] + wave_x, t_ref[p, 1, h] + wave_y, t_ref[p, 2, h]
                cross[0, h] = cz * tx - cx * tz
                cross[1, h] = cx * ty - cy * tx
            for m in range(3):
                i = m if side == 0 else nx - 1 - m
                second, third = held[p, 1, i], held[p, 2, i]
                for d in range(m + 1, 4):
                    h = 3 + m - d if side == 0 else d - 1 - m
                    second = second - (sign * FIRST[d - 1]) * cross[1, h]
                    third = third + (sign * FIRST[d - 1]) * cross[0, h]
                held[p, 1, i] = second
                held[p, 2, i] = third
        leave(p, 1)
        leave(p, 2)
    for p in range(problems):
        landed(p, 0)
        leave(p, 0)
    for copy in copies:
        copy.wait()


def shifted(block, axis, distance):
    count = lax.axis_size(axis)
    return lax.ppermute(block, axis, [(i, (i + distance) % count) for i in range(count)])


def swapped(block, axis, first):
    count = lax.axis_size(axis)
    pairs = [(i % count, (i + 1) % count) for i in range(first, count + first, 2)]
    return lax.ppermute(block, axis, pairs + [(b, a) for a, b in pairs])


def shards(velocity, tests):
    _, nx, half, n = velocity.shape
    problems, _, _, ny, _ = tests.shape
    lines = nx * ny
    constants, places = make_tables(n, nx * lax.axis_size("gx"), ny, n * lax.axis_size("gz"))
    vmem = pl.BlockSpec(memory_space=pltpu.VMEM)

    def shape(*dims):
        return jax.ShapeDtypeStruct(dims, F32)

    def run(kernel, name, args, outs, scratch=(), flops=10**8, out_specs=None, bind=True):
        body = kernel if not bind else (lambda *refs: kernel(places, *refs))
        moved = 4 * sum(math.prod(a.shape) for a in (*args, *outs))
        return pl.pallas_call(
            body,
            in_specs=[vmem] * len(args),
            out_specs=[vmem] * len(outs) if out_specs is None else out_specs,
            out_shape=list(outs),
            scratch_shapes=list(scratch),
            compiler_params=pltpu.CompilerParams(vmem_limit_bytes=VMEM_LIMIT),
            cost_estimate=pl.CostEstimate(flops=flops, bytes_accessed=moved, transcendentals=0),
            name=name,
        )(*args)

    whole_shape = (3, nx, ny, n)
    tests_shape = (problems, 3, nx, ny, n)
    other = shifted(velocity, "sec", 1)
    (tables,) = run(tables_kernel, "tables", [jnp.asarray(constants)], [shape(*constants.shape)], bind=False)
    v_low, v_high = run(faces_kernel, "flow_faces", [velocity], [shape(3, 3, half, n)] * 2, bind=False)
    v_own = [shifted(v_high, "gx", 1), shifted(v_low, "gx", -1)]
    t_low, t_high = run(faces_kernel, "test_faces", [tests], [shape(problems, 3, 3, ny, n)] * 2, bind=False)
    t_faces = [shifted(t_high, "gx", 1), shifted(t_low, "gx", -1)]
    (packed,) = run(pack_kernel, "pack", v_own, [shape(2, 3, 3, half, n)], bind=False)
    v_other = shifted(packed, "sec", 1)
    whole, inner, outer = run(
        whole_kernel, "whole", [velocity, other, tables],
        [shape(*whole_shape)] + [shape(4, 3 * lines)] * 2,
    )
    outer = swapped(outer, "gz", 1)
    inner = swapped(inner, "gz", 0)
    acc, part, sent = run(
        local_kernel, "local", [whole, tests, tables],
        [shape(*whole_shape), shape(*tests_shape), shape(8, problems * 3 * lines)],
        [pltpu.VMEM((3, ny + 16, n), F32), pltpu.VMEM(whole_shape, F32), pltpu.VMEM(whole_shape, F32)],
        flops=4 * 10**9,
    )
    moved, cross, low, high = run(
        step_kernel, "step", [whole, acc, *v_own, v_other, inner, outer, tests, tables],
        [shape(*whole_shape), shape(*tests_shape)] + [shape(3, 3, ny, n)] * 2,
        [pltpu.VMEM(whole_shape, F32)] * 2 + [pltpu.VMEM((3, 3, ny, n), F32)] * 2, flops=10**9,
    )
    from_low = shifted(high, "gx", 1)
    from_high = shifted(low, "gx", -1)
    inner, outer = run(
        sums_kernel, "sums", [cross, sent, tables], [shape(4, problems * 3 * lines)] * 2,
    )
    outer = swapped(outer, "gz", 1)
    inner = swapped(inner, "gz", 0)
    part, velocity_next = run(
        curl_kernel, "curl", [part, cross, *t_faces, moved, tables], [shape(*tests_shape), shape(3, nx, half, n)],
        [pltpu.VMEM((2, ny + 16, n), F32), pltpu.SemaphoreType.DMA], flops=10**9,
        out_specs=[vmem, pl.BlockSpec(memory_space=pl.ANY)],
    )
    (test_next,) = run(
        finish_kernel, "finish",
        [part, inner, outer, *t_faces, from_low, from_high, tables],
        [shape(*tests_shape)],
        [
            pltpu.VMEM(tests_shape, F32), pltpu.VMEM((2, 3, ny, n), F32),
            pltpu.SemaphoreType.DMA((3 * problems,)),
        ],
        out_specs=[pl.BlockSpec(memory_space=pl.ANY)],
    )
    return velocity_next, test_next


def solution(mesh):
    placed = (P(None, "gx", "sec", "gz"), P("sec", None, "gx", None, "gz"))
    return jax.shard_map(shards, mesh=mesh, in_specs=placed, out_specs=placed, check_vma=False)
```

```python
import math

import jax
import jax.numpy as jnp
import numpy as np
from jax import lax
from jax.experimental import pallas as pl
from jax.experimental.pallas import tpu as pltpu
from jax.sharding import PartitionSpec as P

STEP = 0.2
VISC = 0.1
DIFF = 0.1
FIRST = (45.0 / 60.0, -9.0 / 60.0, 1.0 / 60.0)
SECOND = (270.0 / 180.0, -27.0 / 180.0, 2.0 / 180.0)
MID = -490.0 / 180.0
ROOT = math.sqrt(5.0 / 9.0)
DECAY = -(1.0 - ROOT) / (2.0 / 3.0)
VMEM_LIMIT = 12 * 1024 * 1024
FACES_LIMIT = int(52.0 * 1024 * 1024)
F32 = jnp.float32
BF16 = jnp.bfloat16


def compact_weight(distance):
    d = np.asarray(distance)

    def green(k):
        return DECAY ** np.abs(k) / ROOT

    return 7.0 / 9.0 * (green(d + 1) - green(d - 1)) + 1.0 / 36.0 * (green(d + 2) - green(d - 2))


def second_weight(distance):
    table = np.array([MID, *SECOND, 0.0])
    return table[np.minimum(np.abs(distance), 4)]


TAIL = float(compact_weight(2)) / DECAY**2
CORNER = float(compact_weight(1)) - TAIL * DECAY


def halves(table):
    table = np.asarray(table, np.float32)
    high = np.asarray(np.asarray(table, jnp.bfloat16), np.float32)
    low = np.asarray(np.asarray(table - high, jnp.bfloat16), np.float32)
    return high, low


def make_tables(n, x_total, y_total, z_total):
    j = np.arange(n)
    gap = j[None, :] - j[:, None]
    inner_first = compact_weight(gap)
    inner_second = second_weight(gap)
    pick = np.zeros((8, n))
    for k in range(3):
        pick[k, n - 1 - k] = 1.0
        pick[4 + k, k] = 1.0
    pick[3] = DECAY ** (n - 1 - j)
    pick[7] = DECAY**j
    spread_first = np.zeros((8, n))
    spread_second = np.zeros((8, n))
    for k in range(3):
        for z in range(3 - k):
            spread_second[k, z] = SECOND[z + k]
            spread_second[4 + k, n - 1 - z] = SECOND[z + k]
    spread_first[0, 0] = CORNER
    spread_first[4, n - 1] = -CORNER
    spread_first[3] = TAIL * DECAY ** (j + 1)
    spread_first[7] = -TAIL * DECAY ** (n - j)
    lay_test = np.zeros((8, n))
    lay_cross = np.zeros((8, n))
    for z in range(3):
        for k in range(3 - z):
            lay_test[z, n - 1 - k] = STEP * DIFF * SECOND[z + k]
            lay_test[4 + z, k] = STEP * DIFF * SECOND[z + k]
    lay_cross[0, n - 1] = STEP * CORNER
    lay_cross[4, 0] = -STEP * CORNER
    lay_cross[3] = STEP * DECAY ** (n - 1 - j)
    lay_cross[7] = STEP * DECAY**j
    land = np.zeros((8, n))
    for z in range(3):
        land[z, z] = 1.0
        land[4 + z, n - 1 - z] = 1.0
    land[3] = spread_first[3]
    land[7] = spread_first[7]

    def stacked(table):
        high, low = halves(table)
        return np.concatenate([high, high, low, np.zeros_like(high)])

    def wide(column):
        return np.broadcast_to(np.asarray(column)[:, None], (len(column), n))

    phase_x = 2.0 * math.pi / x_total * np.arange(x_total)
    phase_y = 2.0 * math.pi / y_total * np.arange(y_total)
    angle = 2.0 * math.pi / z_total * np.arange(z_total)
    parts = {
        "pick": np.concatenate(halves(pick)),
        "lay_test": np.concatenate(halves(lay_test)),
        "lay_cross": np.concatenate(halves(lay_cross)),
        "spread_first": stacked(spread_first),
        "spread_second": stacked(spread_second),
        "land": stacked(land),
        "flow_first": np.concatenate(halves(inner_first)),
        "flow_second": np.concatenate(halves(inner_second)),
        "test_first": np.concatenate(halves(STEP * inner_first)),
        "test_second": np.concatenate(halves(STEP * DIFF * inner_second)),
        "sin_x": wide(np.sin(phase_x)),
        "cos_x": wide(np.cos(phase_x)),
        "sin_y": wide(np.sin(phase_y)),
        "cos_y": wide(np.cos(phase_y)),
        "wave": np.concatenate([np.cos(angle), np.sin(angle)]).reshape(-1, n),
    }
    places, rows = {}, 0
    for name, part in parts.items():
        places[name] = (rows, len(part))
        rows += len(part)
    return np.concatenate(list(parts.values())).astype(np.float32), places


def split(values):
    high = values.astype(BF16)
    low = (values - high.astype(F32)).astype(BF16)
    return high, low


def dot(a, b):
    return jnp.dot(a, b, preferred_element_type=F32)


def three(values, high, low):
    a, b = split(values)
    return dot(a, high) + dot(b, high) + dot(a, low)


def lines_out(values, both):
    a, b = split(values)
    nt = (((1,), (1,)), ((), ()))
    main = lax.dot_general(both, a, nt, preferred_element_type=F32)
    rest = lax.dot_general(both, b, nt, preferred_element_type=F32)
    return main[0:8] + main[8:16] + rest[0:8]


def lines_in(raw, tables):
    high = raw.astype(BF16).astype(F32)
    low = raw - high
    packed = jnp.concatenate([high, low, high, jnp.zeros_like(high)], 0).astype(BF16)
    return lax.dot_general(packed, tables, (((0,), (0,)), ((), ())), preferred_element_type=F32)


class Tables:
    def __init__(self, ref, places):
        self.ref = ref
        self.places = places

    def get(self, name):
        start, rows = self.places[name]
        return self.ref[start : start + rows]

    def pair(self, name):
        start, rows = self.places[name]
        half = rows // 2
        return self.ref[start : start + half].astype(BF16), self.ref[start + half : start + rows].astype(BF16)

    def row(self, name, index):
        return self.ref[pl.ds(self.places[name][0] + index, 1)]


def in_chip():
    return lax.rem(lax.axis_index("gz"), 2) == 0


def hand_out(sent, inner_ref, outer_ref):
    even = in_chip()
    inner_ref[...] = jnp.where(even, sent[0:4], sent[4:8])
    outer_ref[...] = jnp.where(even, sent[4:8], sent[0:4])


def taken_in(inner_ref, outer_ref):
    even = in_chip()
    left = jnp.where(even, outer_ref[...], inner_ref[...])
    right = jnp.where(even, inner_ref[...], outer_ref[...])
    return jnp.concatenate([left, right], 0)


def wave_parts(tables, problem, slabs):
    wave = tables.row("wave", problem * slabs + lax.axis_index("gz"))
    first = lax.axis_index("sec") == 0
    return jnp.where(first, wave, 0.0), jnp.where(first, 0.0, wave)


def wrap(pad, k, values):
    ny = values.shape[0]
    pad[k, 0:8] = values[ny - 8 : ny]
    pad[k, 8 : 8 + ny] = values
    pad[k, 8 + ny : 16 + ny] = values[0:8]


def tables_kernel(source, out):
    out[...] = source[...]


def faces_kernel(ref, low_ref, high_ref):
    nx = ref.shape[-3]
    low_ref[...] = ref[..., 0:3, :, :]
    high_ref[...] = ref[..., nx - 3 : nx, :, :]


def test_faces_kernel(tests_ref, low_ref, high_ref, sems):
    nx = tests_ref.shape[2]
    copies = [
        pltpu.make_async_copy(tests_ref.at[:, :, pl.ds(start, 3)], out, sems.at[k])
        for k, (start, out) in enumerate(((0, low_ref), (nx - 3, high_ref)))
    ]
    for copy in copies:
        copy.start()
    for copy in copies:
        copy.wait()


def pack_kernel(first, second, out):
    out[0] = first[...]
    out[1] = second[...]


def spread_kernel(places, tests_ref, tables_ref, out_ref, sent_ref, pad):
    problems, _, nx, ny, n = tests_ref.shape
    tables = Tables(tables_ref, places)
    high, low = tables.pair("test_second")
    lay = tables.get("lay_test").astype(BF16)
    lines = nx * ny
    for p in range(problems):
        for c in range(3):
            flat = tests_ref[p, c].reshape(lines, n)
            out_ref[p, c] = three(flat, high, low).reshape(nx, ny, n)
            at = (3 * p + c) * lines
            sent_ref[:, at : at + lines] = lines_out(flat, lay)
        for i in range(nx):
            for c in range(3):
                wrap(pad, c, tests_ref[p, c, i])
            for c in range(3):
                value = out_ref[p, c, i] + (1.0 + STEP * DIFF * 2.0 * MID) * tests_ref[p, c, i]
                for k, w in zip((1, 2, 3), SECOND):
                    near = pad[c, 8 + k : 8 + k + ny] + pad[c, 8 - k : 8 - k + ny]
                    for j in (i + k, i - k):
                        if 0 <= j < nx:
                            near = near + tests_ref[p, c, j]
                    value = value + (STEP * DIFF * w) * near
                out_ref[p, c, i] = value


def whole_kernel(places, own_ref, other_ref, tables_ref, whole_ref, inner_ref, outer_ref):
    _, nx, half, n = own_ref.shape
    section = lax.axis_index("sec")
    whole_ref[:, :, pl.ds(pl.multiple_of(section * half, half), half)] = own_ref[...]
    whole_ref[:, :, pl.ds(pl.multiple_of((1 - section) * half, half), half)] = other_ref[...]
    pick = Tables(tables_ref, places).get("pick").astype(BF16)
    hand_out(lines_out(whole_ref[...].reshape(-1, n), pick), inner_ref, outer_ref)


def flow_kernel(places, whole_ref, tables_ref, acc_ref, pad, grad_z, lap_z):
    _, nx, ny, n = whole_ref.shape
    tables = Tables(tables_ref, places)
    flat = whole_ref[...].reshape(-1, n)
    grad_z[...] = three(flat, *tables.pair("flow_first")).reshape(grad_z.shape)
    lap_z[...] = three(flat, *tables.pair("flow_second")).reshape(lap_z.shape)
    sin_y, cos_y = tables.get("sin_y"), tables.get("cos_y")
    column = lax.axis_index("gx") * nx
    for i in range(nx):
        sin_x, cos_x = tables.row("sin_x", column + i), tables.row("cos_x", column + i)
        drive = (sin_x * cos_y, -(cos_x * sin_y), math.sqrt(2.0) * (sin_x * sin_y))
        for c in range(3):
            wrap(pad, c, whole_ref[c, i])
        own = [whole_ref[c, i] for c in range(3)]
        for c in range(3):
            grad_x = grad_y = None
            lap = lap_z[c, i] + (2.0 * MID) * own[c]
            for k, first, second in zip((1, 2, 3), FIRST, SECOND):
                up, down = pad[c, 8 + k : 8 + k + ny], pad[c, 8 - k : 8 - k + ny]
                term = first * (up - down)
                grad_y = term if grad_y is None else grad_y + term
                near = up + down
                for j, sign in ((i + k, first), (i - k, -first)):
                    if 0 <= j < nx:
                        value = whole_ref[c, j]
                        near = near + value
                        grad_x = sign * value if grad_x is None else grad_x + sign * value
                lap = lap + second * near
            advect = own[0] * grad_x + own[1] * grad_y + own[2] * grad_z[c, i]
            acc_ref[c, i] = own[c] + STEP * (VISC * lap - advect + drive[c])


def local_kernel(places, whole_ref, tests_ref, tables_ref, acc_ref, part_ref, sent_ref, pad, grad_z, lap_z):
    flow_kernel(places, whole_ref, tables_ref, acc_ref, pad, grad_z, lap_z)
    spread_kernel(places, tests_ref, tables_ref, part_ref, sent_ref, pad)


def step_kernel(
    places, whole_ref, acc_ref, low_own, high_own, other_faces, inner_in, outer_in, tests_ref,
    tables_ref, moved_ref, cross_ref, low_out, high_out, grad_z, lap_z, low_ref, high_ref,
):
    _, nx, ny, n = whole_ref.shape
    half = ny // 2
    problems = tests_ref.shape[0]
    section = lax.axis_index("sec")
    mine = pl.ds(pl.multiple_of(section * half, half), half)
    theirs = pl.ds(pl.multiple_of((1 - section) * half, half), half)
    for side, (face, faces_own) in enumerate(((low_ref, low_own), (high_ref, high_own))):
        face[:, :, mine] = faces_own[...]
        face[:, :, theirs] = other_faces[side]
    tables = Tables(tables_ref, places)
    raw = taken_in(inner_in, outer_in)
    grad_z[...] = lines_in(raw, tables.get("spread_first").astype(BF16)).reshape(grad_z.shape)
    lap_z[...] = lines_in(raw, tables.get("spread_second").astype(BF16)).reshape(lap_z.shape)
    waves = [wave_parts(tables, p, places["wave"][1] // 2) for p in range(problems)]
    for i in range(nx):
        own = [whole_ref[c, i] for c in range(3)]
        centred = []
        for c in range(3):
            lap, grad_x = lap_z[c, i], None
            for k, first, second in zip((1, 2, 3), FIRST, SECOND):
                for j, sign in ((i + k, first), (i - k, -first)):
                    if not 0 <= j < nx:
                        value = low_ref[c, j + 3] if j < 0 else high_ref[c, j - nx]
                        lap = lap + second * value
                        grad_x = sign * value if grad_x is None else grad_x + sign * value
            advect = own[2] * grad_z[c, i]
            if grad_x is not None:
                advect = advect + own[0] * grad_x
            moved = acc_ref[c, i] + STEP * (VISC * lap - advect)
            moved_ref[c, i] = moved
            centred.append(0.5 * (own[c] + moved))
            if i < 3:
                low_out[c, i] = centred[c]
            if i >= nx - 3:
                high_out[c, i - nx + 3] = centred[c]
        cx, cy, cz = centred
        for p in range(problems):
            tx, ty, tz = tests_ref[p, 0, i] + waves[p][0], tests_ref[p, 1, i] + waves[p][1], tests_ref[p, 2, i]
            cross_ref[p, 0, i] = cx * tz - cz * tx
            cross_ref[p, 1, i] = cy * tz - cz * ty
            cross_ref[p, 2, i] = cx * ty - cy * tx


def sums_kernel(places, cross_ref, sent_ref, tables_ref, inner_out, outer_out):
    problems, _, nx, ny, n = cross_ref.shape
    tables = Tables(tables_ref, places)
    lay = tables.get("lay_cross").astype(BF16)
    lines = nx * ny
    even = in_chip()
    for p in range(problems):
        at = 3 * p * lines
        added = lines_out(cross_ref[p, 0:2].reshape(-1, n), lay)
        for start, stop, sent in (
            (at, at + 2 * lines, sent_ref[:, at : at + 2 * lines] + added),
            (at + 2 * lines, at + 3 * lines, sent_ref[:, at + 2 * lines : at + 3 * lines]),
        ):
            inner_out[:, start:stop] = jnp.where(even, sent[0:4], sent[4:8])
            outer_out[:, start:stop] = jnp.where(even, sent[4:8], sent[0:4])


def curl_kernel(places, part_ref, cross_ref, low_ref, high_ref, moved_ref, tables_ref, out_ref, next_ref, pad, sem):
    problems, _, nx, ny, n = part_ref.shape
    half = ny // 2
    mine = pl.ds(pl.multiple_of(lax.axis_index("sec") * half, half), half)
    copy = pltpu.make_async_copy(moved_ref.at[:, :, mine], next_ref, sem)
    copy.start()
    tables = Tables(tables_ref, places)
    high, low = tables.pair("test_first")
    for p in range(problems):
        for c in range(2):
            total = three(cross_ref[p, c].reshape(-1, n), high, low)
            out_ref[p, c] = part_ref[p, c] + total.reshape(nx, ny, n)
        for i in range(nx):
            wrap(pad, 0, cross_ref[p, 1, i])
            wrap(pad, 1, cross_ref[p, 2, i])
            value = [out_ref[p, 0, i], out_ref[p, 1, i], part_ref[p, 2, i]]
            for k, first, second in zip((1, 2, 3), FIRST, SECOND):
                w = STEP * first
                value[0] = value[0] + w * (pad[1, 8 + k : 8 + k + ny] - pad[1, 8 - k : 8 - k + ny])
                value[2] = value[2] - w * (pad[0, 8 + k : 8 + k + ny] - pad[0, 8 - k : 8 - k + ny])
                for j, sign in ((i + k, w), (i - k, -w)):
                    if 0 <= j < nx:
                        value[1] = value[1] - sign * cross_ref[p, 2, j]
                        value[2] = value[2] - sign * cross_ref[p, 0, j]
                    else:
                        face, h = (low_ref, j + 3) if j < 0 else (high_ref, j - nx)
                        for c in range(3):
                            value[c] = value[c] + (STEP * DIFF * second) * face[p, c, h]
            for c in range(3):
                out_ref[p, c, i] = value[c]
    copy.wait()


def finish_kernel(
    places, part_ref, inner_in, outer_in, t_low, t_high, c_low, c_high, tables_ref,
    out_ref, held, cross, sems,
):
    problems, _, nx, ny, n = part_ref.shape
    tables = Tables(tables_ref, places)
    land = tables.get("land").astype(BF16)
    raw = taken_in(inner_in, outer_in)
    lines = nx * ny
    copies = []

    def landed(p, c):
        at = (3 * p + c) * lines
        held[p, c] = part_ref[p, c] + lines_in(raw[:, at : at + lines], land).reshape(nx, ny, n)

    def leave(p, c):
        copies.append(pltpu.make_async_copy(held.at[p, c], out_ref.at[p, c], sems.at[3 * p + c]))
        copies[-1].start()

    for p in range(problems):
        landed(p, 1)
        landed(p, 2)
        wave_x, wave_y = wave_parts(tables, p, places["wave"][1] // 2)
        for side, (t_ref, c_ref, sign) in enumerate(((t_low, c_low, -STEP), (t_high, c_high, STEP))):
            for h in range(3):
                cx, cy, cz = c_ref[0, h], c_ref[1, h], c_ref[2, h]
                tx, ty, tz = t_ref[p, 0, h] + wave_x, t_ref[p, 1, h] + wave_y, t_ref[p, 2, h]
                cross[0, h] = cz * tx - cx * tz
                cross[1, h] = cx * ty - cy * tx
            for m in range(3):
                i = m if side == 0 else nx - 1 - m
                second, third = held[p, 1, i], held[p, 2, i]
                for d in range(m + 1, 4):
                    h = 3 + m - d if side == 0 else d - 1 - m
                    second = second - (sign * FIRST[d - 1]) * cross[1, h]
                    third = third + (sign * FIRST[d - 1]) * cross[0, h]
                held[p, 1, i] = second
                held[p, 2, i] = third
        leave(p, 1)
        leave(p, 2)
    for p in range(problems):
        landed(p, 0)
        leave(p, 0)
    for copy in copies:
        copy.wait()


def shifted(block, axis, distance):
    count = lax.axis_size(axis)
    return lax.ppermute(block, axis, [(i, (i + distance) % count) for i in range(count)])


def swapped(block, axis, first):
    count = lax.axis_size(axis)
    pairs = [(i % count, (i + 1) % count) for i in range(first, count + first, 2)]
    return lax.ppermute(block, axis, pairs + [(b, a) for a, b in pairs])


def shards(velocity, tests):
    _, nx, half, n = velocity.shape
    problems, _, _, ny, _ = tests.shape
    lines = nx * ny
    constants, places = make_tables(n, nx * lax.axis_size("gx"), ny, n * lax.axis_size("gz"))
    vmem = pl.BlockSpec(memory_space=pltpu.VMEM)

    def shape(*dims):
        return jax.ShapeDtypeStruct(dims, F32)

    def run(kernel, name, args, outs, scratch=(), flops=10**8, out_specs=None, bind=True, in_space=pltpu.VMEM, limit=VMEM_LIMIT):
        body = kernel if not bind else (lambda *refs: kernel(places, *refs))
        moved = 4 * sum(math.prod(a.shape) for a in (*args, *outs))
        return pl.pallas_call(
            body,
            in_specs=[pl.BlockSpec(memory_space=in_space)] * len(args),
            out_specs=[vmem] * len(outs) if out_specs is None else out_specs,
            out_shape=list(outs),
            scratch_shapes=list(scratch),
            compiler_params=pltpu.CompilerParams(vmem_limit_bytes=limit),
            cost_estimate=pl.CostEstimate(flops=flops, bytes_accessed=moved, transcendentals=0),
            name=name,
        )(*args)

    whole_shape = (3, nx, ny, n)
    tests_shape = (problems, 3, nx, ny, n)
    other = shifted(velocity, "sec", 1)
    (tables,) = run(tables_kernel, "tables", [jnp.asarray(constants)], [shape(*constants.shape)], bind=False)
    v_low, v_high = run(faces_kernel, "flow_faces", [velocity], [shape(3, 3, half, n)] * 2, bind=False)
    v_own = [shifted(v_high, "gx", 1), shifted(v_low, "gx", -1)]
    t_low, t_high = run(
        test_faces_kernel, "test_faces", [tests], [shape(problems, 3, 3, ny, n)] * 2,
        [pltpu.SemaphoreType.DMA((2,))], bind=False, in_space=pl.ANY, limit=FACES_LIMIT,
    )
    t_faces = [shifted(t_high, "gx", 1), shifted(t_low, "gx", -1)]
    (packed,) = run(pack_kernel, "pack", v_own, [shape(2, 3, 3, half, n)], bind=False)
    v_other = shifted(packed, "sec", 1)
    whole, inner, outer = run(
        whole_kernel, "whole", [velocity, other, tables],
        [shape(*whole_shape)] + [shape(4, 3 * lines)] * 2,
    )
    outer = swapped(outer, "gz", 1)
    inner = swapped(inner, "gz", 0)
    acc, part, sent = run(
        local_kernel, "local", [whole, tests, tables],
        [shape(*whole_shape), shape(*tests_shape), shape(8, problems * 3 * lines)],
        [pltpu.VMEM((3, ny + 16, n), F32), pltpu.VMEM(whole_shape, F32), pltpu.VMEM(whole_shape, F32)],
        flops=4 * 10**9,
    )
    moved, cross, low, high = run(
        step_kernel, "step", [whole, acc, *v_own, v_other, inner, outer, tests, tables],
        [shape(*whole_shape), shape(*tests_shape)] + [shape(3, 3, ny, n)] * 2,
        [pltpu.VMEM(whole_shape, F32)] * 2 + [pltpu.VMEM((3, 3, ny, n), F32)] * 2, flops=10**9,
    )
    from_low = shifted(high, "gx", 1)
    from_high = shifted(low, "gx", -1)
    inner, outer = run(
        sums_kernel, "sums", [cross, sent, tables], [shape(4, problems * 3 * lines)] * 2,
    )
    outer = swapped(outer, "gz", 1)
    inner = swapped(inner, "gz", 0)
    part, velocity_next = run(
        curl_kernel, "curl", [part, cross, *t_faces, moved, tables], [shape(*tests_shape), shape(3, nx, half, n)],
        [pltpu.VMEM((2, ny + 16, n), F32), pltpu.SemaphoreType.DMA], flops=10**9,
        out_specs=[vmem, pl.BlockSpec(memory_space=pl.ANY)],
    )
    (test_next,) = run(
        finish_kernel, "finish",
        [part, inner, outer, *t_faces, from_low, from_high, tables],
        [shape(*tests_shape)],
        [
            pltpu.VMEM(tests_shape, F32), pltpu.VMEM((2, 3, ny, n), F32),
            pltpu.SemaphoreType.DMA((3 * problems,)),
        ],
        out_specs=[pl.BlockSpec(memory_space=pl.ANY)],
    )
    return velocity_next, test_next


def solution(mesh):
    placed = (P(None, "gx", "sec", "gz"), P("sec", None, "gx", None, "gz"))
    return jax.shard_map(shards, mesh=mesh, in_specs=placed, out_specs=placed, check_vma=False)
```

```python
import math

import jax
import jax.numpy as jnp
import numpy as np
from jax import lax
from jax.experimental import pallas as pl
from jax.experimental.pallas import tpu as pltpu
from jax.sharding import PartitionSpec as P

STEP = 0.2
VISC = 0.1
DIFF = 0.1
FIRST = (45.0 / 60.0, -9.0 / 60.0, 1.0 / 60.0)
SECOND = (270.0 / 180.0, -27.0 / 180.0, 2.0 / 180.0)
MID = -490.0 / 180.0
ROOT = math.sqrt(5.0 / 9.0)
DECAY = -(1.0 - ROOT) / (2.0 / 3.0)
VMEM_LIMIT = 12 * 1024 * 1024
FACES_LIMIT = int(52.0 * 1024 * 1024)
F32 = jnp.float32
BF16 = jnp.bfloat16


def compact_weight(distance):
    d = np.asarray(distance)

    def green(k):
        return DECAY ** np.abs(k) / ROOT

    return 7.0 / 9.0 * (green(d + 1) - green(d - 1)) + 1.0 / 36.0 * (green(d + 2) - green(d - 2))


def second_weight(distance):
    table = np.array([MID, *SECOND, 0.0])
    return table[np.minimum(np.abs(distance), 4)]


TAIL = float(compact_weight(2)) / DECAY**2
CORNER = float(compact_weight(1)) - TAIL * DECAY


def halves(table):
    table = np.asarray(table, np.float32)
    high = np.asarray(np.asarray(table, jnp.bfloat16), np.float32)
    low = np.asarray(np.asarray(table - high, jnp.bfloat16), np.float32)
    return high, low


def make_tables(n, x_total, y_total, z_total):
    j = np.arange(n)
    gap = j[None, :] - j[:, None]
    inner_first = compact_weight(gap)
    inner_second = second_weight(gap)
    pick = np.zeros((8, n))
    for k in range(3):
        pick[k, n - 1 - k] = 1.0
        pick[4 + k, k] = 1.0
    pick[3] = DECAY ** (n - 1 - j)
    pick[7] = DECAY**j
    spread_first = np.zeros((8, n))
    spread_second = np.zeros((8, n))
    for k in range(3):
        for z in range(3 - k):
            spread_second[k, z] = SECOND[z + k]
            spread_second[4 + k, n - 1 - z] = SECOND[z + k]
    spread_first[0, 0] = CORNER
    spread_first[4, n - 1] = -CORNER
    spread_first[3] = TAIL * DECAY ** (j + 1)
    spread_first[7] = -TAIL * DECAY ** (n - j)
    lay_test = np.zeros((8, n))
    lay_cross = np.zeros((8, n))
    for z in range(3):
        for k in range(3 - z):
            lay_test[z, n - 1 - k] = STEP * DIFF * SECOND[z + k]
            lay_test[4 + z, k] = STEP * DIFF * SECOND[z + k]
    lay_cross[0, n - 1] = STEP * CORNER
    lay_cross[4, 0] = -STEP * CORNER
    lay_cross[3] = STEP * DECAY ** (n - 1 - j)
    lay_cross[7] = STEP * DECAY**j
    land = np.zeros((8, n))
    for z in range(3):
        land[z, z] = 1.0
        land[4 + z, n - 1 - z] = 1.0
    land[3] = spread_first[3]
    land[7] = spread_first[7]

    def stacked(table):
        high, low = halves(table)
        return np.concatenate([high, high, low, np.zeros_like(high)])

    def wide(column):
        return np.broadcast_to(np.asarray(column)[:, None], (len(column), n))

    phase_x = 2.0 * math.pi / x_total * np.arange(x_total)
    phase_y = 2.0 * math.pi / y_total * np.arange(y_total)
    angle = 2.0 * math.pi / z_total * np.arange(z_total)
    parts = {
        "pick": np.concatenate(halves(pick)),
        "lay_test": np.concatenate(halves(lay_test)),
        "lay_cross": np.concatenate(halves(lay_cross)),
        "spread_first": stacked(spread_first),
        "spread_second": stacked(spread_second),
        "land": stacked(land),
        "flow_first": np.concatenate(halves(inner_first)),
        "flow_second": np.concatenate(halves(inner_second)),
        "test_first": np.concatenate(halves(STEP * inner_first)),
        "test_second": np.concatenate(halves(STEP * DIFF * inner_second)),
        "sin_x": wide(np.sin(phase_x)),
        "cos_x": wide(np.cos(phase_x)),
        "sin_y": wide(np.sin(phase_y)),
        "cos_y": wide(np.cos(phase_y)),
        "wave": np.concatenate([np.cos(angle), np.sin(angle)]).reshape(-1, n),
    }
    places, rows = {}, 0
    for name, part in parts.items():
        places[name] = (rows, len(part))
        rows += len(part)
    return np.concatenate(list(parts.values())).astype(np.float32), places


def split(values):
    high = values.astype(BF16)
    low = (values - high.astype(F32)).astype(BF16)
    return high, low


def dot(a, b):
    return jnp.dot(a, b, preferred_element_type=F32)


def three(values, high, low):
    a, b = split(values)
    return dot(a, high) + dot(b, high) + dot(a, low)


def lines_out(values, both):
    a, b = split(values)
    nt = (((1,), (1,)), ((), ()))
    main = lax.dot_general(both, a, nt, preferred_element_type=F32)
    rest = lax.dot_general(both, b, nt, preferred_element_type=F32)
    return main[0:8] + main[8:16] + rest[0:8]


def lines_in(raw, tables):
    high = raw.astype(BF16).astype(F32)
    low = raw - high
    packed = jnp.concatenate([high, low, high, jnp.zeros_like(high)], 0).astype(BF16)
    return lax.dot_general(packed, tables, (((0,), (0,)), ((), ())), preferred_element_type=F32)


class Tables:
    def __init__(self, ref, places):
        self.ref = ref
        self.places = places

    def get(self, name):
        start, rows = self.places[name]
        return self.ref[start : start + rows]

    def pair(self, name):
        start, rows = self.places[name]
        half = rows // 2
        return self.ref[start : start + half].astype(BF16), self.ref[start + half : start + rows].astype(BF16)

    def row(self, name, index):
        return self.ref[pl.ds(self.places[name][0] + index, 1)]


def in_chip():
    return lax.rem(lax.axis_index("gz"), 2) == 0


def hand_out(sent, inner_ref, outer_ref):
    even = in_chip()
    inner_ref[...] = jnp.where(even, sent[0:4], sent[4:8])
    outer_ref[...] = jnp.where(even, sent[4:8], sent[0:4])


def taken_in(inner_ref, outer_ref):
    even = in_chip()
    left = jnp.where(even, outer_ref[...], inner_ref[...])
    right = jnp.where(even, inner_ref[...], outer_ref[...])
    return jnp.concatenate([left, right], 0)


def wave_parts(tables, problem, slabs):
    wave = tables.row("wave", problem * slabs + lax.axis_index("gz"))
    first = lax.axis_index("sec") == 0
    return jnp.where(first, wave, 0.0), jnp.where(first, 0.0, wave)


def wrap(pad, k, values):
    ny = values.shape[0]
    pad[k, 0:8] = values[ny - 8 : ny]
    pad[k, 8 : 8 + ny] = values
    pad[k, 8 + ny : 16 + ny] = values[0:8]


def tables_kernel(source, out):
    out[...] = source[...]


def faces_kernel(ref, low_ref, high_ref):
    nx = ref.shape[-3]
    low_ref[...] = ref[..., 0:3, :, :]
    high_ref[...] = ref[..., nx - 3 : nx, :, :]


def test_faces_kernel(tests_ref, low_ref, high_ref, sems):
    nx = tests_ref.shape[2]
    copies = [
        pltpu.make_async_copy(tests_ref.at[:, :, pl.ds(start, 3)], out, sems.at[k])
        for k, (start, out) in enumerate(((0, low_ref), (nx - 3, high_ref)))
    ]
    for copy in copies:
        copy.start()
    for copy in copies:
        copy.wait()


def pack_kernel(first, second, out):
    out[0] = first[...]
    out[1] = second[...]


def spread_kernel(places, tests_ref, tables_ref, out_ref, sent_ref, pad):
    problems, _, nx, ny, n = tests_ref.shape
    tables = Tables(tables_ref, places)
    high, low = tables.pair("test_second")
    lay = tables.get("lay_test").astype(BF16)
    lines = nx * ny
    for p in range(problems):
        for c in range(3):
            flat = tests_ref[p, c].reshape(lines, n)
            out_ref[p, c] = three(flat, high, low).reshape(nx, ny, n)
            at = (3 * p + c) * lines
            sent_ref[:, at : at + lines] = lines_out(flat, lay)
        for i in range(nx):
            for c in range(3):
                wrap(pad, c, tests_ref[p, c, i])
            for c in range(3):
                value = out_ref[p, c, i] + (1.0 + STEP * DIFF * 2.0 * MID) * tests_ref[p, c, i]
                for k, w in zip((1, 2, 3), SECOND):
                    near = pad[c, 8 + k : 8 + k + ny] + pad[c, 8 - k : 8 - k + ny]
                    for j in (i + k, i - k):
                        if 0 <= j < nx:
                            near = near + tests_ref[p, c, j]
                    value = value + (STEP * DIFF * w) * near
                out_ref[p, c, i] = value


def whole_kernel(places, own_ref, other_ref, tables_ref, whole_ref, inner_ref, outer_ref):
    _, nx, half, n = own_ref.shape
    section = lax.axis_index("sec")
    whole_ref[:, :, pl.ds(pl.multiple_of(section * half, half), half)] = own_ref[...]
    whole_ref[:, :, pl.ds(pl.multiple_of((1 - section) * half, half), half)] = other_ref[...]
    pick = Tables(tables_ref, places).get("pick").astype(BF16)
    hand_out(lines_out(whole_ref[...].reshape(-1, n), pick), inner_ref, outer_ref)


def flow_kernel(places, whole_ref, tables_ref, acc_ref, pad, grad_z, lap_z):
    _, nx, ny, n = whole_ref.shape
    tables = Tables(tables_ref, places)
    flat = whole_ref[...].reshape(-1, n)
    grad_z[...] = three(flat, *tables.pair("flow_first")).reshape(grad_z.shape)
    lap_z[...] = three(flat, *tables.pair("flow_second")).reshape(lap_z.shape)
    sin_y, cos_y = tables.get("sin_y"), tables.get("cos_y")
    column = lax.axis_index("gx") * nx
    for i in range(nx):
        sin_x, cos_x = tables.row("sin_x", column + i), tables.row("cos_x", column + i)
        drive = (sin_x * cos_y, -(cos_x * sin_y), math.sqrt(2.0) * (sin_x * sin_y))
        for c in range(3):
            wrap(pad, c, whole_ref[c, i])
        own = [whole_ref[c, i] for c in range(3)]
        for c in range(3):
            grad_x = grad_y = None
            lap = lap_z[c, i] + (2.0 * MID) * own[c]
            for k, first, second in zip((1, 2, 3), FIRST, SECOND):
                up, down = pad[c, 8 + k : 8 + k + ny], pad[c, 8 - k : 8 - k + ny]
                term = first * (up - down)
                grad_y = term if grad_y is None else grad_y + term
                near = up + down
                for j, sign in ((i + k, first), (i - k, -first)):
                    if 0 <= j < nx:
                        value = whole_ref[c, j]
                        near = near + value
                        grad_x = sign * value if grad_x is None else grad_x + sign * value
                lap = lap + second * near
            advect = own[0] * grad_x + own[1] * grad_y + own[2] * grad_z[c, i]
            acc_ref[c, i] = own[c] + STEP * (VISC * lap - advect + drive[c])


def local_kernel(places, whole_ref, tests_ref, tables_ref, acc_ref, part_ref, sent_ref, pad, grad_z, lap_z):
    flow_kernel(places, whole_ref, tables_ref, acc_ref, pad, grad_z, lap_z)
    spread_kernel(places, tests_ref, tables_ref, part_ref, sent_ref, pad)


def step_kernel(
    places, whole_ref, acc_ref, low_own, high_own, other_faces, inner_in, outer_in, tests_ref,
    tables_ref, moved_ref, cross_ref, low_out, high_out, grad_z, lap_z, low_ref, high_ref,
):
    _, nx, ny, n = whole_ref.shape
    half = ny // 2
    problems = tests_ref.shape[0]
    section = lax.axis_index("sec")
    mine = pl.ds(pl.multiple_of(section * half, half), half)
    theirs = pl.ds(pl.multiple_of((1 - section) * half, half), half)
    for side, (face, faces_own) in enumerate(((low_ref, low_own), (high_ref, high_own))):
        face[:, :, mine] = faces_own[...]
        face[:, :, theirs] = other_faces[side]
    tables = Tables(tables_ref, places)
    raw = taken_in(inner_in, outer_in)
    grad_z[...] = lines_in(raw, tables.get("spread_first").astype(BF16)).reshape(grad_z.shape)
    lap_z[...] = lines_in(raw, tables.get("spread_second").astype(BF16)).reshape(lap_z.shape)
    waves = [wave_parts(tables, p, places["wave"][1] // 2) for p in range(problems)]
    for i in range(nx):
        own = [whole_ref[c, i] for c in range(3)]
        centred = []
        for c in range(3):
            lap, grad_x = lap_z[c, i], None
            for k, first, second in zip((1, 2, 3), FIRST, SECOND):
                for j, sign in ((i + k, first), (i - k, -first)):
                    if not 0 <= j < nx:
                        value = low_ref[c, j + 3] if j < 0 else high_ref[c, j - nx]
                        lap = lap + second * value
                        grad_x = sign * value if grad_x is None else grad_x + sign * value
            advect = own[2] * grad_z[c, i]
            if grad_x is not None:
                advect = advect + own[0] * grad_x
            moved = acc_ref[c, i] + STEP * (VISC * lap - advect)
            moved_ref[c, i] = moved
            centred.append(0.5 * (own[c] + moved))
            if i < 3:
                low_out[c, i] = centred[c]
            if i >= nx - 3:
                high_out[c, i - nx + 3] = centred[c]
        cx, cy, cz = centred
        for p in range(problems):
            tx, ty, tz = tests_ref[p, 0, i] + waves[p][0], tests_ref[p, 1, i] + waves[p][1], tests_ref[p, 2, i]
            cross_ref[p, 0, i] = cx * tz - cz * tx
            cross_ref[p, 1, i] = cy * tz - cz * ty
            cross_ref[p, 2, i] = cx * ty - cy * tx


def sums_kernel(places, cross_ref, sent_ref, tables_ref, inner_out, outer_out):
    problems, _, nx, ny, n = cross_ref.shape
    tables = Tables(tables_ref, places)
    lay = tables.get("lay_cross").astype(BF16)
    lines = nx * ny
    even = in_chip()
    for p in range(problems):
        at = 3 * p * lines
        added = lines_out(cross_ref[p, 0:2].reshape(-1, n), lay)
        for start, stop, sent in (
            (at, at + 2 * lines, sent_ref[:, at : at + 2 * lines] + added),
            (at + 2 * lines, at + 3 * lines, sent_ref[:, at + 2 * lines : at + 3 * lines]),
        ):
            inner_out[:, start:stop] = jnp.where(even, sent[0:4], sent[4:8])
            outer_out[:, start:stop] = jnp.where(even, sent[4:8], sent[0:4])


def curl_kernel(places, part_ref, cross_ref, low_ref, high_ref, moved_ref, tables_ref, out_ref, next_ref, pad, sem):
    problems, _, nx, ny, n = part_ref.shape
    half = ny // 2
    mine = pl.ds(pl.multiple_of(lax.axis_index("sec") * half, half), half)
    copy = pltpu.make_async_copy(moved_ref.at[:, :, mine], next_ref, sem)
    copy.start()
    tables = Tables(tables_ref, places)
    high, low = tables.pair("test_first")
    for p in range(problems):
        for c in range(2):
            total = three(cross_ref[p, c].reshape(-1, n), high, low)
            out_ref[p, c] = part_ref[p, c] + total.reshape(nx, ny, n)
        for i in range(nx):
            wrap(pad, 0, cross_ref[p, 1, i])
            wrap(pad, 1, cross_ref[p, 2, i])
            value = [out_ref[p, 0, i], out_ref[p, 1, i], part_ref[p, 2, i]]
            for k, first, second in zip((1, 2, 3), FIRST, SECOND):
                w = STEP * first
                value[0] = value[0] + w * (pad[1, 8 + k : 8 + k + ny] - pad[1, 8 - k : 8 - k + ny])
                value[2] = value[2] - w * (pad[0, 8 + k : 8 + k + ny] - pad[0, 8 - k : 8 - k + ny])
                for j, sign in ((i + k, w), (i - k, -w)):
                    if 0 <= j < nx:
                        value[1] = value[1] - sign * cross_ref[p, 2, j]
                        value[2] = value[2] - sign * cross_ref[p, 0, j]
                    else:
                        face, h = (low_ref, j + 3) if j < 0 else (high_ref, j - nx)
                        for c in range(3):
                            value[c] = value[c] + (STEP * DIFF * second) * face[p, c, h]
            for c in range(3):
                out_ref[p, c, i] = value[c]
    copy.wait()


def finish_kernel(
    places, part_ref, inner_in, outer_in, t_low, t_high, c_low, c_high, tables_ref,
    out_ref, held, cross, sems,
):
    problems, _, nx, ny, n = part_ref.shape
    tables = Tables(tables_ref, places)
    land = tables.get("land").astype(BF16)
    raw = taken_in(inner_in, outer_in)
    lines = nx * ny
    copies = []

    def landed(p, c):
        at = (3 * p + c) * lines
        held[p, c] = part_ref[p, c] + lines_in(raw[:, at : at + lines], land).reshape(nx, ny, n)

    def leave(*place):
        copies.append(pltpu.make_async_copy(held.at[place], out_ref.at[place], sems.at[len(copies)]))
        copies[-1].start()

    for p in range(problems):
        landed(p, 1)
        landed(p, 2)
        wave_x, wave_y = wave_parts(tables, p, places["wave"][1] // 2)
        for side, (t_ref, c_ref, sign) in enumerate(((t_low, c_low, -STEP), (t_high, c_high, STEP))):
            for h in range(3):
                cx, cy, cz = c_ref[0, h], c_ref[1, h], c_ref[2, h]
                tx, ty, tz = t_ref[p, 0, h] + wave_x, t_ref[p, 1, h] + wave_y, t_ref[p, 2, h]
                cross[0, h] = cz * tx - cx * tz
                cross[1, h] = cx * ty - cy * tx
            for m in range(3):
                i = m if side == 0 else nx - 1 - m
                second, third = held[p, 1, i], held[p, 2, i]
                for d in range(m + 1, 4):
                    h = 3 + m - d if side == 0 else d - 1 - m
                    second = second - (sign * FIRST[d - 1]) * cross[1, h]
                    third = third + (sign * FIRST[d - 1]) * cross[0, h]
                held[p, 1, i] = second
                held[p, 2, i] = third
        leave(p, pl.ds(1, 2))
    for p in range(problems):
        landed(p, 0)
    leave(pl.ds(0, problems), 0)
    for copy in copies:
        copy.wait()


def shifted(block, axis, distance):
    count = lax.axis_size(axis)
    return lax.ppermute(block, axis, [(i, (i + distance) % count) for i in range(count)])


def swapped(block, axis, first):
    count = lax.axis_size(axis)
    pairs = [(i % count, (i + 1) % count) for i in range(first, count + first, 2)]
    return lax.ppermute(block, axis, pairs + [(b, a) for a, b in pairs])


def shards(velocity, tests):
    _, nx, half, n = velocity.shape
    problems, _, _, ny, _ = tests.shape
    lines = nx * ny
    constants, places = make_tables(n, nx * lax.axis_size("gx"), ny, n * lax.axis_size("gz"))
    vmem = pl.BlockSpec(memory_space=pltpu.VMEM)

    def shape(*dims):
        return jax.ShapeDtypeStruct(dims, F32)

    def run(kernel, name, args, outs, scratch=(), flops=10**8, out_specs=None, bind=True, in_space=pltpu.VMEM, limit=VMEM_LIMIT):
        body = kernel if not bind else (lambda *refs: kernel(places, *refs))
        moved = 4 * sum(math.prod(a.shape) for a in (*args, *outs))
        return pl.pallas_call(
            body,
            in_specs=[pl.BlockSpec(memory_space=in_space)] * len(args),
            out_specs=[vmem] * len(outs) if out_specs is None else out_specs,
            out_shape=list(outs),
            scratch_shapes=list(scratch),
            compiler_params=pltpu.CompilerParams(vmem_limit_bytes=limit),
            cost_estimate=pl.CostEstimate(flops=flops, bytes_accessed=moved, transcendentals=0),
            name=name,
        )(*args)

    whole_shape = (3, nx, ny, n)
    tests_shape = (problems, 3, nx, ny, n)
    other = shifted(velocity, "sec", 1)
    (tables,) = run(tables_kernel, "tables", [jnp.asarray(constants)], [shape(*constants.shape)], bind=False)
    v_low, v_high = run(faces_kernel, "flow_faces", [velocity], [shape(3, 3, half, n)] * 2, bind=False)
    v_own = [shifted(v_high, "gx", 1), shifted(v_low, "gx", -1)]
    t_low, t_high = run(
        test_faces_kernel, "test_faces", [tests], [shape(problems, 3, 3, ny, n)] * 2,
        [pltpu.SemaphoreType.DMA((2,))], bind=False, in_space=pl.ANY, limit=FACES_LIMIT,
    )
    t_faces = [shifted(t_high, "gx", 1), shifted(t_low, "gx", -1)]
    (packed,) = run(pack_kernel, "pack", v_own, [shape(2, 3, 3, half, n)], bind=False)
    v_other = shifted(packed, "sec", 1)
    whole, inner, outer = run(
        whole_kernel, "whole", [velocity, other, tables],
        [shape(*whole_shape)] + [shape(4, 3 * lines)] * 2,
    )
    outer = swapped(outer, "gz", 1)
    inner = swapped(inner, "gz", 0)
    acc, part, sent = run(
        local_kernel, "local", [whole, tests, tables],
        [shape(*whole_shape), shape(*tests_shape), shape(8, problems * 3 * lines)],
        [pltpu.VMEM((3, ny + 16, n), F32), pltpu.VMEM(whole_shape, F32), pltpu.VMEM(whole_shape, F32)],
        flops=4 * 10**9,
    )
    moved, cross, low, high = run(
        step_kernel, "step", [whole, acc, *v_own, v_other, inner, outer, tests, tables],
        [shape(*whole_shape), shape(*tests_shape)] + [shape(3, 3, ny, n)] * 2,
        [pltpu.VMEM(whole_shape, F32)] * 2 + [pltpu.VMEM((3, 3, ny, n), F32)] * 2, flops=10**9,
    )
    from_low = shifted(high, "gx", 1)
    from_high = shifted(low, "gx", -1)
    inner, outer = run(
        sums_kernel, "sums", [cross, sent, tables], [shape(4, problems * 3 * lines)] * 2,
    )
    outer = swapped(outer, "gz", 1)
    inner = swapped(inner, "gz", 0)
    part, velocity_next = run(
        curl_kernel, "curl", [part, cross, *t_faces, moved, tables], [shape(*tests_shape), shape(3, nx, half, n)],
        [pltpu.VMEM((2, ny + 16, n), F32), pltpu.SemaphoreType.DMA], flops=10**9,
        out_specs=[vmem, pl.BlockSpec(memory_space=pl.ANY)],
    )
    (test_next,) = run(
        finish_kernel, "finish",
        [part, inner, outer, *t_faces, from_low, from_high, tables],
        [shape(*tests_shape)],
        [
            pltpu.VMEM(tests_shape, F32), pltpu.VMEM((2, 3, ny, n), F32),
            pltpu.SemaphoreType.DMA((3 * problems,)),
        ],
        out_specs=[pl.BlockSpec(memory_space=pl.ANY)],
    )
    return velocity_next, test_next


def solution(mesh):
    placed = (P(None, "gx", "sec", "gz"), P("sec", None, "gx", None, "gz"))
    return jax.shard_map(shards, mesh=mesh, in_specs=placed, out_specs=placed, check_vma=False)
```

```python
import math

import jax
import jax.numpy as jnp
import numpy as np
from jax import lax
from jax.experimental import pallas as pl
from jax.experimental.pallas import tpu as pltpu
from jax.sharding import PartitionSpec as P

STEP = 0.2
VISC = 0.1
DIFF = 0.1
FIRST = (45.0 / 60.0, -9.0 / 60.0, 1.0 / 60.0)
SECOND = (270.0 / 180.0, -27.0 / 180.0, 2.0 / 180.0)
MID = -490.0 / 180.0
ROOT = math.sqrt(5.0 / 9.0)
DECAY = -(1.0 - ROOT) / (2.0 / 3.0)
VMEM_LIMIT = 12 * 1024 * 1024
FACES_LIMIT = int(52.0 * 1024 * 1024)
F32 = jnp.float32
BF16 = jnp.bfloat16


def compact_weight(distance):
    d = np.asarray(distance)

    def green(k):
        return DECAY ** np.abs(k) / ROOT

    return 7.0 / 9.0 * (green(d + 1) - green(d - 1)) + 1.0 / 36.0 * (green(d + 2) - green(d - 2))


def second_weight(distance):
    table = np.array([MID, *SECOND, 0.0])
    return table[np.minimum(np.abs(distance), 4)]


TAIL = float(compact_weight(2)) / DECAY**2
CORNER = float(compact_weight(1)) - TAIL * DECAY


def halves(table):
    table = np.asarray(table, np.float32)
    high = np.asarray(np.asarray(table, jnp.bfloat16), np.float32)
    low = np.asarray(np.asarray(table - high, jnp.bfloat16), np.float32)
    return high, low


def make_tables(n, x_total, y_total, z_total):
    j = np.arange(n)
    gap = j[None, :] - j[:, None]
    inner_first = compact_weight(gap)
    inner_second = second_weight(gap)
    pick = np.zeros((8, n))
    for k in range(3):
        pick[k, n - 1 - k] = 1.0
        pick[4 + k, k] = 1.0
    pick[3] = DECAY ** (n - 1 - j)
    pick[7] = DECAY**j
    spread_first = np.zeros((8, n))
    spread_second = np.zeros((8, n))
    for k in range(3):
        for z in range(3 - k):
            spread_second[k, z] = SECOND[z + k]
            spread_second[4 + k, n - 1 - z] = SECOND[z + k]
    spread_first[0, 0] = CORNER
    spread_first[4, n - 1] = -CORNER
    spread_first[3] = TAIL * DECAY ** (j + 1)
    spread_first[7] = -TAIL * DECAY ** (n - j)
    lay_test = np.zeros((8, n))
    lay_cross = np.zeros((8, n))
    for z in range(3):
        for k in range(3 - z):
            lay_test[z, n - 1 - k] = STEP * DIFF * SECOND[z + k]
            lay_test[4 + z, k] = STEP * DIFF * SECOND[z + k]
    lay_cross[0, n - 1] = STEP * CORNER
    lay_cross[4, 0] = -STEP * CORNER
    lay_cross[3] = STEP * DECAY ** (n - 1 - j)
    lay_cross[7] = STEP * DECAY**j
    land = np.zeros((8, n))
    for z in range(3):
        land[z, z] = 1.0
        land[4 + z, n - 1 - z] = 1.0
    land[3] = spread_first[3]
    land[7] = spread_first[7]

    def stacked(table):
        high, low = halves(table)
        return np.concatenate([high, high, low, np.zeros_like(high)])

    def wide(column):
        return np.broadcast_to(np.asarray(column)[:, None], (len(column), n))

    phase_x = 2.0 * math.pi / x_total * np.arange(x_total)
    phase_y = 2.0 * math.pi / y_total * np.arange(y_total)
    angle = 2.0 * math.pi / z_total * np.arange(z_total)
    parts = {
        "pick": np.concatenate(halves(pick)),
        "lay_test": np.concatenate(halves(lay_test)),
        "lay_cross": np.concatenate(halves(lay_cross)),
        "spread_first": stacked(spread_first),
        "spread_second": stacked(spread_second),
        "land": stacked(land),
        "flow_first": np.concatenate(halves(inner_first)),
        "flow_second": np.concatenate(halves(inner_second)),
        "test_first": np.concatenate(halves(STEP * inner_first)),
        "test_second": np.concatenate(halves(STEP * DIFF * inner_second)),
        "sin_x": wide(np.sin(phase_x)),
        "cos_x": wide(np.cos(phase_x)),
        "sin_y": wide(np.sin(phase_y)),
        "cos_y": wide(np.cos(phase_y)),
        "wave": np.concatenate([np.cos(angle), np.sin(angle)]).reshape(-1, n),
    }
    places, rows = {}, 0
    for name, part in parts.items():
        places[name] = (rows, len(part))
        rows += len(part)
    return np.concatenate(list(parts.values())).astype(np.float32), places


def split(values):
    high = values.astype(BF16)
    low = (values - high.astype(F32)).astype(BF16)
    return high, low


def dot(a, b):
    return jnp.dot(a, b, preferred_element_type=F32)


def three(values, high, low):
    a, b = split(values)
    return dot(a, high) + dot(b, high) + dot(a, low)


def lines_out(values, both):
    a, b = split(values)
    nt = (((1,), (1,)), ((), ()))
    main = lax.dot_general(both, a, nt, preferred_element_type=F32)
    rest = lax.dot_general(both, b, nt, preferred_element_type=F32)
    return main[0:8] + main[8:16] + rest[0:8]


def lines_in(raw, tables):
    high = raw.astype(BF16).astype(F32)
    low = raw - high
    packed = jnp.concatenate([high, low, high, jnp.zeros_like(high)], 0).astype(BF16)
    return lax.dot_general(packed, tables, (((0,), (0,)), ((), ())), preferred_element_type=F32)


class Tables:
    def __init__(self, ref, places):
        self.ref = ref
        self.places = places

    def get(self, name):
        start, rows = self.places[name]
        return self.ref[start : start + rows]

    def pair(self, name):
        start, rows = self.places[name]
        half = rows // 2
        return self.ref[start : start + half].astype(BF16), self.ref[start + half : start + rows].astype(BF16)

    def row(self, name, index):
        return self.ref[pl.ds(self.places[name][0] + index, 1)]


def in_chip():
    return lax.rem(lax.axis_index("gz"), 2) == 0


def hand_out(sent, inner_ref, outer_ref):
    even = in_chip()
    inner_ref[...] = jnp.where(even, sent[0:4], sent[4:8])
    outer_ref[...] = jnp.where(even, sent[4:8], sent[0:4])


def taken_in(inner_ref, outer_ref):
    even = in_chip()
    left = jnp.where(even, outer_ref[...], inner_ref[...])
    right = jnp.where(even, inner_ref[...], outer_ref[...])
    return jnp.concatenate([left, right], 0)


def wave_parts(tables, problem, slabs):
    wave = tables.row("wave", problem * slabs + lax.axis_index("gz"))
    first = lax.axis_index("sec") == 0
    return jnp.where(first, wave, 0.0), jnp.where(first, 0.0, wave)


def wrap(pad, k, values):
    ny = values.shape[0]
    pad[k, 0:8] = values[ny - 8 : ny]
    pad[k, 8 : 8 + ny] = values
    pad[k, 8 + ny : 16 + ny] = values[0:8]


def faces_kernel(ref, low_ref, high_ref):
    nx = ref.shape[-3]
    low_ref[...] = ref[..., 0:3, :, :]
    high_ref[...] = ref[..., nx - 3 : nx, :, :]


def test_faces_kernel(tests_ref, low_ref, high_ref, sems):
    nx = tests_ref.shape[2]
    copies = [
        pltpu.make_async_copy(tests_ref.at[:, :, pl.ds(start, 3)], out, sems.at[k])
        for k, (start, out) in enumerate(((0, low_ref), (nx - 3, high_ref)))
    ]
    for copy in copies:
        copy.start()
    for copy in copies:
        copy.wait()


def pack_kernel(first, second, out):
    out[0] = first[...]
    out[1] = second[...]


def spread_kernel(places, tests_ref, tables_ref, out_ref, sent_ref, pad):
    problems, _, nx, ny, n = tests_ref.shape
    tables = Tables(tables_ref, places)
    high, low = tables.pair("test_second")
    lay = tables.get("lay_test").astype(BF16)
    lines = nx * ny
    for p in range(problems):
        for c in range(3):
            flat = tests_ref[p, c].reshape(lines, n)
            out_ref[p, c] = three(flat, high, low).reshape(nx, ny, n)
            at = (3 * p + c) * lines
            sent_ref[:, at : at + lines] = lines_out(flat, lay)
        for i in range(nx):
            for c in range(3):
                wrap(pad, c, tests_ref[p, c, i])
            for c in range(3):
                value = out_ref[p, c, i] + (1.0 + STEP * DIFF * 2.0 * MID) * tests_ref[p, c, i]
                for k, w in zip((1, 2, 3), SECOND):
                    near = pad[c, 8 + k : 8 + k + ny] + pad[c, 8 - k : 8 - k + ny]
                    for j in (i + k, i - k):
                        if 0 <= j < nx:
                            near = near + tests_ref[p, c, j]
                    value = value + (STEP * DIFF * w) * near
                out_ref[p, c, i] = value


def whole_kernel(places, own_ref, other_ref, tables_ref, whole_ref, inner_ref, outer_ref):
    _, nx, half, n = own_ref.shape
    section = lax.axis_index("sec")
    whole_ref[:, :, pl.ds(pl.multiple_of(section * half, half), half)] = own_ref[...]
    whole_ref[:, :, pl.ds(pl.multiple_of((1 - section) * half, half), half)] = other_ref[...]
    pick = Tables(tables_ref, places).get("pick").astype(BF16)
    hand_out(lines_out(whole_ref[...].reshape(-1, n), pick), inner_ref, outer_ref)


def flow_kernel(places, whole_ref, tables_ref, acc_ref, pad, grad_z, lap_z):
    _, nx, ny, n = whole_ref.shape
    tables = Tables(tables_ref, places)
    flat = whole_ref[...].reshape(-1, n)
    grad_z[...] = three(flat, *tables.pair("flow_first")).reshape(grad_z.shape)
    lap_z[...] = three(flat, *tables.pair("flow_second")).reshape(lap_z.shape)
    sin_y, cos_y = tables.get("sin_y"), tables.get("cos_y")
    column = lax.axis_index("gx") * nx
    for i in range(nx):
        sin_x, cos_x = tables.row("sin_x", column + i), tables.row("cos_x", column + i)
        drive = (sin_x * cos_y, -(cos_x * sin_y), math.sqrt(2.0) * (sin_x * sin_y))
        for c in range(3):
            wrap(pad, c, whole_ref[c, i])
        own = [whole_ref[c, i] for c in range(3)]
        for c in range(3):
            grad_x = grad_y = None
            lap = lap_z[c, i] + (2.0 * MID) * own[c]
            for k, first, second in zip((1, 2, 3), FIRST, SECOND):
                up, down = pad[c, 8 + k : 8 + k + ny], pad[c, 8 - k : 8 - k + ny]
                term = first * (up - down)
                grad_y = term if grad_y is None else grad_y + term
                near = up + down
                for j, sign in ((i + k, first), (i - k, -first)):
                    if 0 <= j < nx:
                        value = whole_ref[c, j]
                        near = near + value
                        grad_x = sign * value if grad_x is None else grad_x + sign * value
                lap = lap + second * near
            advect = own[0] * grad_x + own[1] * grad_y + own[2] * grad_z[c, i]
            acc_ref[c, i] = own[c] + STEP * (VISC * lap - advect + drive[c])


def local_kernel(places, whole_ref, tests_ref, tables_ref, acc_ref, part_ref, sent_ref, pad, grad_z, lap_z):
    flow_kernel(places, whole_ref, tables_ref, acc_ref, pad, grad_z, lap_z)
    spread_kernel(places, tests_ref, tables_ref, part_ref, sent_ref, pad)


def step_kernel(
    places, whole_ref, acc_ref, low_own, high_own, other_faces, inner_in, outer_in, tests_ref,
    tables_ref, moved_ref, cross_ref, low_out, high_out, grad_z, lap_z, low_ref, high_ref,
):
    _, nx, ny, n = whole_ref.shape
    half = ny // 2
    problems = tests_ref.shape[0]
    section = lax.axis_index("sec")
    mine = pl.ds(pl.multiple_of(section * half, half), half)
    theirs = pl.ds(pl.multiple_of((1 - section) * half, half), half)
    for side, (face, faces_own) in enumerate(((low_ref, low_own), (high_ref, high_own))):
        face[:, :, mine] = faces_own[...]
        face[:, :, theirs] = other_faces[side]
    tables = Tables(tables_ref, places)
    raw = taken_in(inner_in, outer_in)
    grad_z[...] = lines_in(raw, tables.get("spread_first").astype(BF16)).reshape(grad_z.shape)
    lap_z[...] = lines_in(raw, tables.get("spread_second").astype(BF16)).reshape(lap_z.shape)
    waves = [wave_parts(tables, p, places["wave"][1] // 2) for p in range(problems)]
    for i in range(nx):
        own = [whole_ref[c, i] for c in range(3)]
        centred = []
        for c in range(3):
            lap, grad_x = lap_z[c, i], None
            for k, first, second in zip((1, 2, 3), FIRST, SECOND):
                for j, sign in ((i + k, first), (i - k, -first)):
                    if not 0 <= j < nx:
                        value = low_ref[c, j + 3] if j < 0 else high_ref[c, j - nx]
                        lap = lap + second * value
                        grad_x = sign * value if grad_x is None else grad_x + sign * value
            advect = own[2] * grad_z[c, i]
            if grad_x is not None:
                advect = advect + own[0] * grad_x
            moved = acc_ref[c, i] + STEP * (VISC * lap - advect)
            moved_ref[c, i] = moved
            centred.append(0.5 * (own[c] + moved))
            if i < 3:
                low_out[c, i] = centred[c]
            if i >= nx - 3:
                high_out[c, i - nx + 3] = centred[c]
        cx, cy, cz = centred
        for p in range(problems):
            tx, ty, tz = tests_ref[p, 0, i] + waves[p][0], tests_ref[p, 1, i] + waves[p][1], tests_ref[p, 2, i]
            cross_ref[p, 0, i] = cx * tz - cz * tx
            cross_ref[p, 1, i] = cy * tz - cz * ty
            cross_ref[p, 2, i] = cx * ty - cy * tx


def sums_kernel(places, cross_ref, sent_ref, tables_ref, inner_out, outer_out):
    problems, _, nx, ny, n = cross_ref.shape
    tables = Tables(tables_ref, places)
    lay = tables.get("lay_cross").astype(BF16)
    lines = nx * ny
    even = in_chip()
    for p in range(problems):
        at = 3 * p * lines
        added = lines_out(cross_ref[p, 0:2].reshape(-1, n), lay)
        for start, stop, sent in (
            (at, at + 2 * lines, sent_ref[:, at : at + 2 * lines] + added),
            (at + 2 * lines, at + 3 * lines, sent_ref[:, at + 2 * lines : at + 3 * lines]),
        ):
            inner_out[:, start:stop] = jnp.where(even, sent[0:4], sent[4:8])
            outer_out[:, start:stop] = jnp.where(even, sent[4:8], sent[0:4])


def curl_kernel(places, part_ref, cross_ref, low_ref, high_ref, moved_ref, tables_ref, out_ref, next_ref, pad, sem):
    problems, _, nx, ny, n = part_ref.shape
    half = ny // 2
    mine = pl.ds(pl.multiple_of(lax.axis_index("sec") * half, half), half)
    copy = pltpu.make_async_copy(moved_ref.at[:, :, mine], next_ref, sem)
    copy.start()
    tables = Tables(tables_ref, places)
    high, low = tables.pair("test_first")
    for p in range(problems):
        for c in range(2):
            total = three(cross_ref[p, c].reshape(-1, n), high, low)
            out_ref[p, c] = part_ref[p, c] + total.reshape(nx, ny, n)
        for i in range(nx):
            wrap(pad, 0, cross_ref[p, 1, i])
            wrap(pad, 1, cross_ref[p, 2, i])
            value = [out_ref[p, 0, i], out_ref[p, 1, i], part_ref[p, 2, i]]
            for k, first, second in zip((1, 2, 3), FIRST, SECOND):
                w = STEP * first
                value[0] = value[0] + w * (pad[1, 8 + k : 8 + k + ny] - pad[1, 8 - k : 8 - k + ny])
                value[2] = value[2] - w * (pad[0, 8 + k : 8 + k + ny] - pad[0, 8 - k : 8 - k + ny])
                for j, sign in ((i + k, w), (i - k, -w)):
                    if 0 <= j < nx:
                        value[1] = value[1] - sign * cross_ref[p, 2, j]
                        value[2] = value[2] - sign * cross_ref[p, 0, j]
                    else:
                        face, h = (low_ref, j + 3) if j < 0 else (high_ref, j - nx)
                        for c in range(3):
                            value[c] = value[c] + (STEP * DIFF * second) * face[p, c, h]
            for c in range(3):
                out_ref[p, c, i] = value[c]
    copy.wait()


def finish_kernel(
    places, part_ref, inner_in, outer_in, t_low, t_high, c_low, c_high, tables_ref,
    out_ref, held, cross, sems,
):
    problems, _, nx, ny, n = part_ref.shape
    tables = Tables(tables_ref, places)
    land = tables.get("land").astype(BF16)
    raw = taken_in(inner_in, outer_in)
    lines = nx * ny
    copies = []

    def landed(p, c):
        at = (3 * p + c) * lines
        held[p, c] = part_ref[p, c] + lines_in(raw[:, at : at + lines], land).reshape(nx, ny, n)

    def leave(p, c):
        copies.append(pltpu.make_async_copy(held.at[p, c], out_ref.at[p, c], sems.at[3 * p + c]))
        copies[-1].start()

    for p in range(problems):
        landed(p, 1)
        landed(p, 2)
        wave_x, wave_y = wave_parts(tables, p, places["wave"][1] // 2)
        for side, (t_ref, c_ref, sign) in enumerate(((t_low, c_low, -STEP), (t_high, c_high, STEP))):
            for h in range(3):
                cx, cy, cz = c_ref[0, h], c_ref[1, h], c_ref[2, h]
                tx, ty, tz = t_ref[p, 0, h] + wave_x, t_ref[p, 1, h] + wave_y, t_ref[p, 2, h]
                cross[0, h] = cz * tx - cx * tz
                cross[1, h] = cx * ty - cy * tx
            for m in range(3):
                i = m if side == 0 else nx - 1 - m
                second, third = held[p, 1, i], held[p, 2, i]
                for d in range(m + 1, 4):
                    h = 3 + m - d if side == 0 else d - 1 - m
                    second = second - (sign * FIRST[d - 1]) * cross[1, h]
                    third = third + (sign * FIRST[d - 1]) * cross[0, h]
                held[p, 1, i] = second
                held[p, 2, i] = third
        leave(p, 1)
        leave(p, 2)
    for p in range(problems):
        landed(p, 0)
        leave(p, 0)
    for copy in copies:
        copy.wait()


def shifted(block, axis, distance):
    count = lax.axis_size(axis)
    return lax.ppermute(block, axis, [(i, (i + distance) % count) for i in range(count)])


def swapped(block, axis, first):
    count = lax.axis_size(axis)
    pairs = [(i % count, (i + 1) % count) for i in range(first, count + first, 2)]
    return lax.ppermute(block, axis, pairs + [(b, a) for a, b in pairs])


def shards(velocity, tests):
    _, nx, half, n = velocity.shape
    problems, _, _, ny, _ = tests.shape
    lines = nx * ny
    constants, places = make_tables(n, nx * lax.axis_size("gx"), ny, n * lax.axis_size("gz"))
    vmem = pl.BlockSpec(memory_space=pltpu.VMEM)

    def shape(*dims):
        return jax.ShapeDtypeStruct(dims, F32)

    def run(kernel, name, args, outs, scratch=(), flops=10**8, out_specs=None, bind=True, in_space=pltpu.VMEM, limit=VMEM_LIMIT):
        body = kernel if not bind else (lambda *refs: kernel(places, *refs))
        moved = 4 * sum(math.prod(a.shape) for a in (*args, *outs))
        return pl.pallas_call(
            body,
            in_specs=[pl.BlockSpec(memory_space=in_space)] * len(args),
            out_specs=[vmem] * len(outs) if out_specs is None else out_specs,
            out_shape=list(outs),
            scratch_shapes=list(scratch),
            compiler_params=pltpu.CompilerParams(vmem_limit_bytes=limit),
            cost_estimate=pl.CostEstimate(flops=flops, bytes_accessed=moved, transcendentals=0),
            name=name,
        )(*args)

    whole_shape = (3, nx, ny, n)
    tests_shape = (problems, 3, nx, ny, n)
    other = shifted(velocity, "sec", 1)
    tables = jnp.asarray(constants)
    v_low, v_high = run(faces_kernel, "flow_faces", [velocity], [shape(3, 3, half, n)] * 2, bind=False)
    v_own = [shifted(v_high, "gx", 1), shifted(v_low, "gx", -1)]
    t_low, t_high = run(
        test_faces_kernel, "test_faces", [tests], [shape(problems, 3, 3, ny, n)] * 2,
        [pltpu.SemaphoreType.DMA((2,))], bind=False, in_space=pl.ANY, limit=FACES_LIMIT,
    )
    t_faces = [shifted(t_high, "gx", 1), shifted(t_low, "gx", -1)]
    (packed,) = run(pack_kernel, "pack", v_own, [shape(2, 3, 3, half, n)], bind=False)
    v_other = shifted(packed, "sec", 1)
    whole, inner, outer = run(
        whole_kernel, "whole", [velocity, other, tables],
        [shape(*whole_shape)] + [shape(4, 3 * lines)] * 2,
    )
    outer = swapped(outer, "gz", 1)
    inner = swapped(inner, "gz", 0)
    acc, part, sent = run(
        local_kernel, "local", [whole, tests, tables],
        [shape(*whole_shape), shape(*tests_shape), shape(8, problems * 3 * lines)],
        [pltpu.VMEM((3, ny + 16, n), F32), pltpu.VMEM(whole_shape, F32), pltpu.VMEM(whole_shape, F32)],
        flops=4 * 10**9,
    )
    moved, cross, low, high = run(
        step_kernel, "step", [whole, acc, *v_own, v_other, inner, outer, tests, tables],
        [shape(*whole_shape), shape(*tests_shape)] + [shape(3, 3, ny, n)] * 2,
        [pltpu.VMEM(whole_shape, F32)] * 2 + [pltpu.VMEM((3, 3, ny, n), F32)] * 2, flops=10**9,
    )
    from_low = shifted(high, "gx", 1)
    from_high = shifted(low, "gx", -1)
    inner, outer = run(
        sums_kernel, "sums", [cross, sent, tables], [shape(4, problems * 3 * lines)] * 2,
    )
    outer = swapped(outer, "gz", 1)
    inner = swapped(inner, "gz", 0)
    part, velocity_next = run(
        curl_kernel, "curl", [part, cross, *t_faces, moved, tables], [shape(*tests_shape), shape(3, nx, half, n)],
        [pltpu.VMEM((2, ny + 16, n), F32), pltpu.SemaphoreType.DMA], flops=10**9,
        out_specs=[vmem, pl.BlockSpec(memory_space=pl.ANY)],
    )
    (test_next,) = run(
        finish_kernel, "finish",
        [part, inner, outer, *t_faces, from_low, from_high, tables],
        [shape(*tests_shape)],
        [
            pltpu.VMEM(tests_shape, F32), pltpu.VMEM((2, 3, ny, n), F32),
            pltpu.SemaphoreType.DMA((3 * problems,)),
        ],
        out_specs=[pl.BlockSpec(memory_space=pl.ANY)],
    )
    return velocity_next, test_next


def solution(mesh):
    placed = (P(None, "gx", "sec", "gz"), P("sec", None, "gx", None, "gz"))
    return jax.shard_map(shards, mesh=mesh, in_specs=placed, out_specs=placed, check_vma=False)
```
